32 devices in a mesh: dp: 8 (over y, x, core), tensor: 4 (over z).
Axes of the slice: x: 2, y: 2, z: 4, core: 2. Of those that a mesh axis runs over, the one named last changes fastest.
Arguments:
- tokens: bfloat16 [32, 576, 768], P('dp'), may hold values from -6 to 6
- cotangent: bfloat16 [32, 576, 768], P('dp'), may hold values from -6 to 6
- counts: int32 [32], P('dp'), may hold values from 196 to 576, as said below
- qkv_master: float32 [768, 3, 768], P('dp', None, 'tensor'), may hold values from -0.21875 to 0.21875
- qkv_first: float32 [768, 3, 768], P('dp', None, 'tensor'), may hold values from -384 to 384
- qkv_second: float32 [768, 3, 768], P('dp', None, 'tensor'), may hold values from 4608 to 18432
- out_master: float32 [768, 768], P('tensor', 'dp'), may hold values from -1.25 to 1.25
- out_first: float32 [768, 768], P('tensor', 'dp'), may hold values from -112 to 112
- out_second: float32 [768, 768], P('tensor', 'dp'), may hold values from 368 to 1474
- up_master: float32 [768, 4, 768], P('dp', None, 'tensor'), may hold values from -0.21875 to 0.21875
- up_first: float32 [768, 4, 768], P('dp', None, 'tensor'), may hold values from -192 to 192
- up_second: float32 [768, 4, 768], P('dp', None, 'tensor'), may hold values from 1152 to 4608
- down_master: float32 [4, 768, 768], P(None, 'tensor', 'dp'), may hold values from -0.109375 to 0.109375
- down_first: float32 [4, 768, 768], P(None, 'tensor', 'dp'), may hold values from -384 to 384
- down_second: float32 [4, 768, 768], P(None, 'tensor', 'dp'), may hold values from 4608 to 18432
- shared_master: float32 [6, 768], P(None, 'dp'), may hold values from -1.5 to 1.5
- shared_first: float32 [6, 768], P(None, 'dp'), may hold values from -512 to 512
- shared_second: float32 [6, 768], P(None, 'dp'), may hold values from 9216 to 36864
- split_master: float32 [6, 768], P(None, ('tensor', 'dp')), may hold values from -1.5 to 1.5
- split_first: float32 [6, 768], P(None, ('tensor', 'dp')), may hold values from -384 to 384
- split_second: float32 [6, 768], P(None, ('tensor', 'dp')), may hold values from 3686 to 14745
Outputs:
- mixed: bfloat16 [32, 576, 768], P('dp')
- input_grad: float32 [32, 576, 768], P('dp')
- qkv_master_new: float32 [768, 3, 768], P('dp', None, 'tensor')
- qkv_copy_new: bfloat16 [768, 3, 768], P('dp', None, 'tensor')
- qkv_first_new: float32 [768, 3, 768], P('dp', None, 'tensor')
- qkv_second_new: float32 [768, 3, 768], P('dp', None, 'tensor')
- out_master_new: float32 [768, 768], P('tensor', 'dp')
- out_copy_new: bfloat16 [768, 768], P('tensor', 'dp')
- out_first_new: float32 [768, 768], P('tensor', 'dp')
- out_second_new: float32 [768, 768], P('tensor', 'dp')
- up_master_new: float32 [768, 4, 768], P('dp', None, 'tensor')
- up_copy_new: bfloat16 [768, 4, 768], P('dp', None, 'tensor')
- up_first_new: float32 [768, 4, 768], P('dp', None, 'tensor')
- up_second_new: float32 [768, 4, 768], P('dp', None, 'tensor')
- down_master_new: float32 [4, 768, 768], P(None, 'tensor', 'dp')
- down_copy_new: bfloat16 [4, 768, 768], P(None, 'tensor', 'dp')
- down_first_new: float32 [4, 768, 768], P(None, 'tensor', 'dp')
- down_second_new: float32 [4, 768, 768], P(None, 'tensor', 'dp')
- shared_master_new: float32 [6, 768], P(None, 'dp')
- shared_copy_new: bfloat16 [6, 768], P(None, 'dp')
- shared_first_new: float32 [6, 768], P(None, 'dp')
- shared_second_new: float32 [6, 768], P(None, 'dp')
- split_master_new: float32 [6, 768], P(None, ('tensor', 'dp'))
- split_copy_new: bfloat16 [6, 768], P(None, ('tensor', 'dp'))
- split_first_new: float32 [6, 768], P(None, ('tensor', 'dp'))
- split_second_new: float32 [6, 768], P(None, ('tensor', 'dp'))
The draws below stay inside these ranges and needn't reach their ends.
Inputs may be any that keep to these rules, and one draw needn't show every extreme that they name: `counts`: every count is 196 or 576, and both values occur in every draw.
All inputs are finite; a program needn't handle non-finite values.
Results may differ from the reference program's by a relative error of at most 0.012.
The reference program's roundings to bfloat16 on the way count: a program that leaves them out, or rounds other values in their place, can miss the bound.
Values may be sent and summed in bfloat16 or wider, within the bound.
A program may use at most 192 MiB of HBM per device.

```python
import math
import jax
import jax.numpy as jnp
from jax import lax

D = 768
FF = 3072
HEADS = 12
HEAD_DIM = 64
LEN = 576
SHORT = 196
STEP = 10
FOLDS = 4
SEQS = 32
TOKENS = 18432


def draw_counts(key, part):
    key = jax.random.fold_in(key, 11)
    coin_key, order_key = jax.random.split(key)
    tosses = jax.random.randint(coin_key, (SEQS,), 0, 2)
    shuffled = jax.random.permutation(order_key, SEQS)
    tosses = tosses.at[shuffled[0]].set(1)
    tosses = tosses.at[shuffled[1]].set(0)
    return jnp.where(tosses > 0, LEN, SHORT).astype(jnp.int32)


def draw_shared_master(key, part):
    key = jax.random.fold_in(key, 23)
    gain_key, shift_key = jax.random.split(key)
    gains = jnp.clip(1.0 + 0.15 * jax.random.normal(gain_key, (2, D), jnp.float32), 0.5, 1.5)
    shifts = jnp.clip(0.3 * jax.random.normal(shift_key, (4, D), jnp.float32), -1.2, 1.2)
    stacked = jnp.stack([gains[0], shifts[0], shifts[1], gains[1], shifts[2], shifts[3]])
    return stacked.astype(jnp.float32)


def shard_levels(own_key, extent, pieces, least, high):
    gain, own = 1.0, jax.random.fold_in(own_key, 6)
    for position, shards_of in pieces:
        heights = jnp.exp(jax.random.uniform(jax.random.fold_in(own, position), (shards_of,), jnp.float32, least / len(pieces), high / len(pieces)))
        gain = gain * jnp.repeat(heights, extent[position] // shards_of).reshape([-1 if axis == position else 1 for axis in range(len(extent))])
    return gain


def bell_draw(key, extent, width, limit, pieces=(), held_as=jnp.bfloat16):
    array = width * jax.random.normal(key, extent, jnp.float32)
    if pieces:
        array = array * shard_levels(key, extent, pieces, -0.22, 0.18)
    return jnp.clip(array, -limit, limit).astype(held_as)


def setup_inputs(seed: int = 0) -> dict:
    streams_of = jax.random.split(jax.random.key(seed), 22)
    return {
        "tokens": bell_draw(streams_of[0], (SEQS, LEN, D), 1.0, 6.0, ((0, 8),)),
        "cotangent": bell_draw(streams_of[1], (SEQS, LEN, D), 1.0, 6.0, ((0, 8),)),
        "counts": draw_counts(jax.random.fold_in(streams_of[21], 71), 0),
        "qkv_master": bell_draw(streams_of[3], (D, 3, D), D ** -0.5, 0.21875, ((0, 8), (2, 4)), jnp.float32),
        "qkv_first": bell_draw(streams_of[4], (D, 3, D), ((TOKENS // 4) ** 0.5), 384.0, ((0, 8), (2, 4)), jnp.float32),
        "qkv_second": jnp.clip(jnp.exp(math.log(18432.0) - 1.3862944 * jax.random.uniform(streams_of[5], (D, 3, D), jnp.float32) ** shard_levels(streams_of[5], (D, 3, D), ((0, 8), (2, 4)), -0.2, 0.2)), 4608.0, 18432.0),
        "out_master": bell_draw(streams_of[6], (D, D), (D * 16 // LEN) ** -0.5, 1.25, ((0, 4), (1, 8)), jnp.float32),
        "out_first": bell_draw(streams_of[7], (D, D), ((TOKENS // 50) ** 0.5), 112.0, ((0, 4), (1, 8)), jnp.float32),
        "out_second": jnp.clip(jnp.exp(math.log(1474.0) - 1.3876521 * jax.random.uniform(streams_of[8], (D, D), jnp.float32) ** shard_levels(streams_of[8], (D, D), ((0, 4), (1, 8)), -0.2, 0.2)), 368.0, 1474.0),
        "up_master": bell_draw(streams_of[9], (D, FOLDS, D), D ** -0.5, 0.21875, ((0, 8), (2, 4)), jnp.float32),
        "up_first": bell_draw(streams_of[10], (D, FOLDS, D), ((TOKENS // 16) ** 0.5), 192.0, ((0, 8), (2, 4)), jnp.float32),
        "up_second": jnp.clip(jnp.exp(math.log(4608.0) - 1.3862944 * jax.random.uniform(streams_of[11], (D, FOLDS, D), jnp.float32) ** shard_levels(streams_of[11], (D, FOLDS, D), ((0, 8), (2, 4)), -0.2, 0.2)), 1152.0, 4608.0),
        "down_master": bell_draw(streams_of[12], (FOLDS, D, D), FF ** -0.5, 0.109375, ((1, 4), (2, 8)), jnp.float32),
        "down_first": bell_draw(streams_of[13], (FOLDS, D, D), ((TOKENS // 4) ** 0.5), 384.0, ((1, 4), (2, 8)), jnp.float32),
        "down_second": jnp.clip(jnp.exp(math.log(18432.0) - 1.3862944 * jax.random.uniform(streams_of[14], (FOLDS, D, D), jnp.float32) ** shard_levels(streams_of[14], (FOLDS, D, D), ((1, 4), (2, 8)), -0.2, 0.2)), 4608.0, 18432.0),
        "shared_master": draw_shared_master(jax.random.fold_in(streams_of[21], 71), 0),
        "shared_first": bell_draw(streams_of[16], (6, D), ((TOKENS // 2) ** 0.5), 512.0, ((1, 8),), jnp.float32),
        "shared_second": jnp.clip(jnp.exp(math.log(36864.0) - 1.3862944 * jax.random.uniform(streams_of[17], (6, D), jnp.float32) ** shard_levels(streams_of[17], (6, D), ((1, 8),), -0.2, 0.2)), 9216.0, 36864.0),
        "split_master": bell_draw(streams_of[18], (2 + FOLDS, D), 0.3, 1.5, ((1, 32),), jnp.float32),
        "split_first": bell_draw(streams_of[19], (2 + FOLDS, D), ((TOKENS // 5) ** 0.5), 384.0, ((1, 32),), jnp.float32),
        "split_second": jnp.clip(jnp.exp(math.log(14745.0) - 1.3863622 * jax.random.uniform(streams_of[20], (2 + FOLDS, D), jnp.float32) ** shard_levels(streams_of[20], (2 + FOLDS, D), ((1, 32),), -0.2, 0.2)), 3686.0, 14745.0),
    }


@jax.custom_vjp
def low(v):
    return lax.optimization_barrier(v.astype(jnp.bfloat16)).astype(jnp.float32)

@jax.custom_vjp
def low_back(v):
    return v

def low_keep(v):
    return (low(v), None)

def low_pass(kept, grad):
    return (grad,)

def back_keep(v):
    return (v, None)

def back_low(kept, grad):
    return (low(grad),)
low.defvjp(low_keep, low_pass)
low_back.defvjp(back_keep, back_low)
PRECISE = lax.Precision.HIGHEST
LN_EPS = 1e-05
MASK_FILL = -1e+30
BETA_ONE = 0.5
BETA_TWO = 0.5
ADAM_EPS = 1e-08
MATRIX_DECAY = 0.01
SQRT_HALF = 0.7071067811865476

def layer_norm(inputs, norm_gain, norm_shift):
    row_mean = lax.optimization_barrier(jnp.mean(inputs, axis=-1, keepdims=True))
    centred = inputs - row_mean
    variance = lax.optimization_barrier(jnp.mean(centred * centred, axis=-1, keepdims=True))
    return centred * lax.rsqrt(variance + LN_EPS) * norm_gain + norm_shift

def gelu_exact(values):
    return 0.5 * values * (1.0 + lax.erf(values * SQRT_HALF))

def forward(qkv_master, out_master, up_master, down_master, shared_master, split_master, inputs, real_count):
    qkv_weight = low(qkv_master)
    out_weight = low(out_master)
    up_weight = low(up_master)
    down_weight = low(down_master)
    shared_weight = low(shared_master)
    split_weight = low(split_master)
    places = jnp.arange(LEN, dtype=jnp.int32)
    valid_rows = (places < real_count).astype(jnp.float32)
    first_in = low(layer_norm(inputs, shared_weight[0], shared_weight[1]))
    projected = jnp.einsum('rd,dkc->rkc', first_in, qkv_weight, precision=PRECISE)
    queries = low(low_back(projected[:, 0] + split_weight[0])).reshape(LEN, HEADS, HEAD_DIM)
    keys_all = low(low_back(projected[:, 1])).reshape(LEN, HEADS, HEAD_DIM)
    values_all = low(low_back(projected[:, 2] + split_weight[1])).reshape(LEN, HEADS, HEAD_DIM)
    raw_scores = jnp.einsum('qhe,khe->hqk', queries, keys_all, precision=PRECISE) * HEAD_DIM ** (-0.5)
    scores = low_back(jnp.where(valid_rows[None, None, :] > 0, raw_scores, MASK_FILL))
    row_top = lax.optimization_barrier(jnp.max(scores, axis=-1, keepdims=True))
    lifted = jnp.exp(scores - row_top)
    probs = low(lifted / lax.optimization_barrier(jnp.sum(lifted, axis=-1, keepdims=True)))
    attended = jnp.einsum('hqk,khe->qhe', probs, values_all, precision=PRECISE).reshape(LEN, D)
    attended = low(low_back(attended))
    branch = low_back(jnp.dot(attended, out_weight, precision=PRECISE))
    middle = inputs + branch + shared_weight[2]
    second_in = low(layer_norm(middle, shared_weight[3], shared_weight[4]))
    hidden_pre = jnp.einsum('rd,dfc->rfc', second_in, up_weight, precision=PRECISE) + split_weight[2:]
    hidden = low(gelu_exact(low_back(hidden_pre)))
    result = middle + jnp.einsum('rfc,fcd->rd', hidden, down_weight, precision=PRECISE) + shared_weight[5]
    return result * valid_rows[:, None]

def kind_rates():
    return (0.7 * D ** (-0.5), 0.7 * (D * 16 // LEN) ** (-0.5), 0.7 * D ** (-0.5), 0.7 * FF ** (-0.5), 0.6, 0.4)

def adamw(master, first, second, gradient, step_rate, decay_rate):
    first_new = BETA_ONE * first + (1.0 - BETA_ONE) * gradient
    second_new = BETA_TWO * second + (1.0 - BETA_TWO) * gradient * gradient
    first_hat = first_new / (1.0 - BETA_ONE ** STEP)
    second_hat = second_new / (1.0 - BETA_TWO ** STEP)
    master_new = master - step_rate * (first_hat / (jnp.sqrt(second_hat) + ADAM_EPS) + decay_rate * master)
    return (master_new, master_new.astype(jnp.bfloat16), first_new, second_new)

def reference(tokens, cotangent, counts, qkv_master, qkv_first, qkv_second, out_master, out_first, out_second, up_master, up_first, up_second, down_master, down_first, down_second, shared_master, shared_first, shared_second, split_master, split_first, split_second):
    masters = (qkv_master, out_master, up_master, down_master, shared_master, split_master)

    def one_slice(totals, scan_item):
        inputs, back_rows, real_count = scan_item

        def apply_layer(qkv_m, out_m, up_m, down_m, shared_m, split_m, layer_in):
            return forward(qkv_m, out_m, up_m, down_m, shared_m, split_m, layer_in, real_count)
        result, pullback = jax.vjp(apply_layer, *masters, inputs.astype(jnp.float32))
        gradients = pullback(back_rows.astype(jnp.float32))
        new_totals = jax.tree.map(jnp.add, totals, tuple(gradients[:6]))
        return (new_totals, (result.astype(jnp.bfloat16), gradients[6]))
    zero_totals = tuple((jnp.zeros(weight.shape, jnp.float32) for weight in masters))
    summed, (mixed, input_grad) = lax.scan(one_slice, zero_totals, (tokens, cotangent, counts))
    firsts = (qkv_first, out_first, up_first, down_first, shared_first, split_first)
    seconds = (qkv_second, out_second, up_second, down_second, shared_second, split_second)
    decays = (MATRIX_DECAY, MATRIX_DECAY, MATRIX_DECAY, MATRIX_DECAY, 0.0, 0.0)
    rates = kind_rates()
    outputs = [mixed, input_grad]
    for kind in range(6):
        outputs.extend(adamw(masters[kind], firsts[kind], seconds[kind], summed[kind], rates[kind], decays[kind]))
    return tuple(outputs)
```

```python
import jax
import jax.numpy as jnp
from jax import lax
from jax.sharding import PartitionSpec as P

D = 768
FF = 3072
HEAD_DIM = 64
LEN = 576
STEP = 10


LN_EPS = 1e-05
MASK_FILL = -1e30
BETA_ONE = 0.5
BETA_TWO = 0.5
ADAM_EPS = 1e-08
MATRIX_DECAY = 0.01
SQRT_HALF = 0.7071067811865476
INV_ROOT_TAU = 0.3989422804014327
AXES = ("tensor", "dp")


def norm_forward(inputs, norm_gain, norm_shift):
    row_mean = jnp.mean(inputs, axis=-1, keepdims=True)
    centred = inputs - row_mean
    variance = jnp.mean(centred * centred, axis=-1, keepdims=True)
    inverse = lax.rsqrt(variance + LN_EPS)
    normal = centred * inverse
    return (normal * norm_gain + norm_shift, normal, inverse)


def norm_backward(grad_normed, normal, inverse, norm_gain):
    scaled = grad_normed * norm_gain
    first_mean = jnp.mean(scaled, axis=-1, keepdims=True)
    second_mean = jnp.mean(scaled * normal, axis=-1, keepdims=True)
    return inverse * (scaled - first_mean - normal * second_mean)


def gelu_exact(values):
    return 0.5 * values * (1.0 + lax.erf(values * SQRT_HALF))


def gelu_slope(values):
    return (
        0.5 * (1.0 + lax.erf(values * SQRT_HALF))
        + values * jnp.exp(-0.5 * values * values) * INV_ROOT_TAU
    )


def kind_rates():
    return (
        0.7 * D ** (-0.5),
        0.7 * (D * 16 // LEN) ** (-0.5),
        0.7 * D ** (-0.5),
        0.7 * FF ** (-0.5),
        0.6,
        0.4,
    )


def adamw(master, first, second, gradient, step_rate, decay_rate):
    first_new = BETA_ONE * first + (1.0 - BETA_ONE) * gradient
    second_new = BETA_TWO * second + (1.0 - BETA_TWO) * gradient * gradient
    first_hat = first_new / (1.0 - BETA_ONE**STEP)
    second_hat = second_new / (1.0 - BETA_TWO**STEP)
    master_new = master - step_rate * (
        first_hat / (jnp.sqrt(second_hat) + ADAM_EPS) + decay_rate * master
    )
    return (master_new, master_new.astype(jnp.bfloat16), first_new, second_new)


def pack_attention(qkv, out):
    q, k, v = qkv[:, 0], qkv[:, 1], qkv[:, 2]
    return jnp.concatenate(
        [
            q[:, :128], k[:, :128], v[:, :128],
            q[:, 128:], out[:, :64], k[:, 128:], out[:, 64:128], v[:, 128:], out[:, 128:],
        ],
        axis=1,
    )


def unpack_attention(block):
    pair = [block[:, 128 * i : 128 * i + 128] for i in range(6)]
    q = jnp.concatenate([pair[0], pair[3][:, :64]], axis=1)
    k = jnp.concatenate([pair[1], pair[4][:, :64]], axis=1)
    v = jnp.concatenate([pair[2], pair[5][:, :64]], axis=1)
    o = jnp.concatenate([pair[3][:, 64:], pair[4][:, 64:], pair[5][:, 64:]], axis=1)
    return jnp.stack([q, k, v], axis=1), o


def local(tokens, cotangent, counts, *state):
    f32 = jnp.float32
    bf16 = jnp.bfloat16
    masters, firsts, seconds = state[0::3], state[1::3], state[2::3]
    qkv_master, out_master, up_master, down_master, shared_master, split_master = masters
    groups = lax.axis_size("tensor")
    copies = lax.axis_size("dp")
    seq_count, length, width = tokens.shape
    share = seq_count // groups
    mine = lax.axis_index("tensor") * share
    rows = share * length
    band = qkv_master.shape[0]

    attn_own = pack_attention(qkv_master.astype(bf16), out_master.astype(bf16).T)
    up_own = up_master.astype(bf16).reshape(band, -1)
    down_own = down_master.astype(bf16).reshape(-1, band).T
    mats = lax.all_gather(jnp.stack([attn_own, up_own, down_own]), AXES, axis=1, tiled=True)
    mats = mats.reshape(3, groups, width, width)
    shared_vecs = lax.all_gather(shared_master.astype(bf16), "dp", axis=1, tiled=True).astype(f32)
    split_vecs = lax.all_gather(split_master.astype(bf16), AXES, axis=1, tiled=True).astype(f32)

    x_low = lax.dynamic_slice_in_dim(tokens, mine, share, 0)
    cot = lax.dynamic_slice_in_dim(cotangent, mine, share, 0)
    cnt = lax.dynamic_slice_in_dim(counts, mine, share, 0)
    inputs = x_low.astype(f32).reshape(rows, width)
    places = lax.broadcasted_iota(jnp.int32, (share, length), 1)
    valid_rows = (places < cnt[:, None]).astype(f32)
    key_valid = valid_rows[None, :, None, None, :] > 0
    row_valid = valid_rows.reshape(rows, 1)

    normed_one, normal_one, inverse_one = norm_forward(inputs, shared_vecs[0], shared_vecs[1])
    first_in = normed_one.astype(bf16)
    proj = jnp.einsum("rd,gdc->grc", first_in, mats[0], preferred_element_type=f32)
    bias = split_vecs[:2].reshape(2, groups, 1, -1)
    part = [proj[:, :, 128 * i : 128 * i + 128] for i in range(6)]
    q = jnp.concatenate([part[0], part[3][:, :, :64]], axis=2) + bias[0]
    k = jnp.concatenate([part[1], part[4][:, :, :64]], axis=2)
    v = jnp.concatenate([part[2], part[5][:, :, :64]], axis=2) + bias[1]
    hs = (groups, share, length, -1, HEAD_DIM)
    q, k, v = (t.astype(bf16).reshape(hs) for t in (q, k, v))
    raw = jnp.einsum("gsqhe,gskhe->gshqk", q, k, preferred_element_type=f32) * HEAD_DIM ** (-0.5)
    scores = jnp.where(key_valid, raw, MASK_FILL)
    top = jnp.max(scores, axis=-1, keepdims=True)
    lifted = jnp.exp(scores - top)
    probs = lifted / jnp.sum(lifted, axis=-1, keepdims=True)
    probs_low = probs.astype(bf16)
    attended = jnp.einsum("gshqk,gskhe->gsqhe", probs_low, v, preferred_element_type=f32)
    attended = attended.reshape(groups, rows, -1).astype(bf16)
    out_t = jnp.concatenate(
        [mats[0][:, :, 128 * i + 64 : 128 * i + 128] for i in (3, 4, 5)], axis=2
    )
    branch = jnp.einsum("grc,gdc->rd", attended, out_t, preferred_element_type=f32)
    middle = inputs + branch + shared_vecs[2]
    normed_two, normal_two, inverse_two = norm_forward(middle, shared_vecs[3], shared_vecs[4])
    second_in = normed_two.astype(bf16)
    up_bias = split_vecs[2:].reshape(-1, groups, 1, width // groups)
    up_bias = jnp.swapaxes(up_bias, 0, 1).reshape(groups, 1, width)
    hidden_pre = jnp.einsum("rd,gdc->grc", second_in, mats[1], preferred_element_type=f32) + up_bias
    hidden = gelu_exact(hidden_pre).astype(bf16)
    down_sum = jnp.einsum("grc,gdc->rd", hidden, mats[2], preferred_element_type=f32)
    mixed = ((middle + down_sum + shared_vecs[5]) * row_valid).astype(bf16)
    mixed = lax.all_gather(mixed.reshape(share, length, width), "tensor", axis=0, tiled=True)

    grad_out = cot.astype(f32).reshape(rows, width) * row_valid
    grad_out_low = grad_out.astype(bf16)
    grad_down = jnp.einsum("rd,grc->gdc", grad_out_low, hidden, preferred_element_type=f32)
    grad_hidden = jnp.einsum("rd,gdc->grc", grad_out_low, mats[2], preferred_element_type=f32)
    grad_pre = (grad_hidden * gelu_slope(hidden_pre)).astype(bf16)
    grad_up = jnp.einsum("rd,grc->gdc", second_in, grad_pre, preferred_element_type=f32)
    grad_up_bias = jnp.sum(grad_pre, axis=1, dtype=f32)
    grad_norm_two = jnp.einsum("grc,gdc->rd", grad_pre, mats[1], preferred_element_type=f32)
    grad_middle = grad_out + norm_backward(grad_norm_two, normal_two, inverse_two, shared_vecs[3])
    grad_middle_low = grad_middle.astype(bf16)
    grad_out_t = jnp.einsum("rd,grc->gdc", grad_middle_low, attended, preferred_element_type=f32)
    grad_att = jnp.einsum("rd,gdc->grc", grad_middle_low, out_t, preferred_element_type=f32)
    grad_att = grad_att.astype(bf16).reshape(hs)
    grad_v = jnp.einsum("gshqk,gsqhe->gskhe", probs_low, grad_att, preferred_element_type=f32)
    grad_probs = jnp.einsum("gsqhe,gskhe->gshqk", grad_att, v, preferred_element_type=f32)
    inner = jnp.sum(probs * grad_probs, axis=-1, keepdims=True)
    grad_scores = (probs * (grad_probs - inner)).astype(bf16)
    scale = HEAD_DIM ** (-0.5)
    grad_q = jnp.einsum("gshqk,gskhe->gsqhe", grad_scores, k, preferred_element_type=f32) * scale
    grad_k = jnp.einsum("gshqk,gsqhe->gskhe", grad_scores, q, preferred_element_type=f32) * scale
    grad_q, grad_k, grad_v = (
        t.reshape(groups, rows, -1).astype(bf16) for t in (grad_q, grad_k, grad_v)
    )
    zero = jnp.zeros((groups, rows, 64), bf16)
    grad_proj = jnp.concatenate(
        [
            grad_q[:, :, :128], grad_k[:, :, :128], grad_v[:, :, :128],
            grad_q[:, :, 128:], zero, grad_k[:, :, 128:], zero, grad_v[:, :, 128:], zero,
        ],
        axis=2,
    )
    grad_attn = jnp.einsum("rd,grc->gdc", first_in, grad_proj, preferred_element_type=f32)
    wide = jnp.concatenate(
        [jnp.pad(grad_out_t[:, :, 64 * i : 64 * i + 64], ((0, 0), (0, 0), (64, 0))) for i in range(3)],
        axis=2,
    )
    grad_attn = grad_attn + jnp.pad(wide, ((0, 0), (0, 0), (384, 0)))
    grad_norm_one = jnp.einsum("grc,gdc->rd", grad_proj, mats[0], preferred_element_type=f32)
    grad_inputs = grad_middle + norm_backward(
        grad_norm_one, normal_one, inverse_one, shared_vecs[0]
    )
    grad_inputs = grad_inputs.astype(bf16).reshape(share, length, width)
    grad_inputs = lax.all_gather(grad_inputs, "tensor", axis=0, tiled=True).astype(f32)

    grads = jnp.stack([grad_attn, grad_up, grad_down]).astype(bf16)
    grads = grads.reshape(3, groups * copies, band, width)
    grads = lax.psum_scatter(grads, AXES, scatter_dimension=1, tiled=False).astype(f32)
    shared_grad = jnp.stack(
        [
            jnp.sum(grad_norm_one * normal_one, axis=0),
            jnp.sum(grad_norm_one, axis=0),
            jnp.sum(grad_middle, axis=0),
            jnp.sum(grad_norm_two * normal_two, axis=0),
            jnp.sum(grad_norm_two, axis=0),
            jnp.sum(grad_out, axis=0),
        ]
    )
    bias_q = jnp.sum(grad_q, axis=1, dtype=f32).reshape(1, width)
    bias_v = jnp.sum(grad_v, axis=1, dtype=f32).reshape(1, width)
    bias_u = jnp.swapaxes(grad_up_bias.reshape(groups, -1, width // groups), 0, 1)
    split_grad = jnp.concatenate([bias_q, bias_v, bias_u.reshape(-1, width)], axis=0)
    vec_sum = lax.psum(jnp.concatenate([shared_grad, split_grad]), AXES)
    at = lax.axis_index("dp")
    shared_sum = lax.dynamic_slice_in_dim(vec_sum[:6], at * band, band, 1)
    thin = split_master.shape[1]
    split_at = (lax.axis_index("tensor") * copies + at) * thin
    split_sum = lax.dynamic_slice_in_dim(vec_sum[6:], split_at, thin, 1)

    sum_qkv, sum_out = unpack_attention(grads[0])
    summed = (
        sum_qkv,
        sum_out.T,
        grads[1].reshape(up_master.shape),
        grads[2].T.reshape(down_master.shape),
        shared_sum,
        split_sum,
    )
    decays = (MATRIX_DECAY, MATRIX_DECAY, MATRIX_DECAY, MATRIX_DECAY, 0.0, 0.0)
    rates = kind_rates()
    outputs = [mixed, grad_inputs]
    for kind in range(6):
        outputs.extend(
            adamw(
                masters[kind], firsts[kind], seconds[kind], summed[kind], rates[kind], decays[kind]
            )
        )
    return tuple(outputs)


def solution(mesh):
    rows = P("dp", None, None)
    state = (
        P("dp", None, "tensor"),
        P("tensor", "dp"),
        P("dp", None, "tensor"),
        P(None, "tensor", "dp"),
        P(None, "dp"),
        P(None, ("tensor", "dp")),
    )
    in_specs = (rows, rows, P("dp")) + tuple(s for s in state for _ in range(3))
    out_specs = (rows, rows) + tuple(s for s in state for _ in range(4))
    return jax.shard_map(local, mesh=mesh, in_specs=in_specs, out_specs=out_specs, check_vma=False)
```

```python
import functools

import jax
import jax.numpy as jnp
from jax import lax
from jax.experimental import pallas as pl
from jax.experimental.pallas import tpu as pltpu
from jax.sharding import PartitionSpec as P

D = 768
FF = 3072
HEAD_DIM = 64
LEN = 576
STEP = 10


LN_EPS = 1e-05
MASK_FILL = -1e30
BETA_ONE = 0.5
BETA_TWO = 0.5
ADAM_EPS = 1e-08
MATRIX_DECAY = 0.01
SQRT_HALF = 0.7071067811865476
INV_ROOT_TAU = 0.3989422804014327
AXES = ("tensor", "dp")
MESH = pl.DeviceIdType.MESH
bf16, f32 = jnp.bfloat16, jnp.float32
NN = (((1,), (0,)), ((), ()))
NT = (((1,), (1,)), ((), ()))
RT = 192
RL = 96


def kind_rates():
    return (
        0.7 * D ** (-0.5),
        0.7 * (D * 16 // LEN) ** (-0.5),
        0.7 * D ** (-0.5),
        0.7 * FF ** (-0.5),
        0.6,
        0.4,
    )


def adamw(master, first, second, gradient, step_rate, decay_rate):
    first_new = BETA_ONE * first + (1.0 - BETA_ONE) * gradient
    second_new = BETA_TWO * second + (1.0 - BETA_TWO) * gradient * gradient
    first_hat = first_new / (1.0 - BETA_ONE**STEP)
    second_hat = second_new / (1.0 - BETA_TWO**STEP)
    master_new = master - step_rate * (
        first_hat / (jnp.sqrt(second_hat) + ADAM_EPS) + decay_rate * master
    )
    return (master_new, master_new.astype(jnp.bfloat16), first_new, second_new)


def flip(index, bit):
    return index + bit - 2 * bit * lax.rem(lax.div(index, bit), 2)

def send(src, dst, ssem, rsem, to):
    return pltpu.make_async_remote_copy(
        src_ref=src, dst_ref=dst, send_sem=ssem, recv_sem=rsem, device_id=to, device_id_type=MESH
    )

def arrived(dst, sem):
    pltpu.make_async_copy(dst, dst, sem).wait()

def gather_kernel(rows_of, own, *refs):
    nb = len(rows_of)
    outs = refs[:nb]
    lsem, zs, zr, ps, pr, ds, dr, cs, cr = refs[nb:]
    z, me = lax.axis_index("tensor"), lax.axis_index("dp")
    nz = lax.axis_size("tensor")
    cp, xp, yp = flip(me, 1), flip(me, 2), flip(me, 4)
    dg = flip(xp, 4)
    pair = (xp, yp)
    bar = pltpu.get_barrier_semaphore()
    for d in (cp, xp, yp):
        pl.semaphore_signal(bar, inc=1, device_id=(d, z), device_id_type=MESH)
    @pl.when(z > 0)
    def _():
        pl.semaphore_signal(bar, inc=1, device_id=(me, z - 1), device_id_type=MESH)
    @pl.when(z < nz - 1)
    def _():
        pl.semaphore_signal(bar, inc=1, device_id=(me, z + 1), device_id_type=MESH)
    edges = jnp.where(z > 0, 1, 0) + jnp.where(z < nz - 1, 1, 0)
    pl.semaphore_wait(bar, 3 + edges)

    starts = [sum(rows_of[:b]) for b in range(nb)]
    def own_ref(b):
        return own.at[pl.ds(starts[b], rows_of[b])]
    def right(b, s, src):
        return send(src, outs[b].at[s, me], zs.at[b, 0, z - s], zr.at[b, s], (me, z + 1))
    def left(b, s, src):
        return send(src, outs[b].at[s, me], zs.at[b, 1, s - z], zr.at[b, s], (me, z - 1))
    def side(b, s, src, k):
        return send(src, outs[b].at[s, me], ps.at[b, k, s], pr.at[b, k, s], (pair[k], z))
    def spread(b, s, src):
        for k in range(2):
            side(b, s, src, k).start()
    half = [[(0, r//32*16), (r//32*16, r - r//32*16)] for r in rows_of]
    def diag(b, k):
        lo, n = half[b][k]
        part = outs[b].at[:, pair[k], pl.ds(lo, n)]
        return send(part, part, ds.at[b, k], dr.at[b, k], (pair[1 - k], z))
    def twin(b, j):
        part = outs[b].at[:, (me, xp, yp, dg)[j]]
        return send(part, part, cs.at[b, j], cr.at[b, j], (cp, z))
    keep = [pltpu.make_async_copy(own_ref(b), outs[b].at[z, me], lsem.at[b]) for b in range(nb)]

    def open_block(b):
        @pl.when(z < nz - 1)
        def _():
            right(b, z, own_ref(b)).start()
        @pl.when(z > 0)
        def _():
            left(b, z, own_ref(b)).start()
        spread(b, z, own_ref(b))
        keep[b].start()

    def hop(b, t):
        @pl.when(z >= t)
        def _():
            s = z - t
            arrived(outs[b].at[s, me], zr.at[b, s])
            @pl.when(z < nz - 1)
            def _():
                right(b, s, outs[b].at[s, me]).start()
            spread(b, s, outs[b].at[s, me])
        @pl.when(z + t < nz)
        def _():
            s = z + t
            arrived(outs[b].at[s, me], zr.at[b, s])
            @pl.when(z > 0)
            def _():
                left(b, s, outs[b].at[s, me]).start()
            spread(b, s, outs[b].at[s, me])
    def twin_own(b):
        keep[b].wait()
        twin(b, 0).start()
    def square(b):
        for k in range(2):
            for s in range(4):
                arrived(outs[b].at[s, pair[k]], pr.at[b, k, s])
            diag(b, k).start()
            twin(b, 1 + k).start()
    def corner(b):
        for k in range(2):
            lo, n = half[b][k]
            arrived(outs[b].at[:, dg, pl.ds(lo, n)], dr.at[b, k])
        twin(b, 3).start()
    def finish(b):
        for j, d in enumerate((cp, flip(xp, 1), flip(yp, 1), flip(dg, 1))):
            arrived(outs[b].at[:, d], cr.at[b, j])
    for b in range(nb):
        open_block(b)
    for t in (1, 2, 3):
        for b in range(nb):
            hop(b, t)
    for step in (twin_own, square, corner):
        for b in range(nb):
            step(b)
    for b in range(nb):
        finish(b)
    for b in range(nb):
        for t in range(4):
            @pl.when((z < nz - 1) & (z >= t))
            def _():
                right(b, z - t, outs[b].at[z - t, me]).wait_send()
            @pl.when((z > 0) & (z + t < nz))
            def _():
                left(b, z + t, outs[b].at[z + t, me]).wait_send()
            for k in range(2):
                side(b, t, outs[b].at[t, me], k).wait_send()
            twin(b, t).wait_send()
        for k in range(2):
            diag(b, k).wait_send()

def gather(own, rows_of, cid=1):
    nb = len(rows_of)
    S = pltpu.SemaphoreType.DMA
    return pl.pallas_call(
        functools.partial(gather_kernel, rows_of),
        out_shape=[jax.ShapeDtypeStruct((4, 8, r, D), jnp.bfloat16) for r in rows_of],
        in_specs=[pl.BlockSpec(memory_space=pltpu.VMEM)],
        out_specs=[pl.BlockSpec(memory_space=pl.ANY)] * nb,
        scratch_shapes=[S((nb,)), S((nb, 2, 4)), S((nb, 4)), S((nb, 2, 4)), S((nb, 2, 4)), S((nb, 2)), S((nb, 2)), S((nb, 4)), S((nb, 4))],
        compiler_params=pltpu.CompilerParams(collective_id=cid, has_side_effects=True),
    )(own)


def mm(a, b, dims=NN):
    return lax.dot_general(a, b, dims, preferred_element_type=f32)

def normal_of(rows):
    mean = jnp.mean(rows, axis=-1, keepdims=True)
    centred = rows - mean
    inverse = lax.rsqrt(jnp.mean(centred * centred, axis=-1, keepdims=True) + LN_EPS)
    return centred * inverse, inverse

def normal_back(grad, normal, inverse, gain):
    scaled = grad * gain
    return inverse * (
        scaled
        - jnp.mean(scaled, axis=-1, keepdims=True)
        - normal * jnp.mean(scaled * normal, axis=-1, keepdims=True)
    )

def row_tiles(size):
    return range(0, LEN, size)

def colsum(v):
    return jnp.sum(v, axis=0, keepdims=True)

def compute_kernel(x, cot, valid_col, keybias, vecs, bias, A, B, C,
                   mixed, ig, gA, gB, gC, vsum, bsum,
                   first_in, second_in, gout_low, gm_low, fT, sT, goT, gmT,
                   qkv, probs, att, middle, acc, acc2, gm, stage, sems):
    for r in row_tiles(RL):
        rs = pl.ds(r, RL)
        n, _ = normal_of(x[rs].astype(f32))
        first_in[rs] = (n * vecs[0:1] + vecs[1:2]).astype(bf16)
        go = cot[rs].astype(f32) * valid_col[rs]
        gout_low[rs] = go.astype(bf16)
    fT[...] = first_in[...].T
    goT[...] = gout_low[...].T
    lane = lax.broadcasted_iota(jnp.int32, (1, 128), 1)
    low = lane < 64
    acc[...] = jnp.zeros_like(acc)

    def forward(g, carry):
        w = A.at[g]
        for r in row_tiles(RT):
            rs = pl.ds(r, RT)
            p = mm(first_in[rs], w[...]) + bias[0, g]
            qkv[g, rs] = p.astype(bf16)
        def tile(i):
            return qkv[g, :, 128 * i : 128 * i + 128]
        outs = []
        for h in range(3):
            q, k, v = (tile(0), tile(1), tile(2)) if h < 2 else (tile(3), tile(4), tile(3))
            q = jnp.where(low if h != 1 else ~low, q, 0) * bf16(0.125)
            vt = v.T
            vt = vt[64:] if h else vt[:64]
            cols = []
            for r in row_tiles(RT):
                s = mm(k, q[r : r + RT], NT) + keybias[...]
                top = jnp.max(s, axis=0, keepdims=True)
                e = jnp.exp(s - top)
                p = (e * (1.0 / jnp.sum(e, axis=0, keepdims=True))).astype(bf16)
                probs[g, h, r // RT] = p
                cols.append(mm(vt, p))
            outs.append(jnp.concatenate(cols, axis=1))
        att[g, :, 128:256] = jnp.concatenate(outs[:2], axis=0).T.astype(bf16)
        att[g, :, 0:128] = jnp.concatenate([jnp.zeros_like(outs[2]), outs[2]], axis=0).T.astype(bf16)
        for r in row_tiles(RT):
            rs = pl.ds(r, RT)
            acc[rs] += mm(att[g, rs], w[:, 512:768], NT)
        return carry
    lax.fori_loop(0, 4, forward, 0)

    for r in row_tiles(RL):
        rs = pl.ds(r, RL)
        m = x[rs].astype(f32) + acc[rs] + vecs[2:3]
        middle[rs] = m
        n, _ = normal_of(m)
        second_in[rs] = (n * vecs[3:4] + vecs[4:5]).astype(bf16)
    sT[...] = second_in[...].T
    acc[...] = jnp.zeros_like(acc)
    acc2[...] = jnp.zeros_like(acc2)

    def put(dst, g, slot, compute):
        @pl.when(g > 0)
        def _():
            pltpu.make_async_copy(stage.at[slot], dst.at[g - 1], sems.at[slot]).wait()
        for c in range(0, D, 256):
            stage[slot, pl.ds(c, 256)] = compute(c).astype(bf16)
        pltpu.make_async_copy(stage.at[slot], dst.at[g], sems.at[slot]).start()
    def drain(dst, slot):
        pltpu.make_async_copy(stage.at[slot], dst.at[3], sems.at[slot]).wait()

    def mlp(g, carry):
        hid, gps = [], []
        for r in row_tiles(RT):
            rs = pl.ds(r, RT)
            u = mm(second_in[rs], B[g]) + bias[1, g]
            phi = 0.5 * (1.0 + lax.erf(u * SQRT_HALF))
            hidden = (u * phi).astype(bf16)
            slope = phi + u * jnp.exp(-0.5 * u * u) * INV_ROOT_TAU
            gp = (mm(gout_low[rs], C[g]) * slope).astype(bf16)
            acc[rs] += mm(hidden, C[g], NT)
            acc2[rs] += mm(gp, B[g], NT)
            hid.append(hidden)
            gps.append(gp)
        hid = jnp.concatenate(hid, axis=0)
        gps = jnp.concatenate(gps, axis=0)
        bsum[1, g] = colsum(gps.astype(f32))
        put(gC, g, 0, lambda c: mm(goT[pl.ds(c, 256)], hid))
        put(gB, g, 1, lambda c: mm(sT[pl.ds(c, 256)], gps))
        return carry
    lax.fori_loop(0, 4, mlp, 0)
    drain(gC, 0)
    drain(gB, 1)

    sums = [jnp.zeros((1, D), f32) for _ in range(6)]
    for r in row_tiles(RL):
        rs = pl.ds(r, RL)
        m = middle[rs]
        mixed[rs] = ((m + acc[rs] + vecs[5:6]) * valid_col[rs]).astype(bf16)
        n, inv = normal_of(m)
        gn = acc2[rs]
        go = gout_low[rs].astype(f32)
        t = go + normal_back(gn, n, inv, vecs[3:4])
        gm[rs] = t
        gm_low[rs] = t.astype(bf16)
        sums[2] += colsum(t)
        sums[3] += colsum(gn * n)
        sums[4] += colsum(gn)
        sums[5] += colsum(go)
    gmT[...] = gm_low[...].T
    acc[...] = jnp.zeros_like(acc)

    def backward(g, carry):
        w = A.at[g]
        ga = mm(gm_low[...], w[:, 512:768]).astype(bf16)
        def tile(i):
            return qkv[g, :, 128 * i : 128 * i + 128]
        dq, dk, dv = [], [], []
        for h in range(3):
            q, k, v = (tile(0), tile(1), tile(2)) if h < 2 else (tile(3), tile(4), tile(3))
            gt = ga[:, 128:256] if h < 2 else ga[:, 0:128]
            gmask = jnp.where(low if h == 0 else ~low, gt, 0)
            kt = k.T
            kt = kt[64:] if h == 1 else kt[:64]
            dqs, dks, dvs = [], 0.0, 0.0
            for r in row_tiles(RT):
                p = probs[g, h, r // RT]
                dp = mm(v, gmask[r : r + RT], NT)
                pf = p.astype(f32)
                inner = jnp.sum(pf * dp, axis=0, keepdims=True)
                ds = (pf * (dp - inner)).astype(bf16)
                dqs.append(mm(kt, ds))
                dks = dks + mm(ds, q[r : r + RT])
                dvs = dvs + mm(p, gt[r : r + RT])
            dq.append(jnp.concatenate(dqs, axis=1))
            dk.append(dks * 0.125)
            dv.append(dvs)
        dq01 = jnp.concatenate(dq[:2], axis=0).T * 0.125
        dq2 = jnp.concatenate([dq[2], jnp.zeros_like(dq[2])], axis=0).T * 0.125
        parts = [
            dq01,
            jnp.where(low, dk[0], dk[1]),
            jnp.where(low, dv[0], dv[1]),
            jnp.where(low, dq2, dv[2]),
            jnp.where(low, dk[2], 0.0),
        ]
        for i, part in enumerate(parts):
            part = part.astype(bf16)
            qkv[g, :, 128 * i : 128 * i + 128] = part
            bsum[0, g, :, 128 * i : 128 * i + 128] = colsum(part.astype(f32))
        qkv[g, :, 640:768] = jnp.zeros((LEN, 128), bf16)
        bsum[0, g, :, 640:768] = jnp.zeros((1, 128), f32)
        for r in row_tiles(RT):
            rs = pl.ds(r, RT)
            acc[rs] += mm(qkv[g, rs], w[...], NT)
        def grad(c):
            left = mm(fT[pl.ds(c, 256)], qkv[g])
            right = mm(gmT[pl.ds(c, 256)], att[g])
            return jnp.concatenate([left[:, :512], left[:, 512:] + right], axis=1)
        put(gA, g, 0, grad)
        return carry
    lax.fori_loop(0, 4, backward, 0)
    drain(gA, 0)

    for r in row_tiles(RL):
        rs = pl.ds(r, RL)
        n, inv = normal_of(x[rs].astype(f32))
        gn = acc[rs]
        ig[rs] = (gm[rs] + normal_back(gn, n, inv, vecs[0:1])).astype(bf16)
        sums[0] += colsum(gn * n)
        sums[1] += colsum(gn)
    for i in range(6):
        vsum[i : i + 1] = sums[i]

def compute(x, cot, valid_col, keybias, vecs, bias, A, B, C):
    V = pltpu.VMEM
    vm = pl.BlockSpec(memory_space=V)
    hb = pl.BlockSpec(memory_space=pl.ANY)
    S = jax.ShapeDtypeStruct
    return pl.pallas_call(
        compute_kernel,
        out_shape=[S((LEN, D), bf16), S((LEN, D), bf16)] + [S((4, D, D), bf16)] * 3 + [S((6, D), f32), S((2, 4, 1, D), f32)],
        in_specs=[vm] * 9,
        out_specs=[vm, vm, hb, hb, hb, vm, vm],
        scratch_shapes=[V((LEN, D), bf16)] * 4 + [V((D, LEN), bf16)] * 4 + [
            V((4, LEN, D), bf16), V((4, 3, 3, LEN, RT), bf16), V((4, LEN, 256), bf16),
            V((LEN, D), f32), V((LEN, D), f32), V((LEN, D), f32), V((LEN, D), f32),
            V((2, D, D), bf16), pltpu.SemaphoreType.DMA((2,)),
        ],
        compiler_params=pltpu.CompilerParams(vmem_limit_bytes=63 * 1024 * 1024),
        cost_estimate=pl.CostEstimate(flops=57_000_000_000, bytes_accessed=32_000_000, transcendentals=6_000_000),
    )(x, cot, valid_col, keybias, vecs, bias, A, B, C)


def pack_attention(qkv, out):
    q, k, v = qkv[:, 0], qkv[:, 1], qkv[:, 2]
    return jnp.concatenate(
        [
            q[:, :128], k[:, :128], v[:, :128],
            q[:, 128:], v[:, 128:], k[:, 128:], out[:, 128:], out[:, :128],
        ],
        axis=1,
    )


def unpack_attention(block):
    pair = [block[:, 128 * i : 128 * i + 128] for i in range(6)]
    q = jnp.concatenate([pair[0], pair[3][:, :64]], axis=1)
    k = jnp.concatenate([pair[1], pair[4][:, :64]], axis=1)
    v = jnp.concatenate([pair[2], pair[3][:, 64:]], axis=1)
    o = jnp.concatenate([pair[5], pair[4][:, 64:]], axis=1)
    return jnp.stack([q, k, v], axis=1), o


def local(tokens, cotangent, counts, *state):
    masters, firsts, seconds = state[0::3], state[1::3], state[2::3]
    qkv_master, out_master, up_master, down_master, shared_master, split_master = masters
    groups = lax.axis_size("tensor")
    copies = lax.axis_size("dp")
    seq_count, length, width = tokens.shape
    share = seq_count // groups
    mine = lax.axis_index("tensor") * share
    band = qkv_master.shape[0]
    thin = split_master.shape[1]

    attn_own = pack_attention(qkv_master.astype(bf16), out_master.astype(bf16).T)
    up_own = up_master.astype(bf16).reshape(band, -1)
    down_own = down_master.astype(bf16).reshape(-1, band).T
    vec_own = jnp.zeros((16, width), bf16)
    vec_own = vec_own.at[:6, :band].set(shared_master.astype(bf16))
    vec_own = vec_own.at[:6, 128 : 128 + thin].set(split_master.astype(bf16))
    own = jnp.concatenate([attn_own, vec_own, up_own, down_own])
    sizes = (band + 16, band, band)
    if (groups, copies) == (4, 8):
        mats = gather(own, sizes)
    else:
        whole = lax.all_gather(own, AXES).reshape(groups, copies, -1, width)
        ends = [0, sizes[0], sizes[0] + sizes[1], sum(sizes)]
        mats = [whole[:, :, ends[i] : ends[i + 1]] for i in range(3)]
    attn_all, up_all, down_all = mats
    vec_all = attn_all[:, :, band:].astype(f32)
    attn_all, up_all, down_all = (
        t[:, :, :band].reshape(groups, width, width) for t in (attn_all, up_all, down_all)
    )
    shared_vecs = jnp.swapaxes(vec_all[0, :, :6, :band], 0, 1).reshape(6, width)
    split_vecs = vec_all[:, :, :6, 128 : 128 + thin].reshape(groups, copies, 6, thin)
    split_vecs = jnp.swapaxes(split_vecs, 1, 2).reshape(groups, 6, copies * thin)
    bq, bv = split_vecs[:, 0], split_vecs[:, 1]
    zero = jnp.zeros((groups, 128), f32)
    attn_bias = jnp.concatenate(
        [bq[:, :128], zero, bv[:, :128], bq[:, 128:], bv[:, 128:], zero, zero], axis=1
    )
    up_bias = split_vecs[:, 2:].reshape(groups, width)
    bias = jnp.stack([attn_bias, up_bias]).reshape(2, groups, 1, width)

    x = lax.dynamic_slice_in_dim(tokens, mine, share, 0).reshape(length, width)
    cot = lax.dynamic_slice_in_dim(cotangent, mine, share, 0).reshape(length, width)
    count = lax.dynamic_slice_in_dim(counts, mine, share, 0)
    valid = lax.broadcasted_iota(jnp.int32, (length, 1), 0) < count
    mixed, grad_inputs, grad_attn, grad_up, grad_down, shared_grad, split_grad = compute(
        x, cot, valid.astype(f32), jnp.where(valid, 0.0, MASK_FILL), shared_vecs, bias,
        attn_all, up_all, down_all,
    )
    mixed = lax.all_gather(mixed[None], "tensor", axis=0, tiled=True)
    grad_inputs = lax.all_gather(grad_inputs[None], "tensor", axis=0, tiled=True).astype(f32)

    grads = jnp.stack([grad_attn, grad_up, grad_down])
    grads = grads.reshape(3, groups * copies, band, width)
    grads = lax.psum_scatter(grads, AXES, scatter_dimension=1, tiled=False).astype(f32)
    cols = split_grad.reshape(2, groups, width)
    grad_bq = jnp.concatenate([cols[0, :, :128], cols[0, :, 384:448]], axis=1).reshape(1, width)
    grad_bv = jnp.concatenate([cols[0, :, 256:384], cols[0, :, 448:512]], axis=1).reshape(1, width)
    grad_bu = jnp.swapaxes(cols[1].reshape(groups, -1, width // groups), 0, 1).reshape(-1, width)
    vec_sum = lax.psum(jnp.concatenate([shared_grad, grad_bq, grad_bv, grad_bu]), AXES)
    at = lax.axis_index("dp")
    shared_sum = lax.dynamic_slice_in_dim(vec_sum[:6], at * band, band, 1)
    split_at = (lax.axis_index("tensor") * copies + at) * thin
    split_sum = lax.dynamic_slice_in_dim(vec_sum[6:], split_at, thin, 1)

    sum_qkv, sum_out = unpack_attention(grads[0])
    summed = (
        sum_qkv,
        sum_out.T,
        grads[1].reshape(up_master.shape),
        grads[2].T.reshape(down_master.shape),
        shared_sum,
        split_sum,
    )
    decays = (MATRIX_DECAY, MATRIX_DECAY, MATRIX_DECAY, MATRIX_DECAY, 0.0, 0.0)
    rates = kind_rates()
    outputs = [mixed, grad_inputs]
    for kind in range(6):
        outputs.extend(
            adamw(
                masters[kind], firsts[kind], seconds[kind], summed[kind], rates[kind], decays[kind]
            )
        )
    return tuple(outputs)


def solution(mesh):
    rows = P("dp", None, None)
    state = (
        P("dp", None, "tensor"),
        P("tensor", "dp"),
        P("dp", None, "tensor"),
        P(None, "tensor", "dp"),
        P(None, "dp"),
        P(None, ("tensor", "dp")),
    )
    in_specs = (rows, rows, P("dp")) + tuple(s for s in state for _ in range(3))
    out_specs = (rows, rows) + tuple(s for s in state for _ in range(4))
    return jax.shard_map(local, mesh=mesh, in_specs=in_specs, out_specs=out_specs, check_vma=False)
```

```python
import functools

import jax
import jax.numpy as jnp
from jax import lax
from jax.experimental import pallas as pl
from jax.experimental.pallas import tpu as pltpu
from jax.sharding import PartitionSpec as P

D = 768
FF = 3072
HEAD_DIM = 64
LEN = 576
STEP = 10


LN_EPS = 1e-05
MASK_FILL = -1e30
BETA_ONE = 0.5
BETA_TWO = 0.5
ADAM_EPS = 1e-08
MATRIX_DECAY = 0.01
SQRT_HALF = 0.7071067811865476
INV_ROOT_TAU = 0.3989422804014327
AXES = ("tensor", "dp")
MESH = pl.DeviceIdType.MESH
bf16, f32 = jnp.bfloat16, jnp.float32
NN = (((1,), (0,)), ((), ()))
NT = (((1,), (1,)), ((), ()))
RT = 192
RL = 96
BAND = 96


def kind_rates():
    return (
        0.7 * D ** (-0.5),
        0.7 * (D * 16 // LEN) ** (-0.5),
        0.7 * D ** (-0.5),
        0.7 * FF ** (-0.5),
        0.6,
        0.4,
    )


def adamw(master, first, second, gradient, step_rate, decay_rate):
    first_new = BETA_ONE * first + (1.0 - BETA_ONE) * gradient
    second_new = BETA_TWO * second + (1.0 - BETA_TWO) * gradient * gradient
    first_hat = first_new / (1.0 - BETA_ONE**STEP)
    second_hat = second_new / (1.0 - BETA_TWO**STEP)
    master_new = master - step_rate * (
        first_hat / (jnp.sqrt(second_hat) + ADAM_EPS) + decay_rate * master
    )
    return (master_new, master_new.astype(jnp.bfloat16), first_new, second_new)


def flip(index, bit):
    return index + bit - 2 * bit * lax.rem(lax.div(index, bit), 2)

def send(src, dst, ssem, rsem, to):
    return pltpu.make_async_remote_copy(
        src_ref=src, dst_ref=dst, send_sem=ssem, recv_sem=rsem, device_id=to, device_id_type=MESH
    )

def arrived(dst, sem):
    pltpu.make_async_copy(dst, dst, sem).wait()

def greet(z, nz, me, others, meanwhile):
    bar = pltpu.get_barrier_semaphore()
    for d in others:
        pl.semaphore_signal(bar, inc=1, device_id=(d, z), device_id_type=MESH)
    @pl.when(z > 0)
    def _():
        pl.semaphore_signal(bar, inc=1, device_id=(me, z - 1), device_id_type=MESH)
    @pl.when(z < nz - 1)
    def _():
        pl.semaphore_signal(bar, inc=1, device_id=(me, z + 1), device_id_type=MESH)
    meanwhile()
    edges = jnp.where(z > 0, 1, 0) + jnp.where(z < nz - 1, 1, 0)
    pl.semaphore_wait(bar, len(others) + edges)


def pack(own, qkv, out, up, down, shared, split):
    band, thin = shared.shape[1], split.shape[1]
    low = [qkv[:, i].astype(bf16) for i in range(3)]
    ot = out[...].T.astype(bf16)
    pieces = [
        low[0][:, :128], low[1][:, :128], low[2][:, :128],
        jnp.concatenate([low[0][:, 128:], low[2][:, 128:]], axis=1),
        jnp.concatenate([low[1][:, 128:], ot[:, 128:]], axis=1),
        ot[:, :128],
    ]
    for i, piece in enumerate(pieces):
        own[0:band, 128 * i : 128 * i + 128] = piece
    own[band : band + 16] = jnp.zeros((16, D), bf16)
    own[band : band + 6, 0:band] = shared[...].astype(bf16)
    own[band : band + 6, 128 : 128 + thin] = split[...].astype(bf16)
    width = D // 4
    for f in range(4):
        own[band + 16 : 2 * band + 16, f * width : (f + 1) * width] = up[:, f].astype(bf16)
        own[2 * band + 16 :, f * width : (f + 1) * width] = down[f].T.astype(bf16)


def gather_kernel(rows_of, *refs):
    nb = len(rows_of)
    masters, outs, own = refs[:6], refs[6 : 6 + nb], refs[6 + nb]
    lsem, zs, zr, ps, pr, ds, dr, cs, cr = refs[7 + nb :]
    z, me = lax.axis_index("tensor"), lax.axis_index("dp")
    nz = lax.axis_size("tensor")
    cp, xp, yp = flip(me, 1), flip(me, 2), flip(me, 4)
    dg = flip(xp, 4)
    pair = (xp, yp)
    greet(z, nz, me, (cp, xp, yp), lambda: pack(own, *masters))

    starts = [sum(rows_of[:b]) for b in range(nb)]
    def own_ref(b):
        return own.at[pl.ds(starts[b], rows_of[b])]
    def right(b, s, src):
        return send(src, outs[b].at[s, me], zs.at[b, 0, z - s], zr.at[b, s], (me, z + 1))
    def left(b, s, src):
        return send(src, outs[b].at[s, me], zs.at[b, 1, s - z], zr.at[b, s], (me, z - 1))
    def side(b, s, src, k):
        return send(src, outs[b].at[s, me], ps.at[b, k, s], pr.at[b, k, s], (pair[k], z))
    def spread(b, s, src):
        for k in range(2):
            side(b, s, src, k).start()
    half = [[(0, r//32*16), (r//32*16, r - r//32*16)] for r in rows_of]
    def diag(b, k):
        lo, n = half[b][k]
        part = outs[b].at[:, pair[k], pl.ds(lo, n)]
        return send(part, part, ds.at[b, k], dr.at[b, k], (pair[1 - k], z))
    def twin(b, j):
        part = outs[b].at[:, (me, xp, yp, dg)[j]]
        return send(part, part, cs.at[b, j], cr.at[b, j], (cp, z))
    keep = [pltpu.make_async_copy(own_ref(b), outs[b].at[z, me], lsem.at[b]) for b in range(nb)]

    def open_block(b):
        @pl.when(z < nz - 1)
        def _():
            right(b, z, own_ref(b)).start()
        @pl.when(z > 0)
        def _():
            left(b, z, own_ref(b)).start()
        spread(b, z, own_ref(b))
        keep[b].start()

    def hop(b, t):
        @pl.when(z >= t)
        def _():
            s = z - t
            arrived(outs[b].at[s, me], zr.at[b, s])
            @pl.when(z < nz - 1)
            def _():
                right(b, s, outs[b].at[s, me]).start()
            spread(b, s, outs[b].at[s, me])
        @pl.when(z + t < nz)
        def _():
            s = z + t
            arrived(outs[b].at[s, me], zr.at[b, s])
            @pl.when(z > 0)
            def _():
                left(b, s, outs[b].at[s, me]).start()
            spread(b, s, outs[b].at[s, me])
    def twin_own(b):
        keep[b].wait()
        twin(b, 0).start()
    def square(b):
        for k in range(2):
            for s in range(4):
                arrived(outs[b].at[s, pair[k]], pr.at[b, k, s])
            diag(b, k).start()
            twin(b, 1 + k).start()
    def corner(b):
        for k in range(2):
            lo, n = half[b][k]
            arrived(outs[b].at[:, dg, pl.ds(lo, n)], dr.at[b, k])
        twin(b, 3).start()
    def finish(b):
        for j, d in enumerate((cp, flip(xp, 1), flip(yp, 1), flip(dg, 1))):
            arrived(outs[b].at[:, d], cr.at[b, j])
    for b in range(nb):
        open_block(b)
    for t in (1, 2, 3):
        for b in range(nb):
            hop(b, t)
    for step in (twin_own, square, corner):
        for b in range(nb):
            step(b)
    for b in range(nb):
        finish(b)
    for b in range(nb):
        for t in range(4):
            @pl.when((z < nz - 1) & (z >= t))
            def _():
                right(b, z - t, outs[b].at[z - t, me]).wait_send()
            @pl.when((z > 0) & (z + t < nz))
            def _():
                left(b, z + t, outs[b].at[z + t, me]).wait_send()
            for k in range(2):
                side(b, t, outs[b].at[t, me], k).wait_send()
            twin(b, t).wait_send()
        for k in range(2):
            diag(b, k).wait_send()

def gather(masters, rows_of, cid=1):
    nb = len(rows_of)
    S = pltpu.SemaphoreType.DMA
    return pl.pallas_call(
        functools.partial(gather_kernel, rows_of),
        out_shape=[jax.ShapeDtypeStruct((4, 8, r, D), bf16) for r in rows_of],
        in_specs=[pl.BlockSpec(memory_space=pltpu.VMEM)] * 6,
        out_specs=[pl.BlockSpec(memory_space=pl.ANY)] * nb,
        scratch_shapes=[pltpu.VMEM((sum(rows_of), D), bf16), S((nb,)), S((nb, 2, 4)), S((nb, 4))]
        + [S((nb, 2, 4))] * 2 + [S((nb, 2))] * 2 + [S((nb, 4))] * 2,
        compiler_params=pltpu.CompilerParams(collective_id=cid, has_side_effects=True),
    )(*masters)


def mm(a, b, dims=NN):
    return lax.dot_general(a, b, dims, preferred_element_type=f32)

def normal_of(rows):
    mean = jnp.mean(rows, axis=-1, keepdims=True)
    centred = rows - mean
    inverse = lax.rsqrt(jnp.mean(centred * centred, axis=-1, keepdims=True) + LN_EPS)
    return centred * inverse, inverse

def normal_back(grad, normal, inverse, gain):
    scaled = grad * gain
    return inverse * (
        scaled
        - jnp.mean(scaled, axis=-1, keepdims=True)
        - normal * jnp.mean(scaled * normal, axis=-1, keepdims=True)
    )

def row_tiles(size):
    return range(0, LEN, size)

def colsum(v):
    return jnp.sum(v, axis=0, keepdims=True)

def compute_kernel(x, cot, valid_col, keybias, vecs, bias, A, B, C,
                   mixed, ig, gA, gB, gC,
                   first_in, second_in, gout_low, gm_low, fT, sT, goT, gmT,
                   qkv, probs, att, middle, acc, acc2, gm, stage, bsum, vrow, sems):
    band = stage.shape[2]
    for r in row_tiles(RL):
        rs = pl.ds(r, RL)
        n, _ = normal_of(x[rs].astype(f32))
        first_in[rs] = (n * vecs[0:1] + vecs[1:2]).astype(bf16)
        go = cot[rs].astype(f32) * valid_col[rs]
        gout_low[rs] = go.astype(bf16)
    fT[...] = first_in[...].T
    goT[...] = gout_low[...].T
    lane = lax.broadcasted_iota(jnp.int32, (1, 128), 1)
    low = lane < 64
    acc[...] = jnp.zeros_like(acc)

    def forward(g, carry):
        w = A.at[g]
        for r in row_tiles(RT):
            rs = pl.ds(r, RT)
            p = mm(first_in[rs], w[...]) + bias[0, g]
            qkv[g, rs] = p.astype(bf16)
        def tile(i):
            return qkv[g, :, 128 * i : 128 * i + 128]
        outs = []
        for h in range(3):
            q, k, v = (tile(0), tile(1), tile(2)) if h < 2 else (tile(3), tile(4), tile(3))
            q = jnp.where(low if h != 1 else ~low, q, 0) * bf16(0.125)
            vt = v.T
            vt = vt[64:] if h else vt[:64]
            cols = []
            for r in row_tiles(RT):
                s = mm(k, q[r : r + RT], NT) + keybias[...]
                top = jnp.max(s, axis=0, keepdims=True)
                e = jnp.exp(s - top)
                p = (e * (1.0 / jnp.sum(e, axis=0, keepdims=True))).astype(bf16)
                probs[g, h, r // RT] = p
                cols.append(mm(vt, p))
            outs.append(jnp.concatenate(cols, axis=1))
        att[g, :, 128:256] = jnp.concatenate(outs[:2], axis=0).T.astype(bf16)
        att[g, :, 0:128] = jnp.concatenate([jnp.zeros_like(outs[2]), outs[2]], axis=0).T.astype(bf16)
        for r in row_tiles(RT):
            rs = pl.ds(r, RT)
            acc[rs] += mm(att[g, rs], w[:, 512:768], NT)
        return carry
    lax.fori_loop(0, 4, forward, 0)

    for r in row_tiles(RL):
        rs = pl.ds(r, RL)
        m = x[rs].astype(f32) + acc[rs] + vecs[2:3]
        middle[rs] = m
        n, _ = normal_of(m)
        second_in[rs] = (n * vecs[3:4] + vecs[4:5]).astype(bf16)
    sT[...] = second_in[...].T
    acc[...] = jnp.zeros_like(acc)
    acc2[...] = jnp.zeros_like(acc2)

    def put(dst, g, slot, compute):
        @pl.when(g > 0)
        def _():
            off(dst, g - 1, slot).wait()
        for c in range(0, D, 2 * band):
            stage[slot, pl.ds(c // band, 2)] = compute(c).astype(bf16).reshape(2, band, D)
        off(dst, g, slot).start()
    def off(dst, g, slot):
        return pltpu.make_async_copy(stage.at[slot], dst.at[g, :, pl.ds(0, band)], sems.at[slot])
    def drain(dst, slot):
        off(dst, 3, slot).wait()

    def mlp(g, carry):
        hid, gps = [], []
        for r in row_tiles(RT):
            rs = pl.ds(r, RT)
            u = mm(second_in[rs], B[g]) + bias[1, g]
            phi = 0.5 * (1.0 + lax.erf(u * SQRT_HALF))
            hidden = (u * phi).astype(bf16)
            slope = phi + u * jnp.exp(-0.5 * u * u) * INV_ROOT_TAU
            gp = (mm(gout_low[rs], C[g]) * slope).astype(bf16)
            acc[rs] += mm(hidden, C[g], NT)
            acc2[rs] += mm(gp, B[g], NT)
            hid.append(hidden)
            gps.append(gp)
        hid = jnp.concatenate(hid, axis=0)
        gps = jnp.concatenate(gps, axis=0)
        bsum[1, g] = colsum(gps.astype(f32))
        put(gC, g, 0, lambda c: mm(goT[pl.ds(c, 2 * band)], hid))
        put(gB, g, 1, lambda c: mm(sT[pl.ds(c, 2 * band)], gps))
        return carry
    lax.fori_loop(0, 4, mlp, 0)
    drain(gC, 0)
    drain(gB, 1)

    sums = [jnp.zeros((1, D), f32) for _ in range(6)]
    for r in row_tiles(RL):
        rs = pl.ds(r, RL)
        m = middle[rs]
        mixed[rs] = ((m + acc[rs] + vecs[5:6]) * valid_col[rs]).astype(bf16)
        n, inv = normal_of(m)
        gn = acc2[rs]
        go = gout_low[rs].astype(f32)
        t = go + normal_back(gn, n, inv, vecs[3:4])
        gm[rs] = t
        gm_low[rs] = t.astype(bf16)
        sums[2] += colsum(t)
        sums[3] += colsum(gn * n)
        sums[4] += colsum(gn)
        sums[5] += colsum(go)
    gmT[...] = gm_low[...].T
    acc[...] = jnp.zeros_like(acc)

    def backward(g, carry):
        w = A.at[g]
        ga = mm(gm_low[...], w[:, 512:768]).astype(bf16)
        def tile(i):
            return qkv[g, :, 128 * i : 128 * i + 128]
        dq, dk, dv = [], [], []
        for h in range(3):
            q, k, v = (tile(0), tile(1), tile(2)) if h < 2 else (tile(3), tile(4), tile(3))
            gt = ga[:, 128:256] if h < 2 else ga[:, 0:128]
            gmask = jnp.where(low if h == 0 else ~low, gt, 0)
            kt = k.T
            kt = kt[64:] if h == 1 else kt[:64]
            dqs, dks, dvs = [], 0.0, 0.0
            for r in row_tiles(RT):
                p = probs[g, h, r // RT]
                dp = mm(v, gmask[r : r + RT], NT)
                pf = p.astype(f32)
                inner = jnp.sum(pf * dp, axis=0, keepdims=True)
                ds = (pf * (dp - inner)).astype(bf16)
                dqs.append(mm(kt, ds))
                dks = dks + mm(ds, q[r : r + RT])
                dvs = dvs + mm(p, gt[r : r + RT])
            dq.append(jnp.concatenate(dqs, axis=1))
            dk.append(dks * 0.125)
            dv.append(dvs)
        dq01 = jnp.concatenate(dq[:2], axis=0).T * 0.125
        dq2 = jnp.concatenate([dq[2], jnp.zeros_like(dq[2])], axis=0).T * 0.125
        parts = [
            dq01,
            jnp.where(low, dk[0], dk[1]),
            jnp.where(low, dv[0], dv[1]),
            jnp.where(low, dq2, dv[2]),
            jnp.where(low, dk[2], 0.0),
        ]
        for i, part in enumerate(parts):
            part = part.astype(bf16)
            qkv[g, :, 128 * i : 128 * i + 128] = part
            bsum[0, g, :, 128 * i : 128 * i + 128] = colsum(part.astype(f32))
        qkv[g, :, 640:768] = jnp.zeros((LEN, 128), bf16)
        bsum[0, g, :, 640:768] = jnp.zeros((1, 128), f32)
        for r in row_tiles(RT):
            rs = pl.ds(r, RT)
            acc[rs] += mm(qkv[g, rs], w[...], NT)
        def grad(c):
            left = mm(fT[pl.ds(c, 2 * band)], qkv[g])
            right = mm(gmT[pl.ds(c, 2 * band)], att[g])
            return jnp.concatenate([left[:, :512], left[:, 512:] + right], axis=1)
        put(gA, g, 0, grad)
        return carry
    lax.fori_loop(0, 4, backward, 0)
    drain(gA, 0)

    for r in row_tiles(RL):
        rs = pl.ds(r, RL)
        n, inv = normal_of(x[rs].astype(f32))
        gn = acc[rs]
        ig[rs] = (gm[rs] + normal_back(gn, n, inv, vecs[0:1])).astype(bf16)
        sums[0] += colsum(gn * n)
        sums[1] += colsum(gn)
    lines = sums + [bsum[i, j] for i in range(2) for j in range(4)] + [jnp.zeros((2, D), f32)]
    lines = jnp.concatenate(lines, axis=0).astype(bf16)
    for i in range(8):
        vrow[i] = lines
    def vecs_out(g):
        return pltpu.make_async_copy(vrow, gA.at[g, :, pl.ds(band, 16)], sems.at[2 + g])
    for g in range(4):
        vecs_out(g).start()
    for g in range(4):
        vecs_out(g).wait()


def compute(x, cot, valid_col, keybias, vecs, bias, A, B, C):
    band = BAND
    V = pltpu.VMEM
    vm = pl.BlockSpec(memory_space=V)
    hb = pl.BlockSpec(memory_space=pl.ANY)
    S = jax.ShapeDtypeStruct
    return pl.pallas_call(
        compute_kernel,
        out_shape=[S((LEN, D), bf16)] * 2 + [S((4, D // band, r, D), bf16) for r in (band + 16, band, band)],
        in_specs=[vm] * 9,
        out_specs=[vm, vm, hb, hb, hb],
        scratch_shapes=[V((LEN, D), bf16)] * 4 + [V((D, LEN), bf16)] * 4 + [
            V((4, LEN, D), bf16), V((4, 3, 3, LEN, RT), bf16), V((4, LEN, 256), bf16),
            V((LEN, D), f32), V((LEN, D), f32), V((LEN, D), f32), V((LEN, D), f32),
            V((2, D // band, band, D), bf16), V((2, 4, 1, D), f32), V((8, 16, D), bf16),
            pltpu.SemaphoreType.DMA((6,)),
        ],
        compiler_params=pltpu.CompilerParams(vmem_limit_bytes=63 * 1024 * 1024),
        cost_estimate=pl.CostEstimate(
            flops=57_000_000_000, bytes_accessed=32_000_000, transcendentals=6_000_000
        ),
    )(x, cot, valid_col, keybias, vecs, bias, A, B, C)


def scatter_kernel(rows_of, *refs):
    nb = len(rows_of)
    grads, (mixed, ig), (mixed_all, ig_all, total) = refs[:nb], refs[nb : nb + 2], refs[nb + 2 : nb + 5]
    refs = refs[nb + 5 :]
    own, got1, got2, got3, gotz = (refs[i * nb : (i + 1) * nb] for i in range(5))
    ls, cs, cr, hs, hr, ss, sr, zs, zr, ms, mr, ml = refs[5 * nb :]
    z, me = lax.axis_index("tensor"), lax.axis_index("dp")
    nz = 4
    cp, xp, yp = flip(me, 1), flip(me, 2), flip(me, 4)
    groups = (me, xp, yp, flip(xp, 4))
    pair = (xp, yp)
    greet(z, nz, me, (cp, xp, yp), lambda: None)
    starts = [sum(rows_of[:b]) for b in range(nb)]
    half = [((0, 48), (48, r - 48)) for r in rows_of]

    full = ((mixed, mixed_all), (ig, ig_all))
    def along(i, s, src, step):
        return send(src, full[i][1].at[s], ms.at[i, (step + 1) // 2, jnp.abs(s - z)], mr.at[i, s], (me, z + step))
    def keep(i):
        return pltpu.make_async_copy(full[i][0], full[i][1].at[z], ml.at[i])
    def open_line(i):
        @pl.when(z < nz - 1)
        def _():
            along(i, z, full[i][0], 1).start()
        @pl.when(z > 0)
        def _():
            along(i, z, full[i][0], -1).start()
        keep(i).start()
    def hop(i, t):
        for side, ok in ((-1, z >= t), (1, z + t < nz)):
            @pl.when(ok)
            def _():
                s = z + side * t
                arrived(full[i][1].at[s], mr.at[i, s])
                @pl.when((z < nz - 1) if side < 0 else (z > 0))
                def _():
                    along(i, s, full[i][1].at[s], -side).start()
    def close_line(i):
        keep(i).wait()
        for t in range(4):
            @pl.when((z < nz - 1) & (z >= t))
            def _():
                along(i, z - t, full[i][1].at[z - t], 1).wait_send()
            @pl.when((z > 0) & (z + t < nz))
            def _():
                along(i, z + t, full[i][1].at[z + t], -1).wait_send()

    def twin(b, j):
        return send(grads[b].at[:, flip(groups[j], 1)], got1[b].at[j], cs.at[b, j], cr.at[b, j], (cp, z))
    def load(b, j):
        return pltpu.make_async_copy(grads[b].at[:, groups[j]], own[b].at[j], ls.at[b, j])
    def corner(b, k):
        lo, n = half[b][k]
        return send(own[b].at[3, :, pl.ds(lo, n)], got2[b].at[:, pl.ds(lo, n)], hs.at[b, k], hr.at[b, k], (pair[k], z))
    def square(b, k):
        return send(own[b].at[1 + k], got3[b].at[k], ss.at[b, k], sr.at[b, k], (pair[k], z))
    def line(b, t, step):
        return send(own[b].at[0, t], gotz[b].at[(1 - step) // 2, t], zs.at[b, t], zr.at[b, (1 - step) // 2, t], (me, z + step))

    def add(dst, *srcs):
        dst[...] = sum((s[...].astype(f32) for s in srcs), dst[...].astype(f32)).astype(bf16)
    def over_z(body):
        lax.fori_loop(0, 4, lambda s, c: (body(s), c)[1], 0)

    def first(b):
        for j in (3, 1, 2, 0):
            twin(b, j).start()
            load(b, j).start()
    def merge(b, j):
        load(b, j).wait()
        arrived(got1[b].at[j], cr.at[b, j])
        over_z(lambda s: add(own[b].at[j, s], got1[b].at[j, s]))
    def second(b):
        merge(b, 3)
        for k in range(2):
            corner(b, k).start()
    def third(b):
        for k in range(2):
            lo, n = half[b][k]
            part = pl.ds(lo, n)
            arrived(got2[b].at[:, part], hr.at[b, k])
            over_z(lambda s: add(own[b].at[2 - k, s, part], got2[b].at[s, part]))
        for k in range(2):
            square(b, k).start()
    def fourth(b):
        for k in range(2):
            arrived(got3[b].at[k], sr.at[b, k])
        over_z(lambda s: add(own[b].at[0, s], got3[b].at[0, s], got3[b].at[1, s]))
        for t in (3, 2, 1):
            @pl.when(z + t < nz)
            def _():
                @pl.when(z > 0)
                def _():
                    arrived(gotz[b].at[0, z + t], zr.at[b, 0, z + t])
                    add(own[b].at[0, z + t], gotz[b].at[0, z + t])
                line(b, z + t, 1).start()
            @pl.when(z >= t)
            def _():
                @pl.when(z < nz - 1)
                def _():
                    arrived(gotz[b].at[1, z - t], zr.at[b, 1, z - t])
                    add(own[b].at[0, z - t], gotz[b].at[1, z - t])
                line(b, z - t, -1).start()
    def last(b):
        span = pl.ds(starts[b], rows_of[b])
        total[span] = own[b][0, z].astype(f32)
        for i, ok in ((0, z > 0), (1, z < nz - 1)):
            @pl.when(ok)
            def _():
                arrived(gotz[b].at[i, z], zr.at[b, i, z])
                total[span] += gotz[b][i, z].astype(f32)
    def close(b):
        for j in range(4):
            twin(b, j).wait_send()
        for k in range(2):
            corner(b, k).wait_send()
            square(b, k).wait_send()
        for t in (3, 2, 1):
            @pl.when(z + t < nz)
            def _():
                line(b, z + t, 1).wait_send()
            @pl.when(z >= t)
            def _():
                line(b, z - t, -1).wait_send()
    def rest(b):
        for j in (1, 2, 0):
            merge(b, j)

    for b in (2, 1, 0):
        first(b)
    open_line(0)
    open_line(1)
    second(2)
    rest(2)
    second(1)
    rest(1)
    third(2)
    second(0)
    rest(0)
    hop(0, 1)
    third(1)
    fourth(2)
    hop(1, 1)
    third(0)
    fourth(1)
    hop(0, 2)
    last(2)
    fourth(0)
    hop(1, 2)
    last(1)
    hop(0, 3)
    last(0)
    hop(1, 3)
    for i in range(2):
        close_line(i)
    for b in range(3):
        close(b)


def scatter(grads, mixed, ig, cid=2):
    rows_of = [g.shape[2] for g in grads]
    nb = len(rows_of)
    S, V = pltpu.SemaphoreType.DMA, pltpu.VMEM
    hb = pl.BlockSpec(memory_space=pl.ANY)
    scratch = [V((4, 4, r, D), bf16) for r in rows_of] + [V((4, 4, r, D), bf16) for r in rows_of]
    scratch += [V((4, r, D), bf16) for r in rows_of] + [V((2, 4, r, D), bf16) for r in rows_of] * 2
    scratch += [S((nb, 4))] * 3 + [S((nb, 2))] * 4 + [S((nb, 4)), S((nb, 2, 4)), S((2, 2, 4)), S((2, 4)), S((2,))]
    return pl.pallas_call(
        functools.partial(scatter_kernel, rows_of),
        out_shape=[jax.ShapeDtypeStruct((4, LEN, D), bf16)] * 2 + [jax.ShapeDtypeStruct((sum(rows_of), D), f32)],
        in_specs=[hb] * (nb + 2),
        out_specs=[hb, hb, pl.BlockSpec(memory_space=V)],
        scratch_shapes=scratch,
        compiler_params=pltpu.CompilerParams(collective_id=cid, has_side_effects=True, vmem_limit_bytes=60 * 1024 * 1024),
    )(*grads, mixed, ig)


def step_kernel(total, *refs):
    ins, outs = refs[:18], refs[18:]
    z, me = lax.axis_index("tensor"), lax.axis_index("dp")
    band, thin = ins[12].shape[1], ins[15].shape[1]
    vec = total[band : band + 16]
    row = lax.broadcasted_iota(jnp.int32, (D, 128), 0)
    col = lax.broadcasted_iota(jnp.int32, (D, 128), 1)

    def pick(source):
        chosen = jnp.where(row == source, 1.0, 0.0)
        return lax.dot_general(
            vec, chosen, NN, precision=lax.Precision.HIGHEST, preferred_element_type=f32
        )

    place = me * thin + col
    shared = pick(me * band + col)[:6, :band]
    head = jnp.where(place < 128, place, place + 256)
    late = jnp.where(place < 128, place + 256, place + 320)
    spots = [head, late] + [f * (D // 4) + place for f in range(4)]
    at = lax.broadcasted_iota(jnp.int32, (16, 128), 0)
    lines = []
    for i, spot in enumerate(spots):
        mine = jnp.where(at == z + (6 if i < 2 else 10), pick(spot), 0.0)
        lines.append(jnp.sum(mine, axis=0, keepdims=True)[:, :thin])
    split = jnp.concatenate(lines, axis=0)

    def apply(kind, where, gradient):
        rates, decays = kind_rates(), (MATRIX_DECAY,) * 4 + (0.0, 0.0)
        m, f, s = (ins[3 * kind + i][where] for i in range(3))
        results = adamw(m, f, s, gradient, rates[kind], decays[kind])
        for i in range(4):
            outs[4 * kind + i][where] = results[i]

    attn = total[:band]
    def pair(a, b):
        return jnp.concatenate([attn[:, a : a + 128], attn[:, b : b + 64]], axis=1)
    apply(0, (slice(None), 0), pair(0, 384))
    apply(0, (slice(None), 1), pair(128, 512))
    apply(0, (slice(None), 2), pair(256, 448))
    apply(1, (slice(None),), pair(640, 576).T)
    up = total[band + 16 : 2 * band + 16]
    down = total[2 * band + 16 :]
    down = down.T
    width = D // 4
    for f in range(4):
        apply(2, (slice(None), f), up[:, f * width : (f + 1) * width])
        apply(3, (f,), down[f * width : (f + 1) * width])
    apply(4, (slice(None),), shared)
    apply(5, (slice(None),), split)


def step(total, state):
    vm = pl.BlockSpec(memory_space=pltpu.VMEM)
    shapes = []
    for kind in range(6):
        shape = state[3 * kind].shape
        shapes += [jax.ShapeDtypeStruct(shape, t) for t in (f32, bf16, f32, f32)]
    return pl.pallas_call(
        step_kernel,
        out_shape=shapes,
        in_specs=[vm] * 19,
        out_specs=[vm] * 24,
        compiler_params=pltpu.CompilerParams(vmem_limit_bytes=56 * 1024 * 1024),
    )(total, *state)


def pack_attention(qkv, out):
    q, k, v = qkv[:, 0], qkv[:, 1], qkv[:, 2]
    return jnp.concatenate(
        [
            q[:, :128], k[:, :128], v[:, :128],
            q[:, 128:], v[:, 128:], k[:, 128:], out[:, 128:], out[:, :128],
        ],
        axis=1,
    )


def unpack_attention(block):
    pair = [block[:, 128 * i : 128 * i + 128] for i in range(6)]
    q = jnp.concatenate([pair[0], pair[3][:, :64]], axis=1)
    k = jnp.concatenate([pair[1], pair[4][:, :64]], axis=1)
    v = jnp.concatenate([pair[2], pair[3][:, 64:]], axis=1)
    o = jnp.concatenate([pair[5], pair[4][:, 64:]], axis=1)
    return jnp.stack([q, k, v], axis=1), o


def gather_plain(masters):
    qkv, out, up, down, shared, split = (t.astype(bf16) for t in masters)
    band, thin, width = shared.shape[1], split.shape[1], down.shape[1] * lax.axis_size("tensor")
    groups, copies = lax.axis_size("tensor"), lax.axis_size("dp")
    vecs = jnp.zeros((16, width), bf16).at[:6, :band].set(shared).at[:6, 128 : 128 + thin].set(split)
    own = jnp.concatenate(
        [pack_attention(qkv, out.T), vecs, up.reshape(band, -1), down.reshape(-1, band).T]
    )
    whole = lax.all_gather(own, AXES).reshape(groups, copies, -1, width)
    return jnp.split(whole, [band + 16, 2 * band + 16], axis=2)


def step_plain(grads, mixed, grad_inputs, state):
    masters, firsts, seconds = state[0::3], state[1::3], state[2::3]
    band, thin = masters[4].shape[1], masters[5].shape[1]
    groups, copies = lax.axis_size("tensor"), lax.axis_size("dp")
    z, at = lax.axis_index("tensor"), lax.axis_index("dp")
    width = grads[0].shape[-1]
    summed = [
        lax.psum_scatter(
            g[:, :, :BAND].reshape(groups * copies, band, width), AXES, scatter_dimension=0
        ).astype(f32)
        for g in grads
    ]
    vec = lax.psum(grads[0][0, 0, BAND:].astype(f32), AXES)
    shared = lax.dynamic_slice_in_dim(vec[:6], at * band, band, 1)
    cols = lax.dynamic_slice_in_dim(vec[6:10], z, 1, 0)[0]
    ups = lax.dynamic_slice_in_dim(vec[10:14], z, 1, 0).reshape(-1, width // groups)
    split = jnp.stack(
        [
            jnp.concatenate([cols[:128], cols[384:448]]),
            jnp.concatenate([cols[256:384], cols[448:512]]),
        ]
    )
    split = lax.dynamic_slice_in_dim(jnp.concatenate([split, ups]), at * thin, thin, 1)
    sum_qkv, sum_out = unpack_attention(summed[0])
    gradients = (
        sum_qkv,
        sum_out.T,
        summed[1].reshape(masters[2].shape),
        summed[2].T.reshape(masters[3].shape),
        shared,
        split,
    )
    decays = (MATRIX_DECAY, MATRIX_DECAY, MATRIX_DECAY, MATRIX_DECAY, 0.0, 0.0)
    rates = kind_rates()
    outputs = []
    for kind in range(6):
        outputs.extend(
            adamw(masters[kind], firsts[kind], seconds[kind], gradients[kind], rates[kind], decays[kind])
        )
    mixed, grad_inputs = (lax.all_gather(t, "tensor") for t in (mixed, grad_inputs))
    return mixed, grad_inputs, outputs


def local(tokens, cotangent, counts, *state):
    masters = state[0::3]
    shared_master, split_master = masters[4:]
    groups = lax.axis_size("tensor")
    copies = lax.axis_size("dp")
    seq_count, length, width = tokens.shape
    share = seq_count // groups
    mine = lax.axis_index("tensor") * share
    band = shared_master.shape[1]
    thin = split_master.shape[1]
    linked = (groups, copies) == (4, 8)

    if linked:
        mats = gather(masters, (band + 16, band, band))
    else:
        mats = gather_plain(masters)
    vec_all = mats[0][:, :, band:].astype(f32)
    attn_all, up_all, down_all = (t[:, :, :band].reshape(groups, width, width) for t in mats)
    shared_vecs = jnp.swapaxes(vec_all[0, :, :6, :band], 0, 1).reshape(6, width)
    split_vecs = vec_all[:, :, :6, 128 : 128 + thin].reshape(groups, copies, 6, thin)
    split_vecs = jnp.swapaxes(split_vecs, 1, 2).reshape(groups, 6, copies * thin)
    bq, bv = split_vecs[:, 0], split_vecs[:, 1]
    zero = jnp.zeros((groups, 128), f32)
    attn_bias = jnp.concatenate(
        [bq[:, :128], zero, bv[:, :128], bq[:, 128:], bv[:, 128:], zero, zero], axis=1
    )
    up_bias = split_vecs[:, 2:].reshape(groups, width)
    bias = jnp.stack([attn_bias, up_bias]).reshape(2, groups, 1, width)

    x = lax.dynamic_slice_in_dim(tokens, mine, share, 0).reshape(length, width)
    cot = lax.dynamic_slice_in_dim(cotangent, mine, share, 0).reshape(length, width)
    count = lax.dynamic_slice_in_dim(counts, mine, share, 0)
    valid = lax.broadcasted_iota(jnp.int32, (length, 1), 0) < count
    mixed, grad_inputs, *grads = compute(
        x, cot, valid.astype(f32), jnp.where(valid, 0.0, MASK_FILL), shared_vecs, bias,
        attn_all, up_all, down_all,
    )
    if linked:
        mixed, grad_inputs, total = scatter(grads, mixed, grad_inputs)
        outputs = step(total, state)
    else:
        mixed, grad_inputs, outputs = step_plain(grads, mixed, grad_inputs, state)
    return (mixed, grad_inputs.astype(f32), *outputs)


def solution(mesh):
    rows = P("dp", None, None)
    state = (
        P("dp", None, "tensor"),
        P("tensor", "dp"),
        P("dp", None, "tensor"),
        P(None, "tensor", "dp"),
        P(None, "dp"),
        P(None, ("tensor", "dp")),
    )
    in_specs = (rows, rows, P("dp")) + tuple(s for s in state for _ in range(3))
    out_specs = (rows, rows) + tuple(s for s in state for _ in range(4))
    return jax.shard_map(local, mesh=mesh, in_specs=in_specs, out_specs=out_specs, check_vma=False)
```

```python
import functools

import jax
import jax.numpy as jnp
from jax import lax
from jax.experimental import pallas as pl
from jax.experimental.pallas import tpu as pltpu
from jax.sharding import PartitionSpec as P

D = 768
FF = 3072
HEAD_DIM = 64
LEN = 576
STEP = 10


LN_EPS = 1e-05
MASK_FILL = -1e30
BETA_ONE = 0.5
BETA_TWO = 0.5
ADAM_EPS = 1e-08
MATRIX_DECAY = 0.01
SQRT_HALF = 0.7071067811865476
INV_ROOT_TAU = 0.3989422804014327
AXES = ("tensor", "dp")
MESH = pl.DeviceIdType.MESH
bf16, f32 = jnp.bfloat16, jnp.float32
NN = (((1,), (0,)), ((), ()))
NT = (((1,), (1,)), ((), ()))
RT = 192
RL = 96
BAND = 96


def kind_rates():
    return (
        0.7 * D ** (-0.5),
        0.7 * (D * 16 // LEN) ** (-0.5),
        0.7 * D ** (-0.5),
        0.7 * FF ** (-0.5),
        0.6,
        0.4,
    )


def adamw(master, first, second, gradient, step_rate, decay_rate):
    first_new = BETA_ONE * first + (1.0 - BETA_ONE) * gradient
    second_new = BETA_TWO * second + (1.0 - BETA_TWO) * gradient * gradient
    first_hat = first_new / (1.0 - BETA_ONE**STEP)
    second_hat = second_new / (1.0 - BETA_TWO**STEP)
    master_new = master - step_rate * (
        first_hat / (jnp.sqrt(second_hat) + ADAM_EPS) + decay_rate * master
    )
    return (master_new, master_new.astype(jnp.bfloat16), first_new, second_new)


def flip(index, bit):
    return index + bit - 2 * bit * lax.rem(lax.div(index, bit), 2)

def send(src, dst, ssem, rsem, to):
    return pltpu.make_async_remote_copy(
        src_ref=src, dst_ref=dst, send_sem=ssem, recv_sem=rsem, device_id=to, device_id_type=MESH
    )

def arrived(dst, sem):
    pltpu.make_async_copy(dst, dst, sem).wait()

def greet(z, nz, me, others, meanwhile):
    bar = pltpu.get_barrier_semaphore()
    for d in others:
        pl.semaphore_signal(bar, inc=1, device_id=(d, z), device_id_type=MESH)
    @pl.when(z > 0)
    def _():
        pl.semaphore_signal(bar, inc=1, device_id=(me, z - 1), device_id_type=MESH)
    @pl.when(z < nz - 1)
    def _():
        pl.semaphore_signal(bar, inc=1, device_id=(me, z + 1), device_id_type=MESH)
    meanwhile()
    edges = jnp.where(z > 0, 1, 0) + jnp.where(z < nz - 1, 1, 0)
    pl.semaphore_wait(bar, len(others) + edges)


def mm(a, b, dims=NN):
    return lax.dot_general(a, b, dims, preferred_element_type=f32)

def normal_of(rows):
    mean = jnp.mean(rows, axis=-1, keepdims=True)
    centred = rows - mean
    inverse = lax.rsqrt(jnp.mean(centred * centred, axis=-1, keepdims=True) + LN_EPS)
    return centred * inverse, inverse

def normal_back(grad, normal, inverse, gain):
    scaled = grad * gain
    return inverse * (
        scaled
        - jnp.mean(scaled, axis=-1, keepdims=True)
        - normal * jnp.mean(scaled * normal, axis=-1, keepdims=True)
    )

def row_tiles(size):
    return range(0, LEN, size)

def colsum(v):
    return jnp.sum(v, axis=0, keepdims=True)

def pack(own, pad, qkv, out, up, down, shared, split):
    band, thin = shared.shape[1], split.shape[1]
    me = lax.axis_index("dp")
    low = [qkv[:, i].astype(bf16) for i in range(3)]
    ot = out[...].T.astype(bf16)
    pieces = [
        low[0][:, :128], low[1][:, :128], low[2][:, :128],
        jnp.concatenate([low[0][:, 128:], low[2][:, 128:]], axis=1),
        jnp.concatenate([low[1][:, 128:], ot[:, 128:]], axis=1),
        ot[:, :128],
    ]
    for i, piece in enumerate(pieces):
        own[0:band, 128 * i : 128 * i + 128] = piece
    width = D // 4
    for f in range(4):
        own[band + 16 : 2 * band + 16, f * width : (f + 1) * width] = up[:, f].astype(bf16)
        own[2 * band + 16 :, f * width : (f + 1) * width] = down[f].T.astype(bf16)
    pad[...] = jnp.zeros_like(pad)
    pad[0:6, 0:band] = shared[...]
    pad[8:14, 0:thin] = split[...]
    vals = pad[...].astype(bf16)
    src = lax.broadcasted_iota(jnp.int32, (128, D), 0)
    col = lax.broadcasted_iota(jnp.int32, (128, D), 1)

    def placed(spot):
        return mm(vals, jnp.where(col == spot, 1.0, 0.0).astype(bf16))

    at = me * thin + src
    attn = placed(jnp.where(at < 128, at, at + 256))[8:9]
    attn += placed(jnp.where(at < 128, at + 256, at + 320))[9:10]
    ups = sum(placed(f * width + at)[10 + f : 11 + f] for f in range(4))
    rows = [placed(me * band + src)[0:6], attn, ups, jnp.zeros((8, D), f32)]
    own[band : band + 16] = jnp.concatenate(rows, axis=0).astype(bf16)


def gather_steps(own, outs, masters_rows, z, me, sems):
    rows_of = masters_rows
    nb, nz = len(rows_of), 4
    lsem, zs, zr, ps, pr, ds, dr, cs, cr = sems
    cp, xp, yp = flip(me, 1), flip(me, 2), flip(me, 4)
    dg = flip(xp, 4)
    pair = (xp, yp)
    starts = [sum(rows_of[:b]) for b in range(nb)]
    half = [[(0, 48), (48, r - 48)] for r in rows_of]

    def own_ref(b):
        return own.at[pl.ds(starts[b], rows_of[b])]
    def right(b, s, src):
        return send(src, outs[b].at[s, me], zs.at[b, 0, z - s], zr.at[b, s], (me, z + 1))
    def left(b, s, src):
        return send(src, outs[b].at[s, me], zs.at[b, 1, s - z], zr.at[b, s], (me, z - 1))
    def side(b, s, src, k):
        return send(src, outs[b].at[s, me], ps.at[b, k, s], pr.at[b, k, s], (pair[k], z))
    def spread(b, s, src):
        for k in range(2):
            side(b, s, src, k).start()
    def diag(b, k):
        lo, n = half[b][k]
        part = outs[b].at[:, pair[k], pl.ds(lo, n)]
        return send(part, part, ds.at[b, k], dr.at[b, k], (pair[1 - k], z))
    def twin(b, j):
        part = outs[b].at[:, (me, xp, yp, dg)[j]]
        return send(part, part, cs.at[b, j], cr.at[b, j], (cp, z))
    def keep(b):
        return pltpu.make_async_copy(own_ref(b), outs[b].at[z, me], lsem.at[b])

    def opens(b):
        @pl.when(z < nz - 1)
        def _():
            right(b, z, own_ref(b)).start()
        @pl.when(z > 0)
        def _():
            left(b, z, own_ref(b)).start()
        spread(b, z, own_ref(b))
        keep(b).start()
    def hop(b, t):
        @pl.when(z >= t)
        def _():
            s = z - t
            arrived(outs[b].at[s, me], zr.at[b, s])
            @pl.when(z < nz - 1)
            def _():
                right(b, s, outs[b].at[s, me]).start()
            spread(b, s, outs[b].at[s, me])
        @pl.when(z + t < nz)
        def _():
            s = z + t
            arrived(outs[b].at[s, me], zr.at[b, s])
            @pl.when(z > 0)
            def _():
                left(b, s, outs[b].at[s, me]).start()
            spread(b, s, outs[b].at[s, me])
    def lined(b):
        keep(b).wait()
        twin(b, 0).start()
    def square(b):
        for k in range(2):
            for s in range(4):
                arrived(outs[b].at[s, pair[k]], pr.at[b, k, s])
            diag(b, k).start()
            twin(b, 1 + k).start()
    def corner(b):
        for k in range(2):
            lo, n = half[b][k]
            arrived(outs[b].at[:, dg, pl.ds(lo, n)], dr.at[b, k])
        twin(b, 3).start()
    def ready(b):
        for j, d in enumerate((cp, flip(xp, 1), flip(yp, 1), flip(dg, 1))):
            arrived(outs[b].at[:, d], cr.at[b, j])
    def sent(b):
        for t in range(4):
            @pl.when((z < nz - 1) & (z >= t))
            def _():
                right(b, z - t, outs[b].at[z - t, me]).wait_send()
            @pl.when((z > 0) & (z + t < nz))
            def _():
                left(b, z + t, outs[b].at[z + t, me]).wait_send()
            for k in range(2):
                side(b, t, outs[b].at[t, me], k).wait_send()
            twin(b, t).wait_send()
        for k in range(2):
            diag(b, k).wait_send()
    return opens, hop, lined, square, corner, ready, sent


def line_steps(block, whole, z, me, sems):
    nz = 4
    ms, mr, ml = sems

    def along(s, src, way):
        return send(src, whole.at[s], ms.at[(way + 1) // 2, jnp.abs(s - z)], mr.at[s], (me, z + way))
    def keep():
        return pltpu.make_async_copy(block, whole.at[z], ml.at[0])
    def opens():
        @pl.when(z < nz - 1)
        def _():
            along(z, block, 1).start()
        @pl.when(z > 0)
        def _():
            along(z, block, -1).start()
        keep().start()
    def hop(t):
        for way, ok in ((-1, z >= t), (1, z + t < nz)):
            @pl.when(ok)
            def _():
                s = z + way * t
                arrived(whole.at[s], mr.at[s])
                @pl.when((z < nz - 1) if way < 0 else (z > 0))
                def _():
                    along(s, whole.at[s], -way).start()
    def close():
        keep().wait()
        for t in range(4):
            @pl.when((z < nz - 1) & (z >= t))
            def _():
                along(z - t, whole.at[z - t], 1).wait_send()
            @pl.when((z > 0) & (z + t < nz))
            def _():
                along(z + t, whole.at[z + t], -1).wait_send()
    return opens, hop, close


QT = ((0, 256), (256, 256), (512, 64))


def layer_kernel(linked, *refs):
    tokens, cotangent, counts = refs[:3]
    weights_in = refs[3 : 9 if linked else 6]
    refs = refs[9 if linked else 6 :]
    mixed_all, ig_out, gA, gB, gC = refs[:5]
    (WA, WB, WC, x, gout_low, first_in, second_in, gm_low, left_t, right_t, qkv, probs, att,
     middle, acc, acc2, hidden, slope, stage, bsum, vrow, vecs, bias, mixed, sems) = refs[5:30]
    z, me = lax.axis_index("tensor"), lax.axis_index("dp")
    band = BAND
    if linked:
        own, pad = refs[30:32]
        opens, hop, lined, square, corner, ready, sent = gather_steps(
            own, (WA, WB, WC), (band + 16, band, band), z, me, refs[32:41]
        )
        mopen, mhop, mclose = line_steps(mixed, mixed_all, z, me, refs[41:44])
    else:
        def nothing(*args):
            return None
        opens = hop = lined = square = corner = sent = mhop = nothing
        def ready(b):
            pltpu.make_async_copy(weights_in[b], (WA, WB, WC)[b], sems.at[8 + b]).wait()
        def mopen():
            pltpu.make_async_copy(mixed, mixed_all, sems.at[11]).start()
        def mclose():
            pltpu.make_async_copy(mixed, mixed_all, sems.at[11]).wait()

    loads = [
        pltpu.make_async_copy(tokens.at[z], x, sems.at[6]),
        pltpu.make_async_copy(cotangent.at[z], gout_low, sems.at[7]),
    ]
    for load in loads:
        load.start()
    if linked:
        greet(z, 4, me, (flip(me, 1), flip(me, 2), flip(me, 4)), lambda: pack(own, pad, *weights_in))
    else:
        for b in range(3):
            pltpu.make_async_copy(weights_in[b], (WA, WB, WC)[b], sems.at[8 + b]).start()
    count = counts[z]
    column = lax.broadcasted_iota(jnp.int32, (LEN, 1), 0)
    keybias = jnp.where(column < count, 0.0, MASK_FILL)
    def valid(r):
        return jnp.where(lax.broadcasted_iota(jnp.int32, (RL, 1), 0) + r < count, 1.0, 0.0)

    opens(0)
    for load in loads:
        load.wait()
    for r in row_tiles(RL):
        rs = pl.ds(r, RL)
        gout_low[rs] = (gout_low[rs].astype(f32) * valid(r)).astype(bf16)
        middle[rs] = normal_of(x[rs].astype(f32))[0]
    hop(0, 1)
    hop(0, 2)
    opens(1)
    right_t[...] = gout_low[...].T
    hop(0, 3)
    lined(0)
    square(0)
    hop(1, 1)
    hop(1, 2)
    opens(2)
    hop(1, 3)
    lined(1)
    corner(0)
    ready(0)
    lines = [sum(WA[g, i, band : band + 16].astype(f32) for i in range(8)) for g in range(4)]
    vecs[...] = lines[0]
    for g in range(4):
        bias[0, g] = lines[g][6:7]
        bias[1, g] = lines[g][7:8]
    for r in row_tiles(RL):
        rs = pl.ds(r, RL)
        first_in[rs] = (middle[rs] * vecs[0:1] + vecs[1:2]).astype(bf16)
    lane = lax.broadcasted_iota(jnp.int32, (1, 128), 1)
    low = lane < 64
    acc[...] = jnp.zeros_like(acc)

    def at(g, table):
        for i, steps in enumerate(table):
            if steps:
                @pl.when(g == i)
                def _():
                    for step, *args in steps:
                        step(*args)
    def wa(g, lo=0, hi=D):
        return WA[g, :, 0:band, lo:hi].reshape(D, hi - lo)
    def wb(g):
        return WB[g].reshape(D, D)
    def wc(g):
        return WC[g].reshape(D, D)

    def forward(g, carry):
        for r in row_tiles(RT):
            rs = pl.ds(r, RT)
            qkv[g, rs] = (mm(first_in[rs], wa(g)) + bias[0, g]).astype(bf16)
        def tile(i):
            return qkv[g, :, 128 * i : 128 * i + 128]
        outs = []
        for h in range(3):
            q, k, v = (tile(0), tile(1), tile(2)) if h < 2 else (tile(3), tile(4), tile(3))
            q = jnp.where(low if h != 1 else ~low, q, 0) * bf16(0.125)
            vt = v.T
            vt = vt[64:] if h else vt[:64]
            cols = []
            for r, n in QT:
                s = mm(k, q[r : r + n], NT) + keybias
                e = jnp.exp(s - jnp.max(s, axis=0, keepdims=True))
                p = (e * (1.0 / jnp.sum(e, axis=0, keepdims=True))).astype(bf16)
                probs[g, h, :, pl.ds(r, n)] = p
                cols.append(mm(vt, p))
            outs.append(jnp.concatenate(cols, axis=1))
        att[g, :, 128:256] = jnp.concatenate(outs[:2], axis=0).T.astype(bf16)
        att[g, :, 0:128] = jnp.concatenate([jnp.zeros_like(outs[2]), outs[2]], axis=0).T.astype(bf16)
        for r in row_tiles(RT):
            rs = pl.ds(r, RT)
            acc[rs] += mm(att[g, rs], wa(g, 512, D), NT)
        at(g, [[(hop, 2, 1), (hop, 2, 2)], [(hop, 2, 3), (lined, 2), (square, 1)], [(corner, 1)], []])
        return carry
    lax.fori_loop(0, 4, forward, 0)

    for r in row_tiles(RL):
        rs = pl.ds(r, RL)
        m = x[rs].astype(f32) + acc[rs] + vecs[2:3]
        middle[rs] = m
        second_in[rs] = (normal_of(m)[0] * vecs[3:4] + vecs[4:5]).astype(bf16)
    left_t[...] = second_in[...].T
    acc[...] = jnp.zeros_like(acc)
    acc2[...] = jnp.zeros_like(acc2)
    ready(1)

    def mlp_up(g, carry):
        for r in row_tiles(RT):
            rs = pl.ds(r, RT)
            u = mm(second_in[rs], wb(g)) + bias[1, g]
            phi = 0.5 * (1.0 + lax.erf(u * SQRT_HALF))
            hidden[g, rs] = (u * phi).astype(bf16)
            slope[g, rs] = (phi + u * jnp.exp(-0.5 * u * u) * INV_ROOT_TAU).astype(bf16)
        at(g, [[], [(square, 2)], [], []])
        return carry
    lax.fori_loop(0, 4, mlp_up, 0)
    corner(2)
    ready(2)

    def mlp_down(g, carry):
        for r in row_tiles(RT):
            rs = pl.ds(r, RT)
            acc[rs] += mm(hidden[g, rs], wc(g), NT)
        return carry
    lax.fori_loop(0, 4, mlp_down, 0)
    for r in row_tiles(RL):
        rs = pl.ds(r, RL)
        mixed[rs] = ((middle[rs] + acc[rs] + vecs[5:6]) * valid(r)).astype(bf16)
    mopen()

    def off(dst, g, slot):
        return pltpu.make_async_copy(stage.at[slot], dst.at[g, :, pl.ds(0, band)], sems.at[slot])
    def put(dst, g, slot, part):
        @pl.when(g > 0)
        def _():
            off(dst, g - 1, slot).wait()
        for c in range(0, D, 2 * band):
            stage[slot, pl.ds(c // band, 2)] = part(c).astype(bf16).reshape(2, band, D)
        off(dst, g, slot).start()

    def mlp_back(g, carry):
        for r in row_tiles(RT):
            rs = pl.ds(r, RT)
            gp = (mm(gout_low[rs], wc(g)) * slope[g, rs].astype(f32)).astype(bf16)
            slope[g, rs] = gp
            acc2[rs] += mm(gp, wb(g), NT)
        bsum[1, g] = colsum(slope[g].astype(f32))
        put(gC, g, 0, lambda c: mm(right_t[pl.ds(c, 2 * band)], hidden[g]))
        put(gB, g, 1, lambda c: mm(left_t[pl.ds(c, 2 * band)], slope[g]))
        return carry
    lax.fori_loop(0, 4, mlp_back, 0)
    off(gC, 3, 0).wait()
    off(gB, 3, 1).wait()

    sums = [jnp.zeros((1, D), f32) for _ in range(6)]
    for r in row_tiles(RL):
        rs = pl.ds(r, RL)
        n, inv = normal_of(middle[rs])
        gn = acc2[rs]
        go = gout_low[rs].astype(f32)
        t = go + normal_back(gn, n, inv, vecs[3:4])
        middle[rs] = t
        gm_low[rs] = t.astype(bf16)
        sums[2] += colsum(t)
        sums[3] += colsum(gn * n)
        sums[4] += colsum(gn)
        sums[5] += colsum(go)
    left_t[...] = first_in[...].T
    right_t[...] = gm_low[...].T
    acc[...] = jnp.zeros_like(acc)

    def backward(g, carry):
        ga = mm(gm_low[...], wa(g, 512, D)).astype(bf16)
        def tile(i):
            return qkv[g, :, 128 * i : 128 * i + 128]
        dq, dk, dv = [], [], []
        for h in range(3):
            q, k, v = (tile(0), tile(1), tile(2)) if h < 2 else (tile(3), tile(4), tile(3))
            gt = ga[:, 128:256] if h < 2 else ga[:, 0:128]
            gmask = jnp.where(low if h == 0 else ~low, gt, 0)
            kt = k.T
            kt = kt[64:] if h == 1 else kt[:64]
            dqs, dks, dvs = [], 0.0, 0.0
            for r, n in QT:
                p = probs[g, h, :, pl.ds(r, n)]
                dp = mm(v, gmask[r : r + n], NT)
                pf = p.astype(f32)
                inner = jnp.sum(pf * dp, axis=0, keepdims=True)
                ds = (pf * (dp - inner)).astype(bf16)
                dqs.append(mm(kt, ds))
                dks = dks + mm(ds, q[r : r + n])
                dvs = dvs + mm(p, gt[r : r + n])
            dq.append(jnp.concatenate(dqs, axis=1))
            dk.append(dks * 0.125)
            dv.append(dvs)
        dq01 = jnp.concatenate(dq[:2], axis=0).T * 0.125
        dq2 = jnp.concatenate([dq[2], jnp.zeros_like(dq[2])], axis=0).T * 0.125
        parts = [
            dq01,
            jnp.where(low, dk[0], dk[1]),
            jnp.where(low, dv[0], dv[1]),
            jnp.where(low, dq2, dv[2]),
            jnp.where(low, dk[2], 0.0),
        ]
        for i, part in enumerate(parts):
            part = part.astype(bf16)
            qkv[g, :, 128 * i : 128 * i + 128] = part
            bsum[0, g, :, 128 * i : 128 * i + 128] = colsum(part.astype(f32))
        qkv[g, :, 640:768] = jnp.zeros((LEN, 128), bf16)
        bsum[0, g, :, 640:768] = jnp.zeros((1, 128), f32)
        for r in row_tiles(RT):
            rs = pl.ds(r, RT)
            acc[rs] += mm(qkv[g, rs], wa(g), NT)
        def part(c):
            first = mm(left_t[pl.ds(c, 2 * band)], qkv[g])
            second = mm(right_t[pl.ds(c, 2 * band)], att[g])
            return jnp.concatenate([first[:, :512], first[:, 512:] + second], axis=1)
        put(gA, g, 0, part)
        at(g, [[(mhop, 1)], [], [(mhop, 2)], []])
        return carry
    lax.fori_loop(0, 4, backward, 0)

    for r in row_tiles(RL):
        rs = pl.ds(r, RL)
        n, inv = normal_of(x[rs].astype(f32))
        gn = acc[rs]
        first_in[rs] = (middle[rs] + normal_back(gn, n, inv, vecs[0:1])).astype(bf16)
        sums[0] += colsum(gn * n)
        sums[1] += colsum(gn)
    ig_copy = pltpu.make_async_copy(first_in, ig_out, sems.at[1])
    ig_copy.start()
    lines = sums + [bsum[i, j] for i in range(2) for j in range(4)] + [jnp.zeros((2, D), f32)]
    lines = jnp.concatenate(lines, axis=0).astype(bf16)
    for i in range(8):
        vrow[i] = lines
    def vecs_out(g):
        return pltpu.make_async_copy(vrow, gA.at[g, :, pl.ds(band, 16)], sems.at[2 + g])
    for g in range(4):
        vecs_out(g).start()
    mhop(3)
    off(gA, 3, 0).wait()
    ig_copy.wait()
    for g in range(4):
        vecs_out(g).wait()
    mclose()
    for b in range(3):
        sent(b)


def layer(linked, tokens, cotangent, counts, weights, cid=1):
    V, S = pltpu.VMEM, pltpu.SemaphoreType.DMA
    shape = jax.ShapeDtypeStruct
    hb, vm = pl.BlockSpec(memory_space=pl.ANY), pl.BlockSpec(memory_space=V)
    band, nb = BAND, 3
    rows_of = (band + 16, band, band)
    mixed_shape = (4, LEN, D) if linked else (LEN, D)
    scratch = [V((4, 8, r, D), bf16) for r in rows_of]
    scratch += [V((LEN, D), bf16)] * 5 + [V((D, LEN), bf16)] * 2
    scratch += [V((4, LEN, D), bf16), V((4, 3, LEN, LEN), bf16), V((4, LEN, 256), bf16)]
    scratch += [V((LEN, D), f32)] * 3 + [V((4, LEN, D), bf16)] * 2
    scratch += [V((2, 8, band, D), bf16), V((2, 4, 1, D), f32), V((8, 16, D), bf16), V((16, D), f32)]
    scratch += [V((2, 4, 1, D), f32), V((LEN, D), bf16), S((12,))]
    if linked:
        scratch += [V((sum(rows_of), D), bf16), V((16, 128), f32)]
        scratch += [S((nb,)), S((nb, 2, 4)), S((nb, 4))]
        scratch += [S((nb, 2, 4))] * 2 + [S((nb, 2))] * 2 + [S((nb, 4))] * 2
        scratch += [S((2, 4)), S((4,)), S((1,))]
    params = dict(collective_id=cid, has_side_effects=True) if linked else {}
    return pl.pallas_call(
        functools.partial(layer_kernel, linked),
        out_shape=[shape(mixed_shape, bf16), shape((LEN, D), bf16)]
        + [shape((4, 8, r, D), bf16) for r in rows_of],
        in_specs=[hb, hb, pl.BlockSpec(memory_space=pltpu.SMEM)] + ([vm] * 6 if linked else [hb] * 3),
        out_specs=[hb] * 5,
        scratch_shapes=scratch,
        compiler_params=pltpu.CompilerParams(vmem_limit_bytes=63 * 1024 * 1024, **params),
        cost_estimate=pl.CostEstimate(
            flops=57_000_000_000, bytes_accessed=32_000_000, transcendentals=6_000_000
        ),
    )(tokens, cotangent, counts, *weights)


def scatter_kernel(rows_of, *refs):
    nb = len(rows_of)
    grads, (ig, ig_all, total) = refs[:nb], refs[nb : nb + 3]
    refs = refs[nb + 3 :]
    own, got1, got2, got3, gotz = (refs[i * nb : (i + 1) * nb] for i in range(5))
    ls, cs, cr, hs, hr, ss, sr, zs, zr = refs[5 * nb : 5 * nb + 9]
    z, me = lax.axis_index("tensor"), lax.axis_index("dp")
    nz = 4
    cp, xp, yp = flip(me, 1), flip(me, 2), flip(me, 4)
    groups = (me, xp, yp, flip(xp, 4))
    pair = (xp, yp)
    greet(z, nz, me, (cp, xp, yp), lambda: None)
    starts = [sum(rows_of[:b]) for b in range(nb)]
    half = [((0, 48), (48, r - 48)) for r in rows_of]

    open_line, hop, close_line = line_steps(ig, ig_all, z, me, refs[5 * nb + 9 :])

    def twin(b, j):
        return send(grads[b].at[:, flip(groups[j], 1)], got1[b].at[j], cs.at[b, j], cr.at[b, j], (cp, z))
    def load(b, j):
        return pltpu.make_async_copy(grads[b].at[:, groups[j]], own[b].at[j], ls.at[b, j])
    def corner(b, k):
        lo, n = half[b][k]
        return send(own[b].at[3, :, pl.ds(lo, n)], got2[b].at[:, pl.ds(lo, n)], hs.at[b, k], hr.at[b, k], (pair[k], z))
    def square(b, k):
        return send(own[b].at[1 + k], got3[b].at[k], ss.at[b, k], sr.at[b, k], (pair[k], z))
    def line(b, t, step):
        return send(own[b].at[0, t], gotz[b].at[(1 - step) // 2, t], zs.at[b, t], zr.at[b, (1 - step) // 2, t], (me, z + step))

    def add(dst, *srcs):
        dst[...] = sum((s[...].astype(f32) for s in srcs), dst[...].astype(f32)).astype(bf16)
    def over_z(body):
        lax.fori_loop(0, 4, lambda s, c: (body(s), c)[1], 0)

    def first(b):
        for j in (3, 1, 2, 0):
            twin(b, j).start()
            load(b, j).start()
    def merge(b, j):
        load(b, j).wait()
        arrived(got1[b].at[j], cr.at[b, j])
        over_z(lambda s: add(own[b].at[j, s], got1[b].at[j, s]))
    def second(b):
        merge(b, 3)
        for k in range(2):
            corner(b, k).start()
    def third(b):
        for k in range(2):
            lo, n = half[b][k]
            part = pl.ds(lo, n)
            arrived(got2[b].at[:, part], hr.at[b, k])
            over_z(lambda s: add(own[b].at[2 - k, s, part], got2[b].at[s, part]))
        for k in range(2):
            square(b, k).start()
    def fourth(b):
        for k in range(2):
            arrived(got3[b].at[k], sr.at[b, k])
        over_z(lambda s: add(own[b].at[0, s], got3[b].at[0, s], got3[b].at[1, s]))
        for t in (3, 2, 1):
            @pl.when(z + t < nz)
            def _():
                @pl.when(z > 0)
                def _():
                    arrived(gotz[b].at[0, z + t], zr.at[b, 0, z + t])
                    add(own[b].at[0, z + t], gotz[b].at[0, z + t])
                line(b, z + t, 1).start()
            @pl.when(z >= t)
            def _():
                @pl.when(z < nz - 1)
                def _():
                    arrived(gotz[b].at[1, z - t], zr.at[b, 1, z - t])
                    add(own[b].at[0, z - t], gotz[b].at[1, z - t])
                line(b, z - t, -1).start()
    def last(b):
        span = pl.ds(starts[b], rows_of[b])
        total[span] = own[b][0, z].astype(f32)
        for i, ok in ((0, z > 0), (1, z < nz - 1)):
            @pl.when(ok)
            def _():
                arrived(gotz[b].at[i, z], zr.at[b, i, z])
                total[span] += gotz[b][i, z].astype(f32)
    def close(b):
        for j in range(4):
            twin(b, j).wait_send()
        for k in range(2):
            corner(b, k).wait_send()
            square(b, k).wait_send()
        for t in (3, 2, 1):
            @pl.when(z + t < nz)
            def _():
                line(b, z + t, 1).wait_send()
            @pl.when(z >= t)
            def _():
                line(b, z - t, -1).wait_send()
    def rest(b):
        for j in (1, 2, 0):
            merge(b, j)

    for b in (2, 1, 0):
        first(b)
    open_line()
    second(2)
    rest(2)
    second(1)
    rest(1)
    third(2)
    second(0)
    rest(0)
    third(1)
    hop(1)
    fourth(2)
    third(0)
    fourth(1)
    hop(2)
    last(2)
    fourth(0)
    last(1)
    hop(3)
    last(0)
    close_line()
    for b in range(3):
        close(b)


def scatter(grads, ig, cid=2):
    rows_of = [g.shape[2] for g in grads]
    nb = len(rows_of)
    S, V = pltpu.SemaphoreType.DMA, pltpu.VMEM
    hb = pl.BlockSpec(memory_space=pl.ANY)
    scratch = [V((4, 4, r, D), bf16) for r in rows_of] + [V((4, 4, r, D), bf16) for r in rows_of]
    scratch += [V((4, r, D), bf16) for r in rows_of] + [V((2, 4, r, D), bf16) for r in rows_of] * 2
    scratch += [S((nb, 4))] * 3 + [S((nb, 2))] * 4 + [S((nb, 4)), S((nb, 2, 4)), S((2, 4)), S((4,)), S((1,))]
    return pl.pallas_call(
        functools.partial(scatter_kernel, rows_of),
        out_shape=[jax.ShapeDtypeStruct((4, LEN, D), bf16)] + [jax.ShapeDtypeStruct((sum(rows_of), D), f32)],
        in_specs=[hb] * (nb + 1),
        out_specs=[hb, pl.BlockSpec(memory_space=V)],
        scratch_shapes=scratch,
        compiler_params=pltpu.CompilerParams(collective_id=cid, has_side_effects=True, vmem_limit_bytes=60 * 1024 * 1024),
    )(*grads, ig)


def step_kernel(total, *refs):
    ins, outs = refs[:18], refs[18:]
    z, me = lax.axis_index("tensor"), lax.axis_index("dp")
    band, thin = ins[12].shape[1], ins[15].shape[1]
    vec = total[band : band + 16]
    row = lax.broadcasted_iota(jnp.int32, (D, 128), 0)
    col = lax.broadcasted_iota(jnp.int32, (D, 128), 1)

    def pick(source):
        chosen = jnp.where(row == source, 1.0, 0.0)
        return lax.dot_general(
            vec, chosen, NN, precision=lax.Precision.HIGHEST, preferred_element_type=f32
        )

    place = me * thin + col
    shared = pick(me * band + col)[:6, :band]
    head = jnp.where(place < 128, place, place + 256)
    late = jnp.where(place < 128, place + 256, place + 320)
    spots = [head, late] + [f * (D // 4) + place for f in range(4)]
    at = lax.broadcasted_iota(jnp.int32, (16, 128), 0)
    lines = []
    for i, spot in enumerate(spots):
        mine = jnp.where(at == z + (6 if i < 2 else 10), pick(spot), 0.0)
        lines.append(jnp.sum(mine, axis=0, keepdims=True)[:, :thin])
    split = jnp.concatenate(lines, axis=0)

    def apply(kind, where, gradient):
        rates, decays = kind_rates(), (MATRIX_DECAY,) * 4 + (0.0, 0.0)
        m, f, s = (ins[3 * kind + i][where] for i in range(3))
        results = adamw(m, f, s, gradient, rates[kind], decays[kind])
        for i in range(4):
            outs[4 * kind + i][where] = results[i]

    attn = total[:band]
    def pair(a, b):
        return jnp.concatenate([attn[:, a : a + 128], attn[:, b : b + 64]], axis=1)
    apply(0, (slice(None), 0), pair(0, 384))
    apply(0, (slice(None), 1), pair(128, 512))
    apply(0, (slice(None), 2), pair(256, 448))
    apply(1, (slice(None),), pair(640, 576).T)
    up = total[band + 16 : 2 * band + 16]
    down = total[2 * band + 16 :]
    down = down.T
    width = D // 4
    for f in range(4):
        apply(2, (slice(None), f), up[:, f * width : (f + 1) * width])
        apply(3, (f,), down[f * width : (f + 1) * width])
    apply(4, (slice(None),), shared)
    apply(5, (slice(None),), split)


def step(total, state):
    vm = pl.BlockSpec(memory_space=pltpu.VMEM)
    shapes = []
    for kind in range(6):
        shape = state[3 * kind].shape
        shapes += [jax.ShapeDtypeStruct(shape, t) for t in (f32, bf16, f32, f32)]
    return pl.pallas_call(
        step_kernel,
        out_shape=shapes,
        in_specs=[vm] * 19,
        out_specs=[vm] * 24,
        compiler_params=pltpu.CompilerParams(vmem_limit_bytes=56 * 1024 * 1024),
    )(total, *state)


def pack_attention(qkv, out):
    q, k, v = qkv[:, 0], qkv[:, 1], qkv[:, 2]
    return jnp.concatenate(
        [
            q[:, :128], k[:, :128], v[:, :128],
            q[:, 128:], v[:, 128:], k[:, 128:], out[:, 128:], out[:, :128],
        ],
        axis=1,
    )


def unpack_attention(block):
    pair = [block[:, 128 * i : 128 * i + 128] for i in range(6)]
    q = jnp.concatenate([pair[0], pair[3][:, :64]], axis=1)
    k = jnp.concatenate([pair[1], pair[4][:, :64]], axis=1)
    v = jnp.concatenate([pair[2], pair[3][:, 64:]], axis=1)
    o = jnp.concatenate([pair[5], pair[4][:, 64:]], axis=1)
    return jnp.stack([q, k, v], axis=1), o


def gather_plain(masters):
    qkv, out, up, down, shared, split = (t.astype(bf16) for t in masters)
    band, thin, width = shared.shape[1], split.shape[1], down.shape[1] * lax.axis_size("tensor")
    groups = lax.axis_size("tensor")
    own = jnp.stack(
        [pack_attention(qkv, out.T), up.reshape(band, -1), down.reshape(-1, band).T]
    )
    mats = lax.all_gather(own, AXES, axis=1, tiled=True).reshape(3, groups, 8, BAND, width)
    shared = lax.all_gather(shared, "dp", axis=1, tiled=True)
    split = lax.all_gather(split, AXES, axis=1, tiled=True).reshape(-1, groups, width // groups)
    bq, bv = split[0], split[1]
    zero = jnp.zeros((groups, 128), bf16)
    attn_bias = [bq[:, :128], zero, bv[:, :128], bq[:, 128:], bv[:, 128:], zero, zero]
    lines = [
        jnp.broadcast_to(shared, (groups, 6, width)),
        jnp.concatenate(attn_bias, axis=1)[:, None],
        jnp.swapaxes(split[2:], 0, 1).reshape(groups, 1, width),
    ]
    lines = jnp.pad(jnp.concatenate(lines, axis=1)[:, None], ((0, 0), (0, 7), (0, 8), (0, 0)))
    return jnp.concatenate([mats[0], lines], axis=2), mats[1], mats[2]


def step_plain(grads, mixed, grad_inputs, state):
    masters, firsts, seconds = state[0::3], state[1::3], state[2::3]
    band, thin = masters[4].shape[1], masters[5].shape[1]
    groups, copies = lax.axis_size("tensor"), lax.axis_size("dp")
    z, at = lax.axis_index("tensor"), lax.axis_index("dp")
    width = grads[0].shape[-1]
    summed = [
        lax.psum_scatter(
            g[:, :, :BAND].reshape(groups * copies, band, width), AXES, scatter_dimension=0
        ).astype(f32)
        for g in grads
    ]
    vec = lax.psum(grads[0][0, 0, BAND:].astype(f32), AXES)
    shared = lax.dynamic_slice_in_dim(vec[:6], at * band, band, 1)
    cols = lax.dynamic_slice_in_dim(vec[6:10], z, 1, 0)[0]
    ups = lax.dynamic_slice_in_dim(vec[10:14], z, 1, 0).reshape(-1, width // groups)
    split = jnp.stack(
        [
            jnp.concatenate([cols[:128], cols[384:448]]),
            jnp.concatenate([cols[256:384], cols[448:512]]),
        ]
    )
    split = lax.dynamic_slice_in_dim(jnp.concatenate([split, ups]), at * thin, thin, 1)
    sum_qkv, sum_out = unpack_attention(summed[0])
    gradients = (
        sum_qkv,
        sum_out.T,
        summed[1].reshape(masters[2].shape),
        summed[2].T.reshape(masters[3].shape),
        shared,
        split,
    )
    decays = (MATRIX_DECAY, MATRIX_DECAY, MATRIX_DECAY, MATRIX_DECAY, 0.0, 0.0)
    rates = kind_rates()
    outputs = []
    for kind in range(6):
        outputs.extend(
            adamw(masters[kind], firsts[kind], seconds[kind], gradients[kind], rates[kind], decays[kind])
        )
    mixed, grad_inputs = (lax.all_gather(t, "tensor") for t in (mixed, grad_inputs))
    return mixed, grad_inputs, outputs


def local(tokens, cotangent, counts, *state):
    masters = state[0::3]
    if (lax.axis_size("tensor"), lax.axis_size("dp")) == (4, 8):
        mixed, grad_inputs, *grads = layer(True, tokens, cotangent, counts, masters)
        grad_inputs, total = scatter(grads, grad_inputs)
        outputs = step(total, state)
    else:
        mats = gather_plain(masters)
        mixed, grad_inputs, *grads = layer(False, tokens, cotangent, counts, mats)
        mixed, grad_inputs, outputs = step_plain(grads, mixed, grad_inputs, state)
    return (mixed, grad_inputs.astype(f32), *outputs)


def solution(mesh):
    rows = P("dp", None, None)
    state = (
        P("dp", None, "tensor"),
        P("tensor", "dp"),
        P("dp", None, "tensor"),
        P(None, "tensor", "dp"),
        P(None, "dp"),
        P(None, ("tensor", "dp")),
    )
    in_specs = (rows, rows, P("dp")) + tuple(s for s in state for _ in range(3))
    out_specs = (rows, rows) + tuple(s for s in state for _ in range(4))
    return jax.shard_map(local, mesh=mesh, in_specs=in_specs, out_specs=out_specs, check_vma=False)
```

```python
import functools

import jax
import jax.numpy as jnp
from jax import lax
from jax.experimental import pallas as pl
from jax.experimental.pallas import tpu as pltpu
from jax.sharding import PartitionSpec as P

D = 768
FF = 3072
HEAD_DIM = 64
LEN = 576
STEP = 10


LN_EPS = 1e-05
MASK_FILL = -1e30
BETA_ONE = 0.5
BETA_TWO = 0.5
ADAM_EPS = 1e-08
MATRIX_DECAY = 0.01
SQRT_HALF = 0.7071067811865476
INV_ROOT_TAU = 0.3989422804014327
AXES = ("tensor", "dp")
MESH = pl.DeviceIdType.MESH
bf16, f32 = jnp.bfloat16, jnp.float32
NN = (((1,), (0,)), ((), ()))
NT = (((1,), (1,)), ((), ()))
RT = 192
RL = 96
BAND = 96


def kind_rates():
    return (
        0.7 * D ** (-0.5),
        0.7 * (D * 16 // LEN) ** (-0.5),
        0.7 * D ** (-0.5),
        0.7 * FF ** (-0.5),
        0.6,
        0.4,
    )


def adamw(master, first, second, gradient, step_rate, decay_rate):
    first_new = BETA_ONE * first + (1.0 - BETA_ONE) * gradient
    second_new = BETA_TWO * second + (1.0 - BETA_TWO) * gradient * gradient
    first_hat = first_new / (1.0 - BETA_ONE**STEP)
    second_hat = second_new / (1.0 - BETA_TWO**STEP)
    master_new = master - step_rate * (
        first_hat / (jnp.sqrt(second_hat) + ADAM_EPS) + decay_rate * master
    )
    return (master_new, master_new.astype(jnp.bfloat16), first_new, second_new)


def flip(index, bit):
    return index + bit - 2 * bit * lax.rem(lax.div(index, bit), 2)

def send(src, dst, ssem, rsem, to):
    return pltpu.make_async_remote_copy(
        src_ref=src, dst_ref=dst, send_sem=ssem, recv_sem=rsem, device_id=to, device_id_type=MESH
    )

def arrived(dst, sem):
    pltpu.make_async_copy(dst, dst, sem).wait()

def greet(z, nz, me, others, meanwhile):
    bar = pltpu.get_barrier_semaphore()
    for d in others:
        pl.semaphore_signal(bar, inc=1, device_id=(d, z), device_id_type=MESH)
    @pl.when(z > 0)
    def _():
        pl.semaphore_signal(bar, inc=1, device_id=(me, z - 1), device_id_type=MESH)
    @pl.when(z < nz - 1)
    def _():
        pl.semaphore_signal(bar, inc=1, device_id=(me, z + 1), device_id_type=MESH)
    meanwhile()
    edges = jnp.where(z > 0, 1, 0) + jnp.where(z < nz - 1, 1, 0)
    pl.semaphore_wait(bar, len(others) + edges)


def mm(a, b, dims=NN):
    return lax.dot_general(a, b, dims, preferred_element_type=f32)

def normal_of(rows):
    mean = jnp.mean(rows, axis=-1, keepdims=True)
    centred = rows - mean
    inverse = lax.rsqrt(jnp.mean(centred * centred, axis=-1, keepdims=True) + LN_EPS)
    return centred * inverse, inverse

def normal_back(grad, normal, inverse, gain):
    scaled = grad * gain
    return inverse * (
        scaled
        - jnp.mean(scaled, axis=-1, keepdims=True)
        - normal * jnp.mean(scaled * normal, axis=-1, keepdims=True)
    )

def row_tiles(size):
    return range(0, LEN, size)

def colsum(v):
    return jnp.sum(v, axis=0, keepdims=True)

def pack(own, pad, qkv, out, up, down, shared, split):
    band, thin = shared.shape[1], split.shape[1]
    me = lax.axis_index("dp")
    low = [qkv[:, i].astype(bf16) for i in range(3)]
    ot = out[...].T.astype(bf16)
    pieces = [
        low[0][:, :128], low[1][:, :128], low[2][:, :128],
        jnp.concatenate([low[0][:, 128:], low[2][:, 128:]], axis=1),
        jnp.concatenate([low[1][:, 128:], ot[:, 128:]], axis=1),
        ot[:, :128],
    ]
    for i, piece in enumerate(pieces):
        own[0:band, 128 * i : 128 * i + 128] = piece
    width = D // 4
    for f in range(4):
        own[band + 16 : 2 * band + 16, f * width : (f + 1) * width] = up[:, f].astype(bf16)
        own[2 * band + 16 : 3 * band + 16, f * width : (f + 1) * width] = down[f].T.astype(bf16)
    pad[...] = jnp.zeros_like(pad)
    pad[0:6, 0:band] = shared[...]
    pad[8:14, 0:thin] = split[...]
    vals = pad[...].astype(bf16)
    src = lax.broadcasted_iota(jnp.int32, (128, D), 0)
    col = lax.broadcasted_iota(jnp.int32, (128, D), 1)

    def placed(spot):
        return mm(vals, jnp.where(col == spot, 1.0, 0.0).astype(bf16))

    at = me * thin + src
    attn = placed(jnp.where(at < 128, at, at + 256))[8:9]
    attn += placed(jnp.where(at < 128, at + 256, at + 320))[9:10]
    ups = sum(placed(f * width + at)[10 + f : 11 + f] for f in range(4))
    rows = [placed(me * band + src)[0:6], attn, ups, jnp.zeros((8, D), f32)]
    own[band : band + 16] = jnp.concatenate(rows, axis=0).astype(bf16)


def gather_steps(own, outs, masters_rows, z, me, sems):
    rows_of = masters_rows
    nb, nz = len(rows_of), 4
    lsem, zs, zr, ps, pr, ds, dr, cs, cr = sems
    cp, xp, yp = flip(me, 1), flip(me, 2), flip(me, 4)
    dg = flip(xp, 4)
    pair = (xp, yp)
    starts = [sum(rows_of[:b]) for b in range(nb)]
    half = [[(0, 48), (48, r - 48)] for r in rows_of]

    def own_ref(b):
        return own.at[pl.ds(starts[b], rows_of[b])]
    def right(b, s, src):
        return send(src, outs[b].at[s, me], zs.at[b, 0, z - s], zr.at[b, s], (me, z + 1))
    def left(b, s, src):
        return send(src, outs[b].at[s, me], zs.at[b, 1, s - z], zr.at[b, s], (me, z - 1))
    def side(b, s, src, k):
        return send(src, outs[b].at[s, me], ps.at[b, k, s], pr.at[b, k, s], (pair[k], z))
    def spread(b, s, src):
        for k in range(2):
            side(b, s, src, k).start()
    def diag(b, k):
        lo, n = half[b][k]
        part = outs[b].at[:, pair[k], pl.ds(lo, n)]
        return send(part, part, ds.at[b, k], dr.at[b, k], (pair[1 - k], z))
    def twin(b, j):
        part = outs[b].at[:, (me, xp, yp, dg)[j]]
        return send(part, part, cs.at[b, j], cr.at[b, j], (cp, z))
    def keep(b):
        return pltpu.make_async_copy(own_ref(b), outs[b].at[z, me], lsem.at[b])

    def opens(b):
        @pl.when(z < nz - 1)
        def _():
            right(b, z, own_ref(b)).start()
        @pl.when(z > 0)
        def _():
            left(b, z, own_ref(b)).start()
        spread(b, z, own_ref(b))
        keep(b).start()
    def hop(b, t):
        @pl.when(z >= t)
        def _():
            s = z - t
            arrived(outs[b].at[s, me], zr.at[b, s])
            @pl.when(z < nz - 1)
            def _():
                right(b, s, outs[b].at[s, me]).start()
            spread(b, s, outs[b].at[s, me])
        @pl.when(z + t < nz)
        def _():
            s = z + t
            arrived(outs[b].at[s, me], zr.at[b, s])
            @pl.when(z > 0)
            def _():
                left(b, s, outs[b].at[s, me]).start()
            spread(b, s, outs[b].at[s, me])
    def lined(b):
        keep(b).wait()
        twin(b, 0).start()
    def square(b):
        for k in range(2):
            for s in range(4):
                arrived(outs[b].at[s, pair[k]], pr.at[b, k, s])
            diag(b, k).start()
            twin(b, 1 + k).start()
    def corner(b):
        for k in range(2):
            lo, n = half[b][k]
            arrived(outs[b].at[:, dg, pl.ds(lo, n)], dr.at[b, k])
        twin(b, 3).start()
    def ready(b):
        for j, d in enumerate((cp, flip(xp, 1), flip(yp, 1), flip(dg, 1))):
            arrived(outs[b].at[:, d], cr.at[b, j])
    def sent(b):
        for t in range(4):
            @pl.when((z < nz - 1) & (z >= t))
            def _():
                right(b, z - t, outs[b].at[z - t, me]).wait_send()
            @pl.when((z > 0) & (z + t < nz))
            def _():
                left(b, z + t, outs[b].at[z + t, me]).wait_send()
            for k in range(2):
                side(b, t, outs[b].at[t, me], k).wait_send()
            twin(b, t).wait_send()
        for k in range(2):
            diag(b, k).wait_send()
    return opens, hop, lined, square, corner, ready, sent


def line_steps(block, whole, z, me, sems):
    nz = 4
    ms, mr, ml = sems

    def along(s, src, way):
        return send(src, whole.at[s], ms.at[(way + 1) // 2, jnp.abs(s - z)], mr.at[s], (me, z + way))
    def keep():
        return pltpu.make_async_copy(block, whole.at[z], ml.at[0])
    def opens():
        @pl.when(z < nz - 1)
        def _():
            along(z, block, 1).start()
        @pl.when(z > 0)
        def _():
            along(z, block, -1).start()
        keep().start()
    def hop(t):
        for way, ok in ((-1, z >= t), (1, z + t < nz)):
            @pl.when(ok)
            def _():
                s = z + way * t
                arrived(whole.at[s], mr.at[s])
                @pl.when((z < nz - 1) if way < 0 else (z > 0))
                def _():
                    along(s, whole.at[s], -way).start()
    def close():
        keep().wait()
        for t in range(4):
            @pl.when((z < nz - 1) & (z >= t))
            def _():
                along(z - t, whole.at[z - t], 1).wait_send()
            @pl.when((z > 0) & (z + t < nz))
            def _():
                along(z + t, whole.at[z + t], -1).wait_send()
    return opens, hop, close


def reduce_steps(own, got_b, landing, rows_of, z, me, sems):
    cs, cr, hs, hr, ss, sr, zs, zr, ds, dr = sems
    nz = 4
    xp, yp = flip(me, 2), flip(me, 4)
    pair = (xp, yp)
    cp = flip(me, 1)
    half = [((0, 48), (48, r - 48)) for r in rows_of]
    everything = slice(None)

    def add(dst, *srcs):
        dst[...] = sum((t[...].astype(f32) for t in srcs), dst[...].astype(f32)).astype(bf16)
    def over_z(body):
        lax.fori_loop(0, nz, lambda g, c: (body(g), c)[1], 0)
    def twin(b, g, src, j):
        return send(src, came(b, j, g), cs.at[b, j, g], cr.at[b, j, g], (cp, z))
    def came(b, j, g):
        return got_b[b - 1].at[j, g] if b else landing(0, 5 + j, g, pl.ds(0, 96))
    def twin_vec(g, j, src):
        return send(src, landing(0, 5 + j, g, pl.ds(96, 16)), ds.at[j, g], dr.at[j, g], (cp, z))
    def merge(b):
        def body(g):
            for j in (3, 1, 2, 0):
                arrived(came(b, j, g), cr.at[b, j, g])
                if b:
                    add(own[b].at[j, g], came(b, j, g))
                else:
                    arrived(landing(0, 5 + j, g, pl.ds(96, 16)), dr.at[j, g])
                    add(own[0].at[j, g], landing(0, 5 + j, g, pl.ds(0, 112)))
        over_z(body)
        for k in range(2):
            corner(b, k).start()
    def corner(b, k):
        part = pl.ds(*half[b][k])
        return send(own[b].at[3, :, part], landing(b, 0, everything, part), hs.at[b, k], hr.at[b, k], (pair[k], z))
    def square(b, k):
        return send(own[b].at[1 + k], landing(b, 1 + k), ss.at[b, k], sr.at[b, k], (pair[k], z))
    def third(b):
        for k in range(2):
            part = pl.ds(*half[b][k])
            arrived(landing(b, 0, everything, part), hr.at[b, k])
            over_z(lambda g: add(own[b].at[2 - k, g, part], landing(b, 0, g, part)))
            square(b, 1 - k).start()
    def fourth(b):
        for k in range(2):
            arrived(landing(b, 1 + k), sr.at[b, k])
        over_z(lambda g: add(own[b].at[0, g], landing(b, 1, g), landing(b, 2, g)))
        along(b, 0)
    def line(b, t, way):
        side = (1 - way) // 2
        return send(own[b].at[0, t], landing(b, 3 + side, t), zs.at[b, t], zr.at[b, side, t], (me, z + way))
    def along(b, i):
        for way, begin in ((1, i), (-1, nz - 1 - i)):
            side = (1 - way) // 2
            targets = range(nz - 1, begin, -1) if way > 0 else range(begin)
            @pl.when(z == begin)
            def _():
                for t in targets:
                    if i:
                        arrived(landing(b, 3 + side, t), zr.at[b, side, t])
                        add(own[b].at[0, t], landing(b, 3 + side, t))
                    line(b, t, way).start()
    def last(b, total, at):
        total[pl.ds(at, rows_of[b])] = own[b][0, z].astype(f32)
        for side, ok in ((0, z > 0), (1, z < nz - 1)):
            @pl.when(ok)
            def _():
                arrived(landing(b, 3 + side, z), zr.at[b, side, z])
                total[pl.ds(at, rows_of[b])] += landing(b, 3 + side, z)[...].astype(f32)
    def closed(b):
        for k in range(2):
            corner(b, k).wait_send()
            square(b, k).wait_send()
        for t in range(nz):
            @pl.when(z < t)
            def _():
                line(b, t, 1).wait_send()
            @pl.when(z > t)
            def _():
                line(b, t, -1).wait_send()
    return twin, twin_vec, merge, third, fourth, along, last, closed


QT = ((0, 256), (256, 256), (512, 64))


def layer_kernel(linked, *refs):
    tokens, cotangent, counts = refs[:3]
    weights_in = refs[3 : 9 if linked else 6]
    refs = refs[9 if linked else 6 :]
    n_out = 3 if linked else 5
    outs, refs = refs[:n_out], refs[n_out:]
    (WA, WB, WC, x, gout_low, first_in, second_in, left_t, right_t, qkv, probs, att,
     middle, acc, hs, stage, bsum, vrow, vecs, bias, mixed, sems) = refs[:22]
    refs = refs[22:]
    gm_low, ig = second_in, first_in
    hidden, slope = hs.at[pl.ds(0, 4)], hs.at[pl.ds(4, 4)]
    z, me = lax.axis_index("tensor"), lax.axis_index("dp")
    band = BAND
    if linked:
        mixed_all, ig_all, total_out = outs
        own, pad = stage, refs[0]
        rows_of = (band + 16, band, band)
        opens, hop, lined, square, corner, ready, sent = gather_steps(
            own, (WA, WB, WC), rows_of, z, me, refs[1:10]
        )
        mopen, mhop, mclose = line_steps(mixed, mixed_all, z, me, refs[10:13])
        iopen, ihop, iclose = line_steps(ig, ig_all, z, me, refs[13:16])
        parts, got_b, freed = refs[16:19], refs[19:21], refs[21]
        def landing(b, i, g=slice(None), part=None):
            if b:
                part = pl.ds(0, band) if part is None else part
                return (WB, WC)[b - 1].at[g, i, part]
            base, spot = (0, 4) if i == 0 else (4, i - 1) if i < 5 else (0, i - 5)
            lo, n = (0, band + 16) if part is None else (part.start, part.size)
            g = pl.ds(base, 4) if isinstance(g, slice) else base + g
            return hs.at[g, pl.ds((band + 16) * spot + lo, n)]
        twin, twin_vec, merge, third, fourth, along, last, closed = reduce_steps(
            parts, got_b, landing, rows_of, z, me, refs[22:32]
        )
        def staged(slot, j):
            return stage.at[pl.ds((4 * slot + j) * band, band)]
        def release():
            for d in (flip(me, 1), flip(me, 2), flip(me, 4)):
                pl.semaphore_signal(freed, inc=1, device_id=(d, z), device_id_type=MESH)
            @pl.when(z > 0)
            def _():
                pl.semaphore_signal(freed, inc=1, device_id=(me, z - 1), device_id_type=MESH)
            @pl.when(z < 3)
            def _():
                pl.semaphore_signal(freed, inc=1, device_id=(me, z + 1), device_id_type=MESH)
        def acquire():
            pl.semaphore_wait(freed, 3 + jnp.where(z > 0, 1, 0) + jnp.where(z < 3, 1, 0))
    else:
        def nothing(*args):
            return None
        opens = hop = lined = square = corner = sent = mhop = nothing
        release = acquire = merge = third = fourth = along = nothing
        mixed_all, ig_out, gA, gB, gC = outs
        def ready(b):
            pltpu.make_async_copy(weights_in[b], (WA, WB, WC)[b], sems.at[8 + b]).wait()
        def mopen():
            pltpu.make_async_copy(mixed, mixed_all, sems.at[11]).start()
        def mclose():
            pltpu.make_async_copy(mixed, mixed_all, sems.at[11]).wait()

    loads = [
        pltpu.make_async_copy(tokens.at[z], x, sems.at[6]),
        pltpu.make_async_copy(cotangent.at[z], gout_low, sems.at[7]),
    ]
    for load in loads:
        load.start()
    if linked:
        greet(z, 4, me, (flip(me, 1), flip(me, 2), flip(me, 4)), lambda: pack(own, pad, *weights_in))
    else:
        for b in range(3):
            pltpu.make_async_copy(weights_in[b], (WA, WB, WC)[b], sems.at[8 + b]).start()
    count = counts[z]
    column = lax.broadcasted_iota(jnp.int32, (LEN, 1), 0)
    keybias = jnp.where(column < count, 0.0, MASK_FILL)
    def valid(r):
        return jnp.where(lax.broadcasted_iota(jnp.int32, (RL, 1), 0) + r < count, 1.0, 0.0)

    def transpose(dst, src):
        turned = src[...].T
        for d in range(8):
            spot = d
            if linked:
                apart = [lax.rem(lax.div(me, 1 << i) + (d >> i), 2) for i in range(3)]
                spot = 4 * apart[0] + apart[1] + 2 * apart[2]
            dst[pl.ds(pl.multiple_of(spot * band, 32), band)] = turned[d * band : (d + 1) * band]

    opens(0)
    for load in loads:
        load.wait()
    for r in row_tiles(RL):
        rs = pl.ds(r, RL)
        gout_low[rs] = (gout_low[rs].astype(f32) * valid(r)).astype(bf16)
        middle[rs] = normal_of(x[rs].astype(f32))[0]
    hop(0, 1)
    hop(0, 2)
    opens(1)
    transpose(right_t, gout_low)
    hop(0, 3)
    lined(0)
    hop(1, 1)
    opens(2)
    square(0)
    hop(1, 2)
    hop(2, 1)
    hop(1, 3)
    lined(1)
    hop(2, 2)
    corner(0)
    hop(2, 3)
    lined(2)
    ready(0)
    lines = [sum(WA[g, i, band : band + 16].astype(f32) for i in range(8)) for g in range(4)]
    vecs[...] = lines[0]
    for g in range(4):
        bias[0, g] = lines[g][6:7]
        bias[1, g] = lines[g][7:8]
    for r in row_tiles(RL):
        rs = pl.ds(r, RL)
        first_in[rs] = (middle[rs] * vecs[0:1] + vecs[1:2]).astype(bf16)
    lane = lax.broadcasted_iota(jnp.int32, (1, 128), 1)
    low = lane < 64
    acc[...] = jnp.zeros_like(acc)

    def at(g, table):
        for i, steps in enumerate(table):
            if steps:
                @pl.when(g == i)
                def _():
                    for step, *args in steps:
                        step(*args)
    def wa(g, lo=0, hi=D):
        return WA[g, :, 0:band, lo:hi].reshape(D, hi - lo)
    def wb(g):
        return WB[g].reshape(D, D)
    def wc(g):
        return WC[g].reshape(D, D)

    def forward(g, carry):
        for r in row_tiles(RT):
            rs = pl.ds(r, RT)
            qkv[g, rs] = (mm(first_in[rs], wa(g)) + bias[0, g]).astype(bf16)
        def tile(i):
            return qkv[g, :, 128 * i : 128 * i + 128]
        outs = []
        for h in range(3):
            q, k, v = (tile(0), tile(1), tile(2)) if h < 2 else (tile(3), tile(4), tile(3))
            q = jnp.where(low if h != 1 else ~low, q, 0) * bf16(0.125)
            vt = v.T
            vt = vt[64:] if h else vt[:64]
            cols = []
            for r, n in QT:
                s = mm(k, q[r : r + n], NT) + keybias
                e = jnp.exp(s - jnp.max(s, axis=0, keepdims=True))
                p = (e * (1.0 / jnp.sum(e, axis=0, keepdims=True))).astype(bf16)
                probs[g, h, :, pl.ds(r, n)] = p
                cols.append(mm(vt, p))
            outs.append(jnp.concatenate(cols, axis=1))
        att[g, :, 128:256] = jnp.concatenate(outs[:2], axis=0).T.astype(bf16)
        att[g, :, 0:128] = jnp.concatenate([jnp.zeros_like(outs[2]), outs[2]], axis=0).T.astype(bf16)
        for r in row_tiles(RT):
            rs = pl.ds(r, RT)
            acc[rs] += mm(att[g, rs], wa(g, 512, D), NT)
        at(g, [[(square, 1)], [], [(corner, 1)], [(square, 2)]])
        return carry
    lax.fori_loop(0, 4, forward, 0)

    for r in row_tiles(RL):
        rs = pl.ds(r, RL)
        m = x[rs].astype(f32) + acc[rs] + vecs[2:3]
        middle[rs] = m
        second_in[rs] = (normal_of(m)[0] * vecs[3:4] + vecs[4:5]).astype(bf16)
    transpose(left_t, second_in)
    acc[...] = jnp.zeros_like(acc)
    ready(1)

    def mlp_up(g, carry):
        for r in row_tiles(RT):
            rs = pl.ds(r, RT)
            u = mm(second_in[rs], wb(g)) + bias[1, g]
            phi = 0.5 * (1.0 + lax.erf(u * SQRT_HALF))
            hidden[g, rs] = (u * phi).astype(bf16)
            slope[g, rs] = (phi + u * jnp.exp(-0.5 * u * u) * INV_ROOT_TAU).astype(bf16)
        return carry
    lax.fori_loop(0, 4, mlp_up, 0)
    corner(2)
    ready(2)

    def mlp_down(g, carry):
        for r in row_tiles(RT):
            rs = pl.ds(r, RT)
            acc[rs] += mm(hidden[g, rs], wc(g), NT)
        return carry
    lax.fori_loop(0, 4, mlp_down, 0)
    for r in row_tiles(RL):
        rs = pl.ds(r, RL)
        mixed[rs] = ((middle[rs] + acc[rs] + vecs[5:6]) * valid(r)).astype(bf16)
    mopen()
    acc[...] = jnp.zeros_like(acc)

    def off(dst, g, slot):
        return pltpu.make_async_copy(stage.at[slot], dst.at[g, :, pl.ds(0, band)], sems.at[slot])
    def put(dst, g, slot, part):
        @pl.when(g > 0)
        def _():
            off(dst, g - 1, slot).wait()
        for c in range(0, D, 2 * band):
            stage[slot, pl.ds(c // band, 2)] = part(c).astype(bf16).reshape(2, band, D)
        off(dst, g, slot).start()
    def share_out(b, g, slot, part):
        def sending(gg):
            return [twin(b, gg, staged(slot, j), j) for j in range(4)]
        kept = part(0, 4 * band).astype(bf16)
        for j in range(4):
            parts[b][j, g, pl.ds(0, band)] = kept[j * band : (j + 1) * band]
        @pl.when(g > 0)
        def _():
            for copy in sending(g - 1):
                copy.wait_send()
        stage[pl.ds(4 * slot * band, 4 * band)] = part(4 * band, 4 * band).astype(bf16)
        for copy in sending(g):
            copy.start()
        @pl.when(g == 3)
        def _():
            for copy in sending(g):
                copy.wait_send()
    def give(b, g, slot, part):
        if linked:
            share_out(b, g, slot, part)
        else:
            put((gA, gB, gC)[b], g, slot, lambda c: part(c, 2 * band))

    def mlp_back(g, carry):
        for r in row_tiles(RT):
            rs = pl.ds(r, RT)
            gp = (mm(gout_low[rs], wc(g)) * slope[g, rs].astype(f32)).astype(bf16)
            slope[g, rs] = gp
            acc[rs] += mm(gp, wb(g), NT)
        bsum[1, g] = colsum(slope[g].astype(f32))
        give(2, g, 0, lambda c, n: mm(right_t[pl.ds(c, n)], hidden[g]))
        give(1, g, 1, lambda c, n: mm(left_t[pl.ds(c, n)], slope[g]))
        return carry
    for b in range(3):
        sent(b)
    lax.fori_loop(0, 4, mlp_back, 0)
    release()
    if not linked:
        off(gC, 3, 0).wait()
        off(gB, 3, 1).wait()

    sums = [jnp.zeros((1, D), f32) for _ in range(6)]
    for r in row_tiles(RL):
        rs = pl.ds(r, RL)
        n, inv = normal_of(middle[rs])
        gn = acc[rs]
        go = gout_low[rs].astype(f32)
        t = go + normal_back(gn, n, inv, vecs[3:4])
        middle[rs] = t
        gm_low[rs] = t.astype(bf16)
        sums[2] += colsum(t)
        sums[3] += colsum(gn * n)
        sums[4] += colsum(gn)
        sums[5] += colsum(go)
    merged = [(acquire,), (merge, 2), (merge, 1), (mhop, 1)]
    for act, *args in merged:
        act(*args)
    transpose(left_t, first_in)
    transpose(right_t, gm_low)
    acc[...] = jnp.zeros_like(acc)

    def backward(g, carry):
        ga = mm(gm_low[...], wa(g, 512, D)).astype(bf16)
        def tile(i):
            return qkv[g, :, 128 * i : 128 * i + 128]
        dq, dk, dv = [], [], []
        for h in range(3):
            q, k, v = (tile(0), tile(1), tile(2)) if h < 2 else (tile(3), tile(4), tile(3))
            gt = ga[:, 128:256] if h < 2 else ga[:, 0:128]
            gmask = jnp.where(low if h == 0 else ~low, gt, 0)
            kt = k.T
            kt = kt[64:] if h == 1 else kt[:64]
            dqs, dks, dvs = [], 0.0, 0.0
            for r, n in QT:
                p = probs[g, h, :, pl.ds(r, n)]
                dp = mm(v, gmask[r : r + n], NT)
                pf = p.astype(f32)
                inner = jnp.sum(pf * dp, axis=0, keepdims=True)
                ds = (pf * (dp - inner)).astype(bf16)
                dqs.append(mm(kt, ds))
                dks = dks + mm(ds, q[r : r + n])
                dvs = dvs + mm(p, gt[r : r + n])
            dq.append(jnp.concatenate(dqs, axis=1))
            dk.append(dks * 0.125)
            dv.append(dvs)
        dq01 = jnp.concatenate(dq[:2], axis=0).T * 0.125
        dq2 = jnp.concatenate([dq[2], jnp.zeros_like(dq[2])], axis=0).T * 0.125
        parts = [
            dq01,
            jnp.where(low, dk[0], dk[1]),
            jnp.where(low, dv[0], dv[1]),
            jnp.where(low, dq2, dv[2]),
            jnp.where(low, dk[2], 0.0),
        ]
        for i, part in enumerate(parts):
            part = part.astype(bf16)
            qkv[g, :, 128 * i : 128 * i + 128] = part
            bsum[0, g, :, 128 * i : 128 * i + 128] = colsum(part.astype(f32))
        qkv[g, :, 640:768] = jnp.zeros((LEN, 128), bf16)
        bsum[0, g, :, 640:768] = jnp.zeros((1, 128), f32)
        for r in row_tiles(RT):
            rs = pl.ds(r, RT)
            acc[rs] += mm(qkv[g, rs], wa(g), NT)
        at(g, [[(third, 2)], [(mhop, 2), (third, 1)], [], []])
        return carry
    lax.fori_loop(0, 4, backward, 0)

    for r in row_tiles(RL):
        rs = pl.ds(r, RL)
        n, inv = normal_of(x[rs].astype(f32))
        gn = acc[rs]
        first_in[rs] = (middle[rs] + normal_back(gn, n, inv, vecs[0:1])).astype(bf16)
        sums[0] += colsum(gn * n)
        sums[1] += colsum(gn)
    lines = sums + [bsum[i, j] for i in range(2) for j in range(4)] + [jnp.zeros((2, D), f32)]
    lines = jnp.concatenate(lines, axis=0).astype(bf16)
    fourth(2)
    if linked:
        iopen()

    def attention_grads(g, carry):
        def part(c, n):
            first = mm(left_t[pl.ds(c, n)], qkv[g])
            second = mm(right_t[pl.ds(c, n)], att[g])
            return jnp.concatenate([first[:, :512], first[:, 512:] + second], axis=1)
        give(0, g, 0, part)
        at(g, [[(mhop, 3)], [], [(along, 2, 1)], []])
        return carry
    lax.fori_loop(0, 4, attention_grads, 0)
    if linked:
        vrow[0] = lines
        def vec_step(g, act):
            for j in range(4):
                act(twin_vec(g, j, vrow.at[0]))
        for g in range(4):
            vec_step(g, lambda copy: copy.start())
            for j in range(4):
                parts[0][j, g, pl.ds(band, 16)] = lines
        fourth(1)
        merge(0)
        third(0)
        ihop(1)
        along(2, 2)
        along(1, 1)
        fourth(0)
        ihop(2)
        along(1, 2)
        last(2, acc, 2 * band + 16)
        along(0, 1)
        last(1, acc, band + 16)
        along(0, 2)
        last(0, acc, 0)
        done = pltpu.make_async_copy(acc.at[pl.ds(0, 3 * band + 16)], total_out, sems.at[1])
        done.start()
        ihop(3)
        for g in range(4):
            vec_step(g, lambda copy: copy.wait_send())
        done.wait()
        iclose()
        for b in range(3):
            closed(b)
    else:
        for i in range(8):
            vrow[i] = lines
        copies = [pltpu.make_async_copy(ig, ig_out, sems.at[1])]
        copies += [pltpu.make_async_copy(vrow, gA.at[g, :, pl.ds(band, 16)], sems.at[2 + g]) for g in range(4)]
        for copy in copies:
            copy.start()
        for copy in copies:
            copy.wait()
        off(gA, 3, 0).wait()
    mclose()


def layer(linked, tokens, cotangent, counts, weights, cid=1):
    V, S = pltpu.VMEM, pltpu.SemaphoreType.DMA
    shape = jax.ShapeDtypeStruct
    hb, vm = pl.BlockSpec(memory_space=pl.ANY), pl.BlockSpec(memory_space=V)
    band, nb = BAND, 3
    rows_of = (band + 16, band, band)
    scratch = [V((4, 8, r, D), bf16) for r in rows_of]
    scratch += [V((LEN, D), bf16)] * 4 + [V((D, LEN), bf16)] * 2
    scratch += [V((4, LEN, D), bf16), V((4, 3, LEN, LEN), bf16), V((4, LEN, 256), bf16)]
    scratch += [V((LEN, D), f32)] * 2 + [V((8, LEN, D), bf16), V((8 * band, D) if linked else (2, 8, band, D), bf16)]
    scratch += [V((2, 4, 1, D), f32), V((1 if linked else 8, 16, D), bf16), V((16, D), f32)]
    scratch += [V((2, 4, 1, D), f32), V((LEN, D), bf16), S((12,))]
    outs = [shape((LEN, D), bf16)] * 2 + [shape((4, 8, r, D), bf16) for r in rows_of]
    if linked:
        outs = [shape((4, LEN, D), bf16)] * 2 + [shape((sum(rows_of), D), f32)]
        scratch += [V((16, 128), f32)]
        scratch += [S((nb,)), S((nb, 2, 4)), S((nb, 4))]
        scratch += [S((nb, 2, 4))] * 2 + [S((nb, 2))] * 2 + [S((nb, 4))] * 2
        scratch += [S((2, 4)), S((4,)), S((1,))] * 2
        scratch += [V((4, 4, r, D), bf16) for r in rows_of] + [V((4, 4, band, D), bf16)] * 2
        scratch += [pltpu.SemaphoreType.REGULAR] + [S((nb, 4, 4))] * 2 + [S((nb, 2))] * 4
        scratch += [S((nb, 4)), S((nb, 2, 4))] + [S((4, 4))] * 2
    params = dict(collective_id=cid, has_side_effects=True) if linked else {}
    return pl.pallas_call(
        functools.partial(layer_kernel, linked),
        out_shape=outs,
        in_specs=[hb, hb, pl.BlockSpec(memory_space=pltpu.SMEM)] + ([vm] * 6 if linked else [hb] * 3),
        out_specs=[hb] * len(outs),
        scratch_shapes=scratch,
        compiler_params=pltpu.CompilerParams(vmem_limit_bytes=63 * 1024 * 1024, **params),
        cost_estimate=pl.CostEstimate(
            flops=57_000_000_000, bytes_accessed=32_000_000, transcendentals=6_000_000
        ),
    )(tokens, cotangent, counts, *weights)


def step_kernel(total, *refs):
    ins, outs = refs[:18], refs[18:]
    z, me = lax.axis_index("tensor"), lax.axis_index("dp")
    band, thin = ins[12].shape[1], ins[15].shape[1]
    vec = total[band : band + 16]
    row = lax.broadcasted_iota(jnp.int32, (D, 128), 0)
    col = lax.broadcasted_iota(jnp.int32, (D, 128), 1)

    def pick(source):
        chosen = jnp.where(row == source, 1.0, 0.0)
        return lax.dot_general(
            vec, chosen, NN, precision=lax.Precision.HIGHEST, preferred_element_type=f32
        )

    place = me * thin + col
    shared = pick(me * band + col)[:6, :band]
    head = jnp.where(place < 128, place, place + 256)
    late = jnp.where(place < 128, place + 256, place + 320)
    spots = [head, late] + [f * (D // 4) + place for f in range(4)]
    at = lax.broadcasted_iota(jnp.int32, (16, 128), 0)
    lines = []
    for i, spot in enumerate(spots):
        mine = jnp.where(at == z + (6 if i < 2 else 10), pick(spot), 0.0)
        lines.append(jnp.sum(mine, axis=0, keepdims=True)[:, :thin])
    split = jnp.concatenate(lines, axis=0)

    def apply(kind, where, gradient):
        rates, decays = kind_rates(), (MATRIX_DECAY,) * 4 + (0.0, 0.0)
        m, f, s = (ins[3 * kind + i][where] for i in range(3))
        results = adamw(m, f, s, gradient, rates[kind], decays[kind])
        for i in range(4):
            outs[4 * kind + i][where] = results[i]

    attn = total[:band]
    def pair(a, b):
        return jnp.concatenate([attn[:, a : a + 128], attn[:, b : b + 64]], axis=1)
    apply(0, (slice(None), 0), pair(0, 384))
    apply(0, (slice(None), 1), pair(128, 512))
    apply(0, (slice(None), 2), pair(256, 448))
    apply(1, (slice(None),), pair(640, 576).T)
    up = total[band + 16 : 2 * band + 16]
    down = total[2 * band + 16 :]
    down = down.T
    width = D // 4
    for f in range(4):
        apply(2, (slice(None), f), up[:, f * width : (f + 1) * width])
        apply(3, (f,), down[f * width : (f + 1) * width])
    apply(4, (slice(None),), shared)
    apply(5, (slice(None),), split)


def step(total, state):
    vm = pl.BlockSpec(memory_space=pltpu.VMEM)
    shapes = []
    for kind in range(6):
        shape = state[3 * kind].shape
        shapes += [jax.ShapeDtypeStruct(shape, t) for t in (f32, bf16, f32, f32)]
    return pl.pallas_call(
        step_kernel,
        out_shape=shapes,
        in_specs=[vm] * 19,
        out_specs=[vm] * 24,
        compiler_params=pltpu.CompilerParams(vmem_limit_bytes=56 * 1024 * 1024),
    )(total, *state)


def pack_attention(qkv, out):
    q, k, v = qkv[:, 0], qkv[:, 1], qkv[:, 2]
    return jnp.concatenate(
        [
            q[:, :128], k[:, :128], v[:, :128],
            q[:, 128:], v[:, 128:], k[:, 128:], out[:, 128:], out[:, :128],
        ],
        axis=1,
    )


def unpack_attention(block):
    pair = [block[:, 128 * i : 128 * i + 128] for i in range(6)]
    q = jnp.concatenate([pair[0], pair[3][:, :64]], axis=1)
    k = jnp.concatenate([pair[1], pair[4][:, :64]], axis=1)
    v = jnp.concatenate([pair[2], pair[3][:, 64:]], axis=1)
    o = jnp.concatenate([pair[5], pair[4][:, 64:]], axis=1)
    return jnp.stack([q, k, v], axis=1), o


def gather_plain(masters):
    qkv, out, up, down, shared, split = (t.astype(bf16) for t in masters)
    band, thin, width = shared.shape[1], split.shape[1], down.shape[1] * lax.axis_size("tensor")
    groups = lax.axis_size("tensor")
    own = jnp.stack(
        [pack_attention(qkv, out.T), up.reshape(band, -1), down.reshape(-1, band).T]
    )
    mats = lax.all_gather(own, AXES, axis=1, tiled=True).reshape(3, groups, 8, BAND, width)
    shared = lax.all_gather(shared, "dp", axis=1, tiled=True)
    split = lax.all_gather(split, AXES, axis=1, tiled=True).reshape(-1, groups, width // groups)
    bq, bv = split[0], split[1]
    zero = jnp.zeros((groups, 128), bf16)
    attn_bias = [bq[:, :128], zero, bv[:, :128], bq[:, 128:], bv[:, 128:], zero, zero]
    lines = [
        jnp.broadcast_to(shared, (groups, 6, width)),
        jnp.concatenate(attn_bias, axis=1)[:, None],
        jnp.swapaxes(split[2:], 0, 1).reshape(groups, 1, width),
    ]
    lines = jnp.pad(jnp.concatenate(lines, axis=1)[:, None], ((0, 0), (0, 7), (0, 8), (0, 0)))
    return jnp.concatenate([mats[0], lines], axis=2), mats[1], mats[2]


def step_plain(grads, mixed, grad_inputs, state):
    masters, firsts, seconds = state[0::3], state[1::3], state[2::3]
    band, thin = masters[4].shape[1], masters[5].shape[1]
    groups, copies = lax.axis_size("tensor"), lax.axis_size("dp")
    z, at = lax.axis_index("tensor"), lax.axis_index("dp")
    width = grads[0].shape[-1]
    summed = [
        lax.psum_scatter(
            g[:, :, :BAND].reshape(groups * copies, band, width), AXES, scatter_dimension=0
        ).astype(f32)
        for g in grads
    ]
    vec = lax.psum(grads[0][0, 0, BAND:].astype(f32), AXES)
    shared = lax.dynamic_slice_in_dim(vec[:6], at * band, band, 1)
    cols = lax.dynamic_slice_in_dim(vec[6:10], z, 1, 0)[0]
    ups = lax.dynamic_slice_in_dim(vec[10:14], z, 1, 0).reshape(-1, width // groups)
    split = jnp.stack(
        [
            jnp.concatenate([cols[:128], cols[384:448]]),
            jnp.concatenate([cols[256:384], cols[448:512]]),
        ]
    )
    split = lax.dynamic_slice_in_dim(jnp.concatenate([split, ups]), at * thin, thin, 1)
    sum_qkv, sum_out = unpack_attention(summed[0])
    gradients = (
        sum_qkv,
        sum_out.T,
        summed[1].reshape(masters[2].shape),
        summed[2].T.reshape(masters[3].shape),
        shared,
        split,
    )
    decays = (MATRIX_DECAY, MATRIX_DECAY, MATRIX_DECAY, MATRIX_DECAY, 0.0, 0.0)
    rates = kind_rates()
    outputs = []
    for kind in range(6):
        outputs.extend(
            adamw(masters[kind], firsts[kind], seconds[kind], gradients[kind], rates[kind], decays[kind])
        )
    mixed, grad_inputs = (lax.all_gather(t, "tensor") for t in (mixed, grad_inputs))
    return mixed, grad_inputs, outputs


def local(tokens, cotangent, counts, *state):
    masters = state[0::3]
    if (lax.axis_size("tensor"), lax.axis_size("dp")) == (4, 8):
        mixed, grad_inputs, total = layer(True, tokens, cotangent, counts, masters)
        outputs = step(total, state)
    else:
        mats = gather_plain(masters)
        mixed, grad_inputs, *grads = layer(False, tokens, cotangent, counts, mats)
        mixed, grad_inputs, outputs = step_plain(grads, mixed, grad_inputs, state)
    return (mixed, grad_inputs.astype(f32), *outputs)


def solution(mesh):
    rows = P("dp", None, None)
    state = (
        P("dp", None, "tensor"),
        P("tensor", "dp"),
        P("dp", None, "tensor"),
        P(None, "tensor", "dp"),
        P(None, "dp"),
        P(None, ("tensor", "dp")),
    )
    in_specs = (rows, rows, P("dp")) + tuple(s for s in state for _ in range(3))
    out_specs = (rows, rows) + tuple(s for s in state for _ in range(4))
    return jax.shard_map(local, mesh=mesh, in_specs=in_specs, out_specs=out_specs, check_vma=False)
```

```python
import functools

import jax
import jax.numpy as jnp
from jax import lax
from jax.experimental import pallas as pl
from jax.experimental.pallas import tpu as pltpu
from jax.sharding import PartitionSpec as P

D = 768
FF = 3072
HEAD_DIM = 64
LEN = 576
STEP = 10


LN_EPS = 1e-05
MASK_FILL = -1e30
BETA_ONE = 0.5
BETA_TWO = 0.5
ADAM_EPS = 1e-08
MATRIX_DECAY = 0.01
SQRT_HALF = 0.7071067811865476
INV_ROOT_TAU = 0.3989422804014327
AXES = ("tensor", "dp")
MESH = pl.DeviceIdType.MESH
bf16, f32 = jnp.bfloat16, jnp.float32
NN = (((1,), (0,)), ((), ()))
NT = (((1,), (1,)), ((), ()))
RT = 192
RL = 96
BAND = 96


def kind_rates():
    return (
        0.7 * D ** (-0.5),
        0.7 * (D * 16 // LEN) ** (-0.5),
        0.7 * D ** (-0.5),
        0.7 * FF ** (-0.5),
        0.6,
        0.4,
    )


def adamw(master, first, second, gradient, step_rate, decay_rate):
    first_new = BETA_ONE * first + (1.0 - BETA_ONE) * gradient
    second_new = BETA_TWO * second + (1.0 - BETA_TWO) * gradient * gradient
    first_hat = first_new / (1.0 - BETA_ONE**STEP)
    second_hat = second_new / (1.0 - BETA_TWO**STEP)
    master_new = master - step_rate * (
        first_hat / (jnp.sqrt(second_hat) + ADAM_EPS) + decay_rate * master
    )
    return (master_new, master_new.astype(jnp.bfloat16), first_new, second_new)


def flip(index, bit):
    return index + bit - 2 * bit * lax.rem(lax.div(index, bit), 2)

def send(src, dst, ssem, rsem, to):
    return pltpu.make_async_remote_copy(
        src_ref=src, dst_ref=dst, send_sem=ssem, recv_sem=rsem, device_id=to, device_id_type=MESH
    )

def arrived(dst, sem):
    pltpu.make_async_copy(dst, dst, sem).wait()

def greet(z, nz, me, others, meanwhile):
    bar = pltpu.get_barrier_semaphore()
    for d in others:
        pl.semaphore_signal(bar, inc=1, device_id=(d, z), device_id_type=MESH)
    @pl.when(z > 0)
    def _():
        pl.semaphore_signal(bar, inc=1, device_id=(me, z - 1), device_id_type=MESH)
    @pl.when(z < nz - 1)
    def _():
        pl.semaphore_signal(bar, inc=1, device_id=(me, z + 1), device_id_type=MESH)
    meanwhile()
    edges = jnp.where(z > 0, 1, 0) + jnp.where(z < nz - 1, 1, 0)
    pl.semaphore_wait(bar, len(others) + edges)


def mm(a, b, dims=NN):
    return lax.dot_general(a, b, dims, preferred_element_type=f32)

def normal_of(rows):
    mean = jnp.mean(rows, axis=-1, keepdims=True)
    centred = rows - mean
    inverse = lax.rsqrt(jnp.mean(centred * centred, axis=-1, keepdims=True) + LN_EPS)
    return centred * inverse, inverse

def normal_back(grad, normal, inverse, gain):
    scaled = grad * gain
    return inverse * (
        scaled
        - jnp.mean(scaled, axis=-1, keepdims=True)
        - normal * jnp.mean(scaled * normal, axis=-1, keepdims=True)
    )

def row_tiles(size):
    return range(0, LEN, size)

def colsum(v):
    return jnp.sum(v, axis=0, keepdims=True)

def pack(own, pad, qkv, out, shared, split):
    band, thin = shared.shape[1], split.shape[1]
    me = lax.axis_index("dp")
    low = [qkv[i].astype(bf16) for i in range(3)]
    ot = out[...].T.astype(bf16)
    pieces = [
        low[0][:, :128], low[1][:, :128], low[2][:, :128],
        jnp.concatenate([low[0][:, 128:], low[2][:, 128:]], axis=1),
        jnp.concatenate([low[1][:, 128:], ot[:, 128:]], axis=1),
        ot[:, :128],
    ]
    for i, piece in enumerate(pieces):
        own[0:band, 128 * i : 128 * i + 128] = piece
    width = D // 4
    pad[...] = jnp.zeros_like(pad)
    pad[0:6, 0:band] = shared[...]
    pad[8:14, 0:thin] = split[...]
    vals = pad[...].astype(bf16)
    src = lax.broadcasted_iota(jnp.int32, (128, D), 0)
    col = lax.broadcasted_iota(jnp.int32, (128, D), 1)

    def placed(spot):
        return mm(vals, jnp.where(col == spot, 1.0, 0.0).astype(bf16))

    at = me * thin + src
    attn = placed(jnp.where(at < 128, at, at + 256))[8:9]
    attn += placed(jnp.where(at < 128, at + 256, at + 320))[9:10]
    ups = sum(placed(f * width + at)[10 + f : 11 + f] for f in range(4))
    rows = [placed(me * band + src)[0:6], attn, ups, jnp.zeros((8, D), f32)]
    own[band : band + 16] = jnp.concatenate(rows, axis=0).astype(bf16)


def pack_rest(own, up, down):
    band = up.shape[0]
    width = D // 4
    for f in range(4):
        own[band + 16 : 2 * band + 16, f * width : (f + 1) * width] = up[:, f].astype(bf16)
        own[2 * band + 16 : 3 * band + 16, f * width : (f + 1) * width] = down[f].T.astype(bf16)


def gather_steps(own, outs, masters_rows, z, me, sems):
    rows_of = masters_rows
    nb, nz = len(rows_of), 4
    lsem, zs, zr, ps, pr, ds, dr, cs, cr = sems
    cp, xp, yp = flip(me, 1), flip(me, 2), flip(me, 4)
    dg = flip(xp, 4)
    pair = (xp, yp)
    starts = [sum(rows_of[:b]) for b in range(nb)]
    half = [[(0, 48), (48, r - 48)] for r in rows_of]

    def own_ref(b):
        return own.at[pl.ds(starts[b], rows_of[b])]
    def right(b, s, src):
        return send(src, outs[b].at[s, me], zs.at[b, 0, z - s], zr.at[b, s], (me, z + 1))
    def left(b, s, src):
        return send(src, outs[b].at[s, me], zs.at[b, 1, s - z], zr.at[b, s], (me, z - 1))
    def side(b, s, src, k):
        return send(src, outs[b].at[s, me], ps.at[b, k, s], pr.at[b, k, s], (pair[k], z))
    def spread(b, s, src):
        for k in range(2):
            side(b, s, src, k).start()
    def diag(b, k):
        lo, n = half[b][k]
        part = outs[b].at[:, pair[k], pl.ds(lo, n)]
        return send(part, part, ds.at[b, k], dr.at[b, k], (pair[1 - k], z))
    def twin(b, j):
        part = outs[b].at[:, (me, xp, yp, dg)[j]]
        return send(part, part, cs.at[b, j], cr.at[b, j], (cp, z))
    def keep(b):
        return pltpu.make_async_copy(own_ref(b), outs[b].at[z, me], lsem.at[b])

    def opens(b):
        @pl.when(z < nz - 1)
        def _():
            right(b, z, own_ref(b)).start()
        @pl.when(z > 0)
        def _():
            left(b, z, own_ref(b)).start()
        spread(b, z, own_ref(b))
        keep(b).start()
    def hop(b, t):
        @pl.when(z >= t)
        def _():
            s = z - t
            arrived(outs[b].at[s, me], zr.at[b, s])
            @pl.when(z < nz - 1)
            def _():
                right(b, s, outs[b].at[s, me]).start()
            spread(b, s, outs[b].at[s, me])
        @pl.when(z + t < nz)
        def _():
            s = z + t
            arrived(outs[b].at[s, me], zr.at[b, s])
            @pl.when(z > 0)
            def _():
                left(b, s, outs[b].at[s, me]).start()
            spread(b, s, outs[b].at[s, me])
    def lined(b):
        keep(b).wait()
        twin(b, 0).start()
    def square(b):
        for k in range(2):
            for s in range(4):
                arrived(outs[b].at[s, pair[k]], pr.at[b, k, s])
            diag(b, k).start()
            twin(b, 1 + k).start()
    def corner(b):
        for k in range(2):
            lo, n = half[b][k]
            arrived(outs[b].at[:, dg, pl.ds(lo, n)], dr.at[b, k])
        twin(b, 3).start()
    def ready(b):
        for j, d in enumerate((cp, flip(xp, 1), flip(yp, 1), flip(dg, 1))):
            arrived(outs[b].at[:, d], cr.at[b, j])
    def sent(b):
        for t in range(4):
            @pl.when((z < nz - 1) & (z >= t))
            def _():
                right(b, z - t, outs[b].at[z - t, me]).wait_send()
            @pl.when((z > 0) & (z + t < nz))
            def _():
                left(b, z + t, outs[b].at[z + t, me]).wait_send()
            for k in range(2):
                side(b, t, outs[b].at[t, me], k).wait_send()
            twin(b, t).wait_send()
        for k in range(2):
            diag(b, k).wait_send()
    return opens, hop, lined, square, corner, ready, sent


def line_steps(block, whole, z, me, sems, rows=pl.ds(0, LEN)):
    nz = 4
    ms, mr, ml = sems

    def along(s, src, way):
        return send(src, whole.at[s, rows], ms.at[(way + 1) // 2, jnp.abs(s - z)], mr.at[s], (me, z + way))
    def keep():
        return pltpu.make_async_copy(block.at[rows], whole.at[z, rows], ml.at[0])
    def opens():
        @pl.when(z < nz - 1)
        def _():
            along(z, block.at[rows], 1).start()
        @pl.when(z > 0)
        def _():
            along(z, block.at[rows], -1).start()
        keep().start()
    def hop(t):
        for way, ok in ((-1, z >= t), (1, z + t < nz)):
            @pl.when(ok)
            def _():
                s = z + way * t
                arrived(whole.at[s, rows], mr.at[s])
                @pl.when((z < nz - 1) if way < 0 else (z > 0))
                def _():
                    along(s, whole.at[s, rows], -way).start()
    def close():
        keep().wait()
        for t in range(4):
            @pl.when((z < nz - 1) & (z >= t))
            def _():
                along(z - t, whole.at[z - t, rows], 1).wait_send()
            @pl.when((z > 0) & (z + t < nz))
            def _():
                along(z + t, whole.at[z + t, rows], -1).wait_send()
    return opens, hop, close


def reduce_steps(own, got_b, landing, rows_of, z, me, sems):
    cs, cr, hs, hr, ss, sr, zs, zr, ds, dr = sems
    nz = 4
    xp, yp = flip(me, 2), flip(me, 4)
    pair = (xp, yp)
    cp = flip(me, 1)
    half = [((0, 48), (48, r - 48)) for r in rows_of]
    everything = slice(None)

    def add(dst, *srcs):
        dst[...] = sum((t[...].astype(f32) for t in srcs), dst[...].astype(f32)).astype(bf16)
    def over_z(body):
        lax.fori_loop(0, nz, lambda g, c: (body(g), c)[1], 0)
    def twin(b, g, src, j):
        return send(src, came(b, j, g), cs.at[b, j, g], cr.at[b, j, g], (cp, z))
    def came(b, j, g):
        return got_b[b - 1].at[j, g] if b else landing(0, 5 + j, g, pl.ds(0, 96))
    def twin_vec(g, j, src):
        return send(src, landing(0, 5 + j, g, pl.ds(96, 16)), ds.at[j, g], dr.at[j, g], (cp, z))
    def merge(b):
        def body(g):
            for j in (3, 1, 2, 0):
                arrived(came(b, j, g), cr.at[b, j, g])
                if b:
                    add(own[b].at[j, g], came(b, j, g))
                else:
                    arrived(landing(0, 5 + j, g, pl.ds(96, 16)), dr.at[j, g])
                    add(own[0].at[j, g], landing(0, 5 + j, g, pl.ds(0, 112)))
        over_z(body)
        for k in range(2):
            corner(b, k).start()
    def corner(b, k):
        part = pl.ds(*half[b][k])
        return send(own[b].at[3, :, part], landing(b, 0, everything, part), hs.at[b, k], hr.at[b, k], (pair[k], z))
    def square(b, k):
        return send(own[b].at[1 + k], landing(b, 1 + k), ss.at[b, k], sr.at[b, k], (pair[k], z))
    def third(b):
        for k in range(2):
            part = pl.ds(*half[b][k])
            arrived(landing(b, 0, everything, part), hr.at[b, k])
            over_z(lambda g: add(own[b].at[2 - k, g, part], landing(b, 0, g, part)))
            square(b, 1 - k).start()
    def fourth(b):
        for k in range(2):
            arrived(landing(b, 1 + k), sr.at[b, k])
        over_z(lambda g: add(own[b].at[0, g], landing(b, 1, g), landing(b, 2, g)))
        along(b, 0)
    def line(b, t, way):
        side = (1 - way) // 2
        return send(own[b].at[0, t], landing(b, 3 + side, t), zs.at[b, t], zr.at[b, side, t], (me, z + way))
    def along(b, i):
        for way, begin in ((1, i), (-1, nz - 1 - i)):
            side = (1 - way) // 2
            targets = range(nz - 1, begin, -1) if way > 0 else range(begin)
            @pl.when(z == begin)
            def _():
                for t in targets:
                    if i:
                        arrived(landing(b, 3 + side, t), zr.at[b, side, t])
                        add(own[b].at[0, t], landing(b, 3 + side, t))
                    line(b, t, way).start()
    def last(b, total, at):
        total[pl.ds(at, rows_of[b])] = own[b][0, z].astype(f32)
        for side, ok in ((0, z > 0), (1, z < nz - 1)):
            @pl.when(ok)
            def _():
                arrived(landing(b, 3 + side, z), zr.at[b, side, z])
                total[pl.ds(at, rows_of[b])] += landing(b, 3 + side, z)[...].astype(f32)
    def closed(b):
        for k in range(2):
            corner(b, k).wait_send()
            square(b, k).wait_send()
        for t in range(nz):
            @pl.when(z < t)
            def _():
                line(b, t, 1).wait_send()
            @pl.when(z > t)
            def _():
                line(b, t, -1).wait_send()
    return twin, twin_vec, merge, third, fourth, along, last, closed


QT = ((0, 256), (256, 256), (512, 64))


def layer_kernel(linked, *refs):
    tokens, cotangent, counts = refs[:3]
    weights_in = refs[3 : 9 if linked else 6]
    refs = refs[9 if linked else 6 :]
    n_out = 3 if linked else 5
    outs, refs = refs[:n_out], refs[n_out:]
    (WA, WB, WC, x, gout_low, first_in, second_in, left_t, right_t, qkv, probs, att,
     middle, acc, hs, stage, bsum, vrow, vecs, bias, mixed, sems) = refs[:22]
    refs = refs[22:]
    gm_low, ig = second_in, first_in
    hidden, slope = hs.at[pl.ds(0, 4)], hs.at[pl.ds(4, 4)]
    z, me = lax.axis_index("tensor"), lax.axis_index("dp")
    band = BAND
    if linked:
        mixed_all, ig_all, total_out = outs
        own, pad = stage, refs[0]
        rows_of = (band + 16, band, band)
        opens, hop, lined, square, corner, ready, sent = gather_steps(
            own, (WA, WB, WC), rows_of, z, me, refs[1:10]
        )
        tail_sems = refs[len(refs) - 18 :]
        pieces = [
            line_steps(block, whole, z, me, tail_sems[3 * (3 * i + c) : 3 * (3 * i + c) + 3], pl.ds(192 * c, 192))
            for i, (block, whole) in enumerate(((mixed, mixed_all), (ig, ig_all)))
            for c in range(3)
        ]
        def mopen():
            for c in range(3):
                pieces[c][0]()
        def mhop(t, c):
            pieces[c][1](t)
        def mclose():
            for c in range(3):
                pieces[c][2]()
        def iopen(c):
            pieces[3 + c][0]()
        def ihop(t, c):
            pieces[3 + c][1](t)
        parts, got_b, freed = refs[10:13], refs[13:15], refs[15]
        def landing(b, i, g=slice(None), part=None):
            if b:
                part = pl.ds(0, band) if part is None else part
                return (WB, WC)[b - 1].at[g, i, part]
            base, spot = (0, 4) if i == 0 else (4, i - 1) if i < 5 else (0, i - 5)
            lo, n = (0, band + 16) if part is None else (part.start, part.size)
            g = pl.ds(base, 4) if isinstance(g, slice) else base + g
            return hs.at[g, pl.ds((band + 16) * spot + lo, n)]
        twin, twin_vec, merge, third, fourth, along, last, closed = reduce_steps(
            parts, got_b, landing, rows_of, z, me, refs[16:26]
        )
        def staged(slot, j):
            return stage.at[pl.ds((4 * slot + j) * band, band)]
        def release():
            for d in (flip(me, 1), flip(me, 2), flip(me, 4)):
                pl.semaphore_signal(freed, inc=1, device_id=(d, z), device_id_type=MESH)
            @pl.when(z > 0)
            def _():
                pl.semaphore_signal(freed, inc=1, device_id=(me, z - 1), device_id_type=MESH)
            @pl.when(z < 3)
            def _():
                pl.semaphore_signal(freed, inc=1, device_id=(me, z + 1), device_id_type=MESH)
        def acquire():
            pl.semaphore_wait(freed, 3 + jnp.where(z > 0, 1, 0) + jnp.where(z < 3, 1, 0))
    else:
        def nothing(*args):
            return None
        opens = hop = lined = square = corner = sent = mhop = nothing
        release = acquire = merge = third = fourth = along = nothing
        mixed_all, ig_out, gA, gB, gC = outs
        def ready(b):
            pltpu.make_async_copy(weights_in[b], (WA, WB, WC)[b], sems.at[8 + b]).wait()
        def mopen():
            pltpu.make_async_copy(mixed, mixed_all, sems.at[11]).start()
        def mclose():
            pltpu.make_async_copy(mixed, mixed_all, sems.at[11]).wait()

    loads = [
        pltpu.make_async_copy(tokens.at[z], x, sems.at[6]),
        pltpu.make_async_copy(cotangent.at[z], gout_low, sems.at[7]),
    ]
    for load in loads:
        load.start()
    if linked:
        greet(z, 4, me, (flip(me, 1), flip(me, 2), flip(me, 4)), lambda: pack(own, pad, *weights_in[:2], *weights_in[4:]))
    else:
        for b in range(3):
            pltpu.make_async_copy(weights_in[b], (WA, WB, WC)[b], sems.at[8 + b]).start()
    count = counts[z]
    column = lax.broadcasted_iota(jnp.int32, (LEN, 1), 0)
    keybias = jnp.where(column < count, 0.0, MASK_FILL)
    def valid(r):
        return jnp.where(lax.broadcasted_iota(jnp.int32, (RL, 1), 0) + r < count, 1.0, 0.0)

    def transpose(dst, src):
        turned = src[...].T
        for d in range(8):
            spot = d
            if linked:
                apart = [lax.rem(lax.div(me, 1 << i) + (d >> i), 2) for i in range(3)]
                spot = 4 * apart[0] + apart[1] + 2 * apart[2]
            dst[pl.ds(pl.multiple_of(spot * band, 32), band)] = turned[d * band : (d + 1) * band]

    opens(0)
    if linked:
        pack_rest(own, *weights_in[2:4])
    for load in loads:
        load.wait()
    for r in row_tiles(RL):
        rs = pl.ds(r, RL)
        gout_low[rs] = (gout_low[rs].astype(f32) * valid(r)).astype(bf16)
        middle[rs] = normal_of(x[rs].astype(f32))[0]
    hop(0, 1)
    hop(0, 2)
    opens(1)
    transpose(right_t, gout_low)
    hop(0, 3)
    lined(0)
    hop(1, 1)
    opens(2)
    square(0)
    hop(1, 2)
    hop(2, 1)
    hop(1, 3)
    lined(1)
    hop(2, 2)
    corner(0)
    hop(2, 3)
    lined(2)
    ready(0)
    lines = [sum(WA[g, i, band : band + 16].astype(f32) for i in range(8)) for g in range(4)]
    vecs[...] = lines[0]
    for g in range(4):
        bias[0, g] = lines[g][6:7]
        bias[1, g] = lines[g][7:8]
    for r in row_tiles(RL):
        rs = pl.ds(r, RL)
        first_in[rs] = (middle[rs] * vecs[0:1] + vecs[1:2]).astype(bf16)
    lane = lax.broadcasted_iota(jnp.int32, (1, 128), 1)
    low = lane < 64
    acc[...] = jnp.zeros_like(acc)

    def at(g, table):
        for i, steps in enumerate(table):
            if steps:
                @pl.when(g == i)
                def _():
                    for step, *args in steps:
                        step(*args)
    def wa(g, lo=0, hi=D):
        return WA[g, :, 0:band, lo:hi].reshape(D, hi - lo)
    def wb(g):
        return WB[g].reshape(D, D)
    def wc(g):
        return WC[g].reshape(D, D)

    def forward(g, carry):
        for r in row_tiles(RT):
            rs = pl.ds(r, RT)
            qkv[g, rs] = (mm(first_in[rs], wa(g)) + bias[0, g]).astype(bf16)
        def tile(i):
            return qkv[g, :, 128 * i : 128 * i + 128]
        outs = []
        for h in range(3):
            q, k, v = (tile(0), tile(1), tile(2)) if h < 2 else (tile(3), tile(4), tile(3))
            q = jnp.where(low if h != 1 else ~low, q, 0) * bf16(0.125)
            vt = v.T
            vt = vt[64:] if h else vt[:64]
            cols = []
            for r, n in QT:
                s = mm(k, q[r : r + n], NT) + keybias
                e = jnp.exp(s - jnp.max(s, axis=0, keepdims=True))
                p = (e * (1.0 / jnp.sum(e, axis=0, keepdims=True))).astype(bf16)
                probs[g, h, :, pl.ds(r, n)] = p
                cols.append(mm(vt, p))
            outs.append(jnp.concatenate(cols, axis=1))
        att[g, :, 128:256] = jnp.concatenate(outs[:2], axis=0).T.astype(bf16)
        att[g, :, 0:128] = jnp.concatenate([jnp.zeros_like(outs[2]), outs[2]], axis=0).T.astype(bf16)
        for r in row_tiles(RT):
            rs = pl.ds(r, RT)
            acc[rs] += mm(att[g, rs], wa(g, 512, D), NT)
        at(g, [[(square, 1)], [], [(corner, 1)], [(square, 2)]])
        return carry
    lax.fori_loop(0, 4, forward, 0)

    for r in row_tiles(RL):
        rs = pl.ds(r, RL)
        m = x[rs].astype(f32) + acc[rs] + vecs[2:3]
        middle[rs] = m
        second_in[rs] = (normal_of(m)[0] * vecs[3:4] + vecs[4:5]).astype(bf16)
    transpose(left_t, second_in)
    acc[...] = jnp.zeros_like(acc)
    ready(1)

    def mlp_up(g, carry):
        for r in row_tiles(RT):
            rs = pl.ds(r, RT)
            u = mm(second_in[rs], wb(g)) + bias[1, g]
            phi = 0.5 * (1.0 + lax.erf(u * SQRT_HALF))
            hidden[g, rs] = (u * phi).astype(bf16)
            slope[g, rs] = (phi + u * jnp.exp(-0.5 * u * u) * INV_ROOT_TAU).astype(bf16)
        return carry
    lax.fori_loop(0, 4, mlp_up, 0)
    corner(2)
    ready(2)

    def mlp_down(g, carry):
        for r in row_tiles(RT):
            rs = pl.ds(r, RT)
            acc[rs] += mm(hidden[g, rs], wc(g), NT)
        return carry
    lax.fori_loop(0, 4, mlp_down, 0)
    for r in row_tiles(RL):
        rs = pl.ds(r, RL)
        mixed[rs] = ((middle[rs] + acc[rs] + vecs[5:6]) * valid(r)).astype(bf16)
    mopen()
    acc[...] = jnp.zeros_like(acc)

    def off(dst, g, slot):
        return pltpu.make_async_copy(stage.at[slot], dst.at[g, :, pl.ds(0, band)], sems.at[slot])
    def put(dst, g, slot, part):
        @pl.when(g > 0)
        def _():
            off(dst, g - 1, slot).wait()
        for c in range(0, D, 2 * band):
            stage[slot, pl.ds(c // band, 2)] = part(c).astype(bf16).reshape(2, band, D)
        off(dst, g, slot).start()
    def share_out(b, g, slot, part):
        def sending(gg):
            return [twin(b, gg, staged(slot, j), j) for j in range(4)]
        kept = part(0, 4 * band).astype(bf16)
        for j in range(4):
            parts[b][j, g, pl.ds(0, band)] = kept[j * band : (j + 1) * band]
        @pl.when(g > 0)
        def _():
            for copy in sending(g - 1):
                copy.wait_send()
        stage[pl.ds(4 * slot * band, 4 * band)] = part(4 * band, 4 * band).astype(bf16)
        for copy in sending(g):
            copy.start()
        @pl.when(g == 3)
        def _():
            for copy in sending(g):
                copy.wait_send()
    def give(b, g, slot, part):
        if linked:
            share_out(b, g, slot, part)
        else:
            put((gA, gB, gC)[b], g, slot, lambda c: part(c, 2 * band))

    def mlp_back(g, carry):
        for r in row_tiles(RT):
            rs = pl.ds(r, RT)
            gp = (mm(gout_low[rs], wc(g)) * slope[g, rs].astype(f32)).astype(bf16)
            slope[g, rs] = gp
            acc[rs] += mm(gp, wb(g), NT)
        bsum[1, g] = colsum(slope[g].astype(f32))
        give(2, g, 0, lambda c, n: mm(right_t[pl.ds(c, n)], hidden[g]))
        give(1, g, 1, lambda c, n: mm(left_t[pl.ds(c, n)], slope[g]))
        at(g, [[], [], [(mhop, 1, 0)], [(mhop, 1, 1)]])
        return carry
    for b in range(3):
        sent(b)
    lax.fori_loop(0, 4, mlp_back, 0)
    release()
    if not linked:
        off(gC, 3, 0).wait()
        off(gB, 3, 1).wait()

    sums = [jnp.zeros((1, D), f32) for _ in range(6)]
    for r in row_tiles(RL):
        rs = pl.ds(r, RL)
        n, inv = normal_of(middle[rs])
        gn = acc[rs]
        go = gout_low[rs].astype(f32)
        t = go + normal_back(gn, n, inv, vecs[3:4])
        middle[rs] = t
        gm_low[rs] = t.astype(bf16)
        sums[2] += colsum(t)
        sums[3] += colsum(gn * n)
        sums[4] += colsum(gn)
        sums[5] += colsum(go)
    merged = [(mhop, 1, 2), (acquire,), (merge, 2), (merge, 1), (mhop, 2, 0)]
    for act, *args in merged:
        act(*args)
    transpose(left_t, first_in)
    transpose(right_t, gm_low)
    acc[...] = jnp.zeros_like(acc)

    def backward(g, carry):
        ga = mm(gm_low[...], wa(g, 512, D)).astype(bf16)
        def tile(i):
            return qkv[g, :, 128 * i : 128 * i + 128]
        dq, dk, dv = [], [], []
        for h in range(3):
            q, k, v = (tile(0), tile(1), tile(2)) if h < 2 else (tile(3), tile(4), tile(3))
            gt = ga[:, 128:256] if h < 2 else ga[:, 0:128]
            gmask = jnp.where(low if h == 0 else ~low, gt, 0)
            kt = k.T
            kt = kt[64:] if h == 1 else kt[:64]
            dqs, dks, dvs = [], 0.0, 0.0
            for r, n in QT:
                p = probs[g, h, :, pl.ds(r, n)]
                dp = mm(v, gmask[r : r + n], NT)
                pf = p.astype(f32)
                inner = jnp.sum(pf * dp, axis=0, keepdims=True)
                ds = (pf * (dp - inner)).astype(bf16)
                dqs.append(mm(kt, ds))
                dks = dks + mm(ds, q[r : r + n])
                dvs = dvs + mm(p, gt[r : r + n])
            dq.append(jnp.concatenate(dqs, axis=1))
            dk.append(dks * 0.125)
            dv.append(dvs)
        dq01 = jnp.concatenate(dq[:2], axis=0).T * 0.125
        dq2 = jnp.concatenate([dq[2], jnp.zeros_like(dq[2])], axis=0).T * 0.125
        parts = [
            dq01,
            jnp.where(low, dk[0], dk[1]),
            jnp.where(low, dv[0], dv[1]),
            jnp.where(low, dq2, dv[2]),
            jnp.where(low, dk[2], 0.0),
        ]
        for i, part in enumerate(parts):
            part = part.astype(bf16)
            qkv[g, :, 128 * i : 128 * i + 128] = part
            bsum[0, g, :, 128 * i : 128 * i + 128] = colsum(part.astype(f32))
        qkv[g, :, 640:768] = jnp.zeros((LEN, 128), bf16)
        bsum[0, g, :, 640:768] = jnp.zeros((1, 128), f32)
        for r in row_tiles(RT):
            rs = pl.ds(r, RT)
            acc[rs] += mm(qkv[g, rs], wa(g), NT)
        at(g, BACK)
        return carry
    BACK = [
        [(third, 2), (mhop, 2, 1)],
        [(mhop, 2, 2), (third, 1)],
        [],
        [],
    ]
    lax.fori_loop(0, 4, backward, 0)

    for r in row_tiles(RL):
        rs = pl.ds(r, RL)
        n, inv = normal_of(x[rs].astype(f32))
        gn = acc[rs]
        first_in[rs] = (middle[rs] + normal_back(gn, n, inv, vecs[0:1])).astype(bf16)
        sums[0] += colsum(gn * n)
        sums[1] += colsum(gn)
    lines = sums + [bsum[i, j] for i in range(2) for j in range(4)] + [jnp.zeros((2, D), f32)]
    lines = jnp.concatenate(lines, axis=0).astype(bf16)
    fourth(2)
    if linked:
        for c in range(3):
            iopen(c)

    def attention_grads(g, carry):
        def part(c, n):
            first = mm(left_t[pl.ds(c, n)], qkv[g])
            second = mm(right_t[pl.ds(c, n)], att[g])
            return jnp.concatenate([first[:, :512], first[:, 512:] + second], axis=1)
        give(0, g, 0, part)
        at(g, [[], [], [(along, 2, 1)], []])
        return carry
    lax.fori_loop(0, 4, attention_grads, 0)
    if linked:
        vrow[0] = lines
        def vec_step(g, act):
            for j in range(4):
                act(twin_vec(g, j, vrow.at[0]))
        for g in range(4):
            vec_step(g, lambda copy: copy.start())
            for j in range(4):
                parts[0][j, g, pl.ds(band, 16)] = lines
        fourth(1)
        merge(0)
        ihop(1, 0)
        third(0)
        ihop(1, 1)
        along(1, 1)
        ihop(1, 2)
        along(2, 2)
        ihop(2, 0)
        fourth(0)
        ihop(2, 1)
        along(1, 2)
        along(0, 1)
        ihop(2, 2)
        last(2, acc, 2 * band + 16)
        along(0, 2)
        last(1, acc, band + 16)
        last(0, acc, 0)
        done = pltpu.make_async_copy(acc.at[pl.ds(0, 3 * band + 16)], total_out, sems.at[1])
        done.start()
        for c in range(3):
            ihop(3, c)
        for g in range(4):
            vec_step(g, lambda copy: copy.wait_send())
        done.wait()
        for c in range(3):
            pieces[3 + c][2]()
        for b in range(3):
            closed(b)
    else:
        for i in range(8):
            vrow[i] = lines
        copies = [pltpu.make_async_copy(ig, ig_out, sems.at[1])]
        copies += [pltpu.make_async_copy(vrow, gA.at[g, :, pl.ds(band, 16)], sems.at[2 + g]) for g in range(4)]
        for copy in copies:
            copy.start()
        for copy in copies:
            copy.wait()
        off(gA, 3, 0).wait()
    for c in range(3):
        mhop(3, c)
    mclose()


def layer(linked, tokens, cotangent, counts, weights, cid=1):
    V, S = pltpu.VMEM, pltpu.SemaphoreType.DMA
    shape = jax.ShapeDtypeStruct
    hb, vm = pl.BlockSpec(memory_space=pl.ANY), pl.BlockSpec(memory_space=V)
    band, nb = BAND, 3
    rows_of = (band + 16, band, band)
    scratch = [V((4, 8, r, D), bf16) for r in rows_of]
    scratch += [V((LEN, D), bf16)] * 4 + [V((D, LEN), bf16)] * 2
    scratch += [V((4, LEN, D), bf16), V((4, 3, LEN, LEN), bf16), V((4, LEN, 256), bf16)]
    scratch += [V((LEN, D), f32)] * 2 + [V((8, LEN, D), bf16), V((8 * band, D) if linked else (2, 8, band, D), bf16)]
    scratch += [V((2, 4, 1, D), f32), V((1 if linked else 8, 16, D), bf16), V((16, D), f32)]
    scratch += [V((2, 4, 1, D), f32), V((LEN, D), bf16), S((12,))]
    outs = [shape((LEN, D), bf16)] * 2 + [shape((4, 8, r, D), bf16) for r in rows_of]
    if linked:
        outs = [shape((4, LEN, D), bf16)] * 2 + [shape((sum(rows_of), D), f32)]
        scratch += [V((16, 128), f32)]
        scratch += [S((nb,)), S((nb, 2, 4)), S((nb, 4))]
        scratch += [S((nb, 2, 4))] * 2 + [S((nb, 2))] * 2 + [S((nb, 4))] * 2
        scratch += [V((4, 4, r, D), bf16) for r in rows_of] + [V((4, 4, band, D), bf16)] * 2
        scratch += [pltpu.SemaphoreType.REGULAR] + [S((nb, 4, 4))] * 2 + [S((nb, 2))] * 4
        scratch += [S((nb, 4)), S((nb, 2, 4))] + [S((4, 4))] * 2
        scratch += [S((2, 4)), S((4,)), S((1,))] * 6
    params = dict(collective_id=cid, has_side_effects=True) if linked else {}
    return pl.pallas_call(
        functools.partial(layer_kernel, linked),
        out_shape=outs,
        in_specs=[hb, hb, pl.BlockSpec(memory_space=pltpu.SMEM)] + ([vm] * 6 if linked else [hb] * 3),
        out_specs=[hb] * len(outs),
        scratch_shapes=scratch,
        compiler_params=pltpu.CompilerParams(vmem_limit_bytes=63 * 1024 * 1024, **params),
        cost_estimate=pl.CostEstimate(
            flops=57_000_000_000, bytes_accessed=32_000_000, transcendentals=6_000_000
        ),
    )(tokens, cotangent, counts, *weights)


def step_kernel(total, low, *refs):
    ins, outs, full, (held, wide, got, put) = refs[:18], refs[18:42], refs[42], refs[43:]
    fetch = [pltpu.make_async_copy(low.at[s], held.at[s], got.at[s]) for s in range(4)]
    store = [pltpu.make_async_copy(wide.at[s], full.at[s], put.at[s]) for s in range(4)]
    for copy in fetch:
        copy.start()
    for s in range(4):
        fetch[s].wait()
        for r in row_tiles(RL):
            wide[s, pl.ds(r, RL)] = held[s, pl.ds(r, RL)].astype(f32)
        store[s].start()
    z, me = lax.axis_index("tensor"), lax.axis_index("dp")
    band, thin = ins[12].shape[1], ins[15].shape[1]
    vec = total[band : band + 16]
    row = lax.broadcasted_iota(jnp.int32, (D, 128), 0)
    col = lax.broadcasted_iota(jnp.int32, (D, 128), 1)

    def pick(source):
        chosen = jnp.where(row == source, 1.0, 0.0)
        return lax.dot_general(
            vec, chosen, NN, precision=lax.Precision.HIGHEST, preferred_element_type=f32
        )

    place = me * thin + col
    shared = pick(me * band + col)[:6, :band]
    head = jnp.where(place < 128, place, place + 256)
    late = jnp.where(place < 128, place + 256, place + 320)
    spots = [head, late] + [f * (D // 4) + place for f in range(4)]
    at = lax.broadcasted_iota(jnp.int32, (16, 128), 0)
    lines = []
    for i, spot in enumerate(spots):
        mine = jnp.where(at == z + (6 if i < 2 else 10), pick(spot), 0.0)
        lines.append(jnp.sum(mine, axis=0, keepdims=True)[:, :thin])
    split = jnp.concatenate(lines, axis=0)

    def apply(kind, where, gradient):
        rates, decays = kind_rates(), (MATRIX_DECAY,) * 4 + (0.0, 0.0)
        m, f, s = (ins[3 * kind + i][where] for i in range(3))
        results = adamw(m, f, s, gradient, rates[kind], decays[kind])
        for i in range(4):
            outs[4 * kind + i][where] = results[i]

    attn = total[:band]
    def pair(a, b):
        return jnp.concatenate([attn[:, a : a + 128], attn[:, b : b + 64]], axis=1)
    apply(0, (0,), pair(0, 384))
    apply(0, (1,), pair(128, 512))
    apply(0, (2,), pair(256, 448))
    apply(1, (slice(None),), pair(640, 576).T)
    up = total[band + 16 : 2 * band + 16]
    down = total[2 * band + 16 :]
    down = down.T
    width = D // 4
    for f in range(4):
        apply(2, (slice(None), f), up[:, f * width : (f + 1) * width])
        apply(3, (f,), down[f * width : (f + 1) * width])
    apply(4, (slice(None),), shared)
    apply(5, (slice(None),), split)
    for copy in store:
        copy.wait()


def step(total, low, state):
    V, S = pltpu.VMEM, pltpu.SemaphoreType.DMA
    vm, hb = pl.BlockSpec(memory_space=V), pl.BlockSpec(memory_space=pl.ANY)
    shapes = []
    for kind in range(6):
        shape = state[3 * kind].shape
        shapes += [jax.ShapeDtypeStruct(shape, t) for t in (f32, bf16, f32, f32)]
    shapes.append(jax.ShapeDtypeStruct(low.shape, f32))
    return pl.pallas_call(
        step_kernel,
        out_shape=shapes,
        in_specs=[vm, hb] + [vm] * 18,
        out_specs=[vm] * 24 + [hb],
        scratch_shapes=[V(low.shape, bf16), V(low.shape, f32), S((4,)), S((4,))],
        compiler_params=pltpu.CompilerParams(vmem_limit_bytes=56 * 1024 * 1024),
    )(total, low, *state)


def pack_attention(qkv, out):
    q, k, v = qkv[:, 0], qkv[:, 1], qkv[:, 2]
    return jnp.concatenate(
        [
            q[:, :128], k[:, :128], v[:, :128],
            q[:, 128:], v[:, 128:], k[:, 128:], out[:, 128:], out[:, :128],
        ],
        axis=1,
    )


def unpack_attention(block):
    pair = [block[:, 128 * i : 128 * i + 128] for i in range(6)]
    q = jnp.concatenate([pair[0], pair[3][:, :64]], axis=1)
    k = jnp.concatenate([pair[1], pair[4][:, :64]], axis=1)
    v = jnp.concatenate([pair[2], pair[3][:, 64:]], axis=1)
    o = jnp.concatenate([pair[5], pair[4][:, 64:]], axis=1)
    return jnp.stack([q, k, v], axis=1), o


def gather_plain(masters):
    qkv, out, up, down, shared, split = (t.astype(bf16) for t in masters)
    band, thin, width = shared.shape[1], split.shape[1], down.shape[1] * lax.axis_size("tensor")
    groups = lax.axis_size("tensor")
    own = jnp.stack(
        [pack_attention(qkv, out.T), up.reshape(band, -1), down.reshape(-1, band).T]
    )
    mats = lax.all_gather(own, AXES, axis=1, tiled=True).reshape(3, groups, 8, BAND, width)
    shared = lax.all_gather(shared, "dp", axis=1, tiled=True)
    split = lax.all_gather(split, AXES, axis=1, tiled=True).reshape(-1, groups, width // groups)
    bq, bv = split[0], split[1]
    zero = jnp.zeros((groups, 128), bf16)
    attn_bias = [bq[:, :128], zero, bv[:, :128], bq[:, 128:], bv[:, 128:], zero, zero]
    lines = [
        jnp.broadcast_to(shared, (groups, 6, width)),
        jnp.concatenate(attn_bias, axis=1)[:, None],
        jnp.swapaxes(split[2:], 0, 1).reshape(groups, 1, width),
    ]
    lines = jnp.pad(jnp.concatenate(lines, axis=1)[:, None], ((0, 0), (0, 7), (0, 8), (0, 0)))
    return jnp.concatenate([mats[0], lines], axis=2), mats[1], mats[2]


def step_plain(grads, mixed, grad_inputs, state):
    masters, firsts, seconds = state[0::3], state[1::3], state[2::3]
    band, thin = masters[4].shape[1], masters[5].shape[1]
    groups, copies = lax.axis_size("tensor"), lax.axis_size("dp")
    z, at = lax.axis_index("tensor"), lax.axis_index("dp")
    width = grads[0].shape[-1]
    summed = [
        lax.psum_scatter(
            g[:, :, :BAND].reshape(groups * copies, band, width), AXES, scatter_dimension=0
        ).astype(f32)
        for g in grads
    ]
    vec = lax.psum(grads[0][0, 0, BAND:].astype(f32), AXES)
    shared = lax.dynamic_slice_in_dim(vec[:6], at * band, band, 1)
    cols = lax.dynamic_slice_in_dim(vec[6:10], z, 1, 0)[0]
    ups = lax.dynamic_slice_in_dim(vec[10:14], z, 1, 0).reshape(-1, width // groups)
    split = jnp.stack(
        [
            jnp.concatenate([cols[:128], cols[384:448]]),
            jnp.concatenate([cols[256:384], cols[448:512]]),
        ]
    )
    split = lax.dynamic_slice_in_dim(jnp.concatenate([split, ups]), at * thin, thin, 1)
    sum_qkv, sum_out = unpack_attention(summed[0])
    gradients = (
        sum_qkv,
        sum_out.T,
        summed[1].reshape(masters[2].shape),
        summed[2].T.reshape(masters[3].shape),
        shared,
        split,
    )
    decays = (MATRIX_DECAY, MATRIX_DECAY, MATRIX_DECAY, MATRIX_DECAY, 0.0, 0.0)
    rates = kind_rates()
    outputs = []
    for kind in range(6):
        outputs.extend(
            adamw(masters[kind], firsts[kind], seconds[kind], gradients[kind], rates[kind], decays[kind])
        )
    mixed, grad_inputs = (lax.all_gather(t, "tensor") for t in (mixed, grad_inputs))
    return mixed, grad_inputs, outputs


def local(tokens, cotangent, counts, *state):
    masters = state[0::3]
    if (lax.axis_size("tensor"), lax.axis_size("dp")) == (4, 8):
        turned = tuple(jnp.swapaxes(t, 0, 1) for t in state[:3])
        mixed, low, total = layer(True, tokens, cotangent, counts, turned[:1] + masters[1:])
        *outputs, grad_inputs = step(total, low, turned + state[3:])
        outputs[:4] = [jnp.swapaxes(t, 0, 1) for t in outputs[:4]]
    else:
        mats = gather_plain(masters)
        mixed, grad_inputs, *grads = layer(False, tokens, cotangent, counts, mats)
        mixed, grad_inputs, outputs = step_plain(grads, mixed, grad_inputs, state)
        grad_inputs = grad_inputs.astype(f32)
    return (mixed, grad_inputs, *outputs)


def solution(mesh):
    rows = P("dp", None, None)
    state = (
        P("dp", None, "tensor"),
        P("tensor", "dp"),
        P("dp", None, "tensor"),
        P(None, "tensor", "dp"),
        P(None, "dp"),
        P(None, ("tensor", "dp")),
    )
    in_specs = (rows, rows, P("dp")) + tuple(s for s in state for _ in range(3))
    out_specs = (rows, rows) + tuple(s for s in state for _ in range(4))
    return jax.shard_map(local, mesh=mesh, in_specs=in_specs, out_specs=out_specs, check_vma=False)
```

```python
import functools

import jax
import jax.numpy as jnp
from jax import lax
from jax.experimental import pallas as pl
from jax.experimental.pallas import tpu as pltpu
from jax.sharding import PartitionSpec as P

D = 768
FF = 3072
HEAD_DIM = 64
LEN = 576
STEP = 10


LN_EPS = 1e-05
MASK_FILL = -1e30
BETA_ONE = 0.5
BETA_TWO = 0.5
ADAM_EPS = 1e-08
MATRIX_DECAY = 0.01
SQRT_HALF = 0.7071067811865476
INV_ROOT_TAU = 0.3989422804014327
AXES = ("tensor", "dp")
MESH = pl.DeviceIdType.MESH
bf16, f32 = jnp.bfloat16, jnp.float32
NN = (((1,), (0,)), ((), ()))
NT = (((1,), (1,)), ((), ()))
RT = 192
RL = 96
BAND = 96


def kind_rates():
    return (
        0.7 * D ** (-0.5),
        0.7 * (D * 16 // LEN) ** (-0.5),
        0.7 * D ** (-0.5),
        0.7 * FF ** (-0.5),
        0.6,
        0.4,
    )


def adamw(master, first, second, gradient, step_rate, decay_rate):
    first_new = BETA_ONE * first + (1.0 - BETA_ONE) * gradient
    second_new = BETA_TWO * second + (1.0 - BETA_TWO) * gradient * gradient
    first_hat = first_new / (1.0 - BETA_ONE**STEP)
    second_hat = second_new / (1.0 - BETA_TWO**STEP)
    master_new = master - step_rate * (
        first_hat / (jnp.sqrt(second_hat) + ADAM_EPS) + decay_rate * master
    )
    return (master_new, master_new.astype(jnp.bfloat16), first_new, second_new)


def flip(index, bit):
    return index + bit - 2 * bit * lax.rem(lax.div(index, bit), 2)

def send(src, dst, ssem, rsem, to):
    return pltpu.make_async_remote_copy(
        src_ref=src, dst_ref=dst, send_sem=ssem, recv_sem=rsem, device_id=to, device_id_type=MESH
    )

def arrived(dst, sem):
    pltpu.make_async_copy(dst, dst, sem).wait()

def greet(z, nz, me, others, meanwhile):
    bar = pltpu.get_barrier_semaphore()
    for d in others:
        pl.semaphore_signal(bar, inc=1, device_id=(d, z), device_id_type=MESH)
    @pl.when(z > 0)
    def _():
        pl.semaphore_signal(bar, inc=1, device_id=(me, z - 1), device_id_type=MESH)
    @pl.when(z < nz - 1)
    def _():
        pl.semaphore_signal(bar, inc=1, device_id=(me, z + 1), device_id_type=MESH)
    meanwhile()
    edges = jnp.where(z > 0, 1, 0) + jnp.where(z < nz - 1, 1, 0)
    pl.semaphore_wait(bar, len(others) + edges)


def mm(a, b, dims=NN):
    return lax.dot_general(a, b, dims, preferred_element_type=f32)

def normal_of(rows):
    mean = jnp.mean(rows, axis=-1, keepdims=True)
    centred = rows - mean
    inverse = lax.rsqrt(jnp.mean(centred * centred, axis=-1, keepdims=True) + LN_EPS)
    return centred * inverse, inverse

def normal_back(grad, normal, inverse, gain):
    scaled = grad * gain
    return inverse * (
        scaled
        - jnp.mean(scaled, axis=-1, keepdims=True)
        - normal * jnp.mean(scaled * normal, axis=-1, keepdims=True)
    )

def row_tiles(size):
    return range(0, LEN, size)

def colsum(v):
    return jnp.sum(v, axis=0, keepdims=True)

def pack(own, pad, qkv, out, shared, split):
    band, thin = shared.shape[1], split.shape[1]
    me = lax.axis_index("dp")
    low = [qkv[i].astype(bf16) for i in range(3)]
    ot = out[...].T.astype(bf16)
    pieces = [
        low[0][:, :128], low[1][:, :128], low[2][:, :128],
        jnp.concatenate([low[0][:, 128:], low[2][:, 128:]], axis=1),
        jnp.concatenate([low[1][:, 128:], ot[:, 128:]], axis=1),
        ot[:, :128],
    ]
    for i, piece in enumerate(pieces):
        own[0:band, 128 * i : 128 * i + 128] = piece
    width = D // 4
    pad[...] = jnp.zeros_like(pad)
    pad[0:6, 0:band] = shared[...]
    pad[8:14, 0:thin] = split[...]
    vals = pad[...].astype(bf16)
    src = lax.broadcasted_iota(jnp.int32, (128, D), 0)
    col = lax.broadcasted_iota(jnp.int32, (128, D), 1)

    def placed(spot):
        return mm(vals, jnp.where(col == spot, 1.0, 0.0).astype(bf16))

    at = me * thin + src
    attn = placed(jnp.where(at < 128, at, at + 256))[8:9]
    attn += placed(jnp.where(at < 128, at + 256, at + 320))[9:10]
    ups = sum(placed(f * width + at)[10 + f : 11 + f] for f in range(4))
    rows = [placed(me * band + src)[0:6], attn, ups, jnp.zeros((8, D), f32)]
    own[band : band + 16] = jnp.concatenate(rows, axis=0).astype(bf16)


def pack_rest(own, up, down):
    band = up.shape[0]
    width = D // 4
    for f in range(4):
        own[band + 16 : 2 * band + 16, f * width : (f + 1) * width] = up[:, f].astype(bf16)
        own[2 * band + 16 : 3 * band + 16, f * width : (f + 1) * width] = down[f].T.astype(bf16)


def gather_steps(own, outs, masters_rows, z, me, sems):
    rows_of = masters_rows
    nb, nz = len(rows_of), 4
    lsem, zs, zr, ps, pr, ds, dr, cs, cr = sems
    cp, xp, yp = flip(me, 1), flip(me, 2), flip(me, 4)
    dg = flip(xp, 4)
    pair = (xp, yp)
    starts = [sum(rows_of[:b]) for b in range(nb)]
    half = [[(0, 48), (48, r - 48)] for r in rows_of]

    def own_ref(b):
        return own.at[pl.ds(starts[b], rows_of[b])]
    def right(b, s, src):
        return send(src, outs[b].at[s, me], zs.at[b, 0, z - s], zr.at[b, s], (me, z + 1))
    def left(b, s, src):
        return send(src, outs[b].at[s, me], zs.at[b, 1, s - z], zr.at[b, s], (me, z - 1))
    def side(b, s, src, k):
        return send(src, outs[b].at[s, me], ps.at[b, k, s], pr.at[b, k, s], (pair[k], z))
    def spread(b, s, src):
        for k in range(2):
            side(b, s, src, k).start()
    def diag(b, k):
        lo, n = half[b][k]
        part = outs[b].at[:, pair[k], pl.ds(lo, n)]
        return send(part, part, ds.at[b, k], dr.at[b, k], (pair[1 - k], z))
    def twin(b, j):
        part = outs[b].at[:, (me, xp, yp, dg)[j]]
        return send(part, part, cs.at[b, j], cr.at[b, j], (cp, z))
    def keep(b):
        return pltpu.make_async_copy(own_ref(b), outs[b].at[z, me], lsem.at[b])

    def opens(b):
        @pl.when(z < nz - 1)
        def _():
            right(b, z, own_ref(b)).start()
        @pl.when(z > 0)
        def _():
            left(b, z, own_ref(b)).start()
        spread(b, z, own_ref(b))
        keep(b).start()
    def hop(b, t):
        @pl.when(z >= t)
        def _():
            s = z - t
            arrived(outs[b].at[s, me], zr.at[b, s])
            @pl.when(z < nz - 1)
            def _():
                right(b, s, outs[b].at[s, me]).start()
            spread(b, s, outs[b].at[s, me])
        @pl.when(z + t < nz)
        def _():
            s = z + t
            arrived(outs[b].at[s, me], zr.at[b, s])
            @pl.when(z > 0)
            def _():
                left(b, s, outs[b].at[s, me]).start()
            spread(b, s, outs[b].at[s, me])
    def lined(b):
        keep(b).wait()
        twin(b, 0).start()
    def square(b):
        for k in range(2):
            for s in range(4):
                arrived(outs[b].at[s, pair[k]], pr.at[b, k, s])
            diag(b, k).start()
            twin(b, 1 + k).start()
    def corner(b):
        for k in range(2):
            lo, n = half[b][k]
            arrived(outs[b].at[:, dg, pl.ds(lo, n)], dr.at[b, k])
        twin(b, 3).start()
    def ready(b):
        for j, d in enumerate((cp, flip(xp, 1), flip(yp, 1), flip(dg, 1))):
            arrived(outs[b].at[:, d], cr.at[b, j])
    def sent(b):
        for t in range(4):
            @pl.when((z < nz - 1) & (z >= t))
            def _():
                right(b, z - t, outs[b].at[z - t, me]).wait_send()
            @pl.when((z > 0) & (z + t < nz))
            def _():
                left(b, z + t, outs[b].at[z + t, me]).wait_send()
            for k in range(2):
                side(b, t, outs[b].at[t, me], k).wait_send()
            twin(b, t).wait_send()
        for k in range(2):
            diag(b, k).wait_send()
    return opens, hop, lined, square, corner, ready, sent


def line_steps(block, whole, z, me, sems, rows=pl.ds(0, LEN)):
    nz = 4
    ms, mr, ml = sems

    def along(s, src, way):
        return send(src, whole.at[s, rows], ms.at[(way + 1) // 2, jnp.abs(s - z)], mr.at[s], (me, z + way))
    def keep():
        return pltpu.make_async_copy(block.at[rows], whole.at[z, rows], ml.at[0])
    def opens():
        @pl.when(z < nz - 1)
        def _():
            along(z, block.at[rows], 1).start()
        @pl.when(z > 0)
        def _():
            along(z, block.at[rows], -1).start()
        keep().start()
    def hop(t):
        for way, ok in ((-1, z >= t), (1, z + t < nz)):
            @pl.when(ok)
            def _():
                s = z + way * t
                arrived(whole.at[s, rows], mr.at[s])
                @pl.when((z < nz - 1) if way < 0 else (z > 0))
                def _():
                    along(s, whole.at[s, rows], -way).start()
    def close():
        keep().wait()
        for t in range(4):
            @pl.when((z < nz - 1) & (z >= t))
            def _():
                along(z - t, whole.at[z - t, rows], 1).wait_send()
            @pl.when((z > 0) & (z + t < nz))
            def _():
                along(z + t, whole.at[z + t, rows], -1).wait_send()
    return opens, hop, close


def reduce_steps(own, got_b, landing, rows_of, z, me, sems):
    cs, cr, hs, hr, ss, sr, zs, zr, ds, dr = sems
    nz = 4
    xp, yp = flip(me, 2), flip(me, 4)
    pair = (xp, yp)
    cp = flip(me, 1)
    half = [((0, 48), (48, r - 48)) for r in rows_of]
    everything = slice(None)

    def add(dst, *srcs):
        dst[...] = sum((t[...].astype(f32) for t in srcs), dst[...].astype(f32)).astype(bf16)
    def over_z(body):
        lax.fori_loop(0, nz, lambda g, c: (body(g), c)[1], 0)
    def twin(b, g, src, j):
        return send(src, came(b, j, g), cs.at[b, j, g], cr.at[b, j, g], (cp, z))
    def came(b, j, g):
        return got_b[b - 1].at[j, g] if b else landing(0, 5 + j, g, pl.ds(0, 96))
    def twin_vec(g, j, src):
        return send(src, landing(0, 5 + j, g, pl.ds(96, 16)), ds.at[j, g], dr.at[j, g], (cp, z))
    def merge(b):
        def body(g):
            for j in (3, 1, 2, 0):
                arrived(came(b, j, g), cr.at[b, j, g])
                if b:
                    add(own[b].at[j, g], came(b, j, g))
                else:
                    arrived(landing(0, 5 + j, g, pl.ds(96, 16)), dr.at[j, g])
                    add(own[0].at[j, g], landing(0, 5 + j, g, pl.ds(0, 112)))
        over_z(body)
        for k in range(2):
            corner(b, k).start()
    def corner(b, k):
        part = pl.ds(*half[b][k])
        return send(own[b].at[3, :, part], landing(b, 0, everything, part), hs.at[b, k], hr.at[b, k], (pair[k], z))
    def square(b, k):
        return send(own[b].at[1 + k], landing(b, 1 + k), ss.at[b, k], sr.at[b, k], (pair[k], z))
    def third(b):
        for k in range(2):
            part = pl.ds(*half[b][k])
            arrived(landing(b, 0, everything, part), hr.at[b, k])
            over_z(lambda g: add(own[b].at[2 - k, g, part], landing(b, 0, g, part)))
            square(b, 1 - k).start()
    def fourth(b):
        for k in range(2):
            arrived(landing(b, 1 + k), sr.at[b, k])
        over_z(lambda g: add(own[b].at[0, g], landing(b, 1, g), landing(b, 2, g)))
        along(b, 0)
    def line(b, t, way):
        side = (1 - way) // 2
        return send(own[b].at[0, t], landing(b, 3 + side, t), zs.at[b, t], zr.at[b, side, t], (me, z + way))
    def along(b, i):
        for way, begin in ((1, i), (-1, nz - 1 - i)):
            side = (1 - way) // 2
            targets = range(nz - 1, begin, -1) if way > 0 else range(begin)
            @pl.when(z == begin)
            def _():
                for t in targets:
                    if i:
                        arrived(landing(b, 3 + side, t), zr.at[b, side, t])
                        add(own[b].at[0, t], landing(b, 3 + side, t))
                    line(b, t, way).start()
    def last(b, total, at):
        total[pl.ds(at, rows_of[b])] = own[b][0, z].astype(f32)
        for side, ok in ((0, z > 0), (1, z < nz - 1)):
            @pl.when(ok)
            def _():
                arrived(landing(b, 3 + side, z), zr.at[b, side, z])
                total[pl.ds(at, rows_of[b])] += landing(b, 3 + side, z)[...].astype(f32)
    def closed(b):
        for k in range(2):
            corner(b, k).wait_send()
            square(b, k).wait_send()
        for t in range(nz):
            @pl.when(z < t)
            def _():
                line(b, t, 1).wait_send()
            @pl.when(z > t)
            def _():
                line(b, t, -1).wait_send()
    return twin, twin_vec, merge, third, fourth, along, last, closed


QT = ((0, 256), (256, 256), (512, 64))


def layer_kernel(linked, *refs):
    tokens, cotangent, counts = refs[:3]
    weights_in = refs[3 : 9 if linked else 6]
    refs = refs[9 if linked else 6 :]
    n_out = 3 if linked else 5
    outs, refs = refs[:n_out], refs[n_out:]
    (WA, WB, WC, x, gout_low, first_in, second_in, left_t, right_t, qkv, probs, att,
     middle, acc, hs, stage, bsum, vrow, vecs, bias, mixed, invs, sems) = refs[:23]
    refs = refs[23:]
    gm_low, ig = second_in, first_in
    hidden, slope = hs.at[pl.ds(0, 4)], hs.at[pl.ds(4, 4)]
    z, me = lax.axis_index("tensor"), lax.axis_index("dp")
    band = BAND
    if linked:
        mixed_all, ig_all, total_out = outs
        own, pad = stage, refs[0]
        rows_of = (band + 16, band, band)
        opens, hop, lined, square, corner, ready, sent = gather_steps(
            own, (WA, WB, WC), rows_of, z, me, refs[1:10]
        )
        tail_sems = refs[len(refs) - 18 :]
        pieces = [
            line_steps(block, whole, z, me, tail_sems[3 * (3 * i + c) : 3 * (3 * i + c) + 3], pl.ds(192 * c, 192))
            for i, (block, whole) in enumerate(((mixed, mixed_all), (ig, ig_all)))
            for c in range(3)
        ]
        def mopen():
            for c in range(3):
                pieces[c][0]()
        def mhop(t, c):
            pieces[c][1](t)
        def mclose():
            for c in range(3):
                pieces[c][2]()
        def iopen(c):
            pieces[3 + c][0]()
        def ihop(t, c):
            pieces[3 + c][1](t)
        parts, got_b, freed = refs[10:13], refs[13:15], refs[15]
        def landing(b, i, g=slice(None), part=None):
            if b:
                part = pl.ds(0, band) if part is None else part
                return (WB, WC)[b - 1].at[g, i, part]
            base, spot = (0, 4) if i == 0 else (4, i - 1) if i < 5 else (0, i - 5)
            lo, n = (0, band + 16) if part is None else (part.start, part.size)
            g = pl.ds(base, 4) if isinstance(g, slice) else base + g
            return hs.at[g, pl.ds((band + 16) * spot + lo, n)]
        twin, twin_vec, merge, third, fourth, along, last, closed = reduce_steps(
            parts, got_b, landing, rows_of, z, me, refs[16:26]
        )
        def staged(slot, j):
            return stage.at[pl.ds((4 * slot + j) * band, band)]
        def release():
            for d in (flip(me, 1), flip(me, 2), flip(me, 4)):
                pl.semaphore_signal(freed, inc=1, device_id=(d, z), device_id_type=MESH)
            @pl.when(z > 0)
            def _():
                pl.semaphore_signal(freed, inc=1, device_id=(me, z - 1), device_id_type=MESH)
            @pl.when(z < 3)
            def _():
                pl.semaphore_signal(freed, inc=1, device_id=(me, z + 1), device_id_type=MESH)
        def acquire():
            pl.semaphore_wait(freed, 3 + jnp.where(z > 0, 1, 0) + jnp.where(z < 3, 1, 0))
    else:
        def nothing(*args):
            return None
        opens = hop = lined = square = corner = sent = mhop = nothing
        release = acquire = merge = third = fourth = along = nothing
        mixed_all, ig_out, gA, gB, gC = outs
        def ready(b):
            pltpu.make_async_copy(weights_in[b], (WA, WB, WC)[b], sems.at[8 + b]).wait()
        def mopen():
            pltpu.make_async_copy(mixed, mixed_all, sems.at[11]).start()
        def mclose():
            pltpu.make_async_copy(mixed, mixed_all, sems.at[11]).wait()

    loads = [
        pltpu.make_async_copy(tokens.at[z], x, sems.at[6]),
        pltpu.make_async_copy(cotangent.at[z], gout_low, sems.at[7]),
    ]
    for load in loads:
        load.start()
    if linked:
        greet(z, 4, me, (flip(me, 1), flip(me, 2), flip(me, 4)), lambda: pack(own, pad, *weights_in[:2], *weights_in[4:]))
    else:
        for b in range(3):
            pltpu.make_async_copy(weights_in[b], (WA, WB, WC)[b], sems.at[8 + b]).start()
    count = counts[z]
    column = lax.broadcasted_iota(jnp.int32, (LEN, 1), 0)
    keybias = jnp.where(column < count, 0.0, MASK_FILL)
    def valid(r):
        return jnp.where(lax.broadcasted_iota(jnp.int32, (RL, 1), 0) + r < count, 1.0, 0.0)

    def transpose(dst, src):
        turned = src[...].T
        for d in range(8):
            spot = d
            if linked:
                apart = [lax.rem(lax.div(me, 1 << i) + (d >> i), 2) for i in range(3)]
                spot = 4 * apart[0] + apart[1] + 2 * apart[2]
            dst[pl.ds(pl.multiple_of(spot * band, 32), band)] = turned[d * band : (d + 1) * band]

    opens(0)
    if linked:
        pack_rest(own, *weights_in[2:4])
    for load in loads:
        load.wait()
    for r in row_tiles(RL):
        rs = pl.ds(r, RL)
        gout_low[rs] = (gout_low[rs].astype(f32) * valid(r)).astype(bf16)
        middle[rs] = normal_of(x[rs].astype(f32))[0]
    hop(0, 1)
    hop(0, 2)
    opens(1)
    transpose(right_t, gout_low)
    hop(0, 3)
    lined(0)
    hop(1, 1)
    opens(2)
    square(0)
    hop(1, 2)
    hop(2, 1)
    hop(1, 3)
    lined(1)
    hop(2, 2)
    corner(0)
    hop(2, 3)
    lined(2)
    ready(0)
    lines = [sum(WA[g, i, band : band + 16].astype(f32) for i in range(8)) for g in range(4)]
    vecs[...] = lines[0]
    for g in range(4):
        bias[0, g] = lines[g][6:7]
        bias[1, g] = lines[g][7:8]
    for r in row_tiles(RL):
        rs = pl.ds(r, RL)
        first_in[rs] = (middle[rs] * vecs[0:1] + vecs[1:2]).astype(bf16)
    lane = lax.broadcasted_iota(jnp.int32, (1, 128), 1)
    low = lane < 64
    acc[...] = jnp.zeros_like(acc)

    def at(g, table):
        for i, steps in enumerate(table):
            if steps:
                @pl.when(g == i)
                def _():
                    for step, *args in steps:
                        step(*args)
    def wa(g, lo=0, hi=D):
        return WA[g, :, 0:band, lo:hi].reshape(D, hi - lo)
    def wb(g):
        return WB[g].reshape(D, D)
    def wc(g):
        return WC[g].reshape(D, D)

    def forward(g, carry):
        for r in row_tiles(RT):
            rs = pl.ds(r, RT)
            qkv[g, rs] = (mm(first_in[rs], wa(g)) + bias[0, g]).astype(bf16)
        def tile(i):
            return qkv[g, :, 128 * i : 128 * i + 128]
        outs, scales = [], []
        for h in range(3):
            q, k, v = (tile(0), tile(1), tile(2)) if h < 2 else (tile(3), tile(4), tile(3))
            q = jnp.where(low if h != 1 else ~low, q, 0) * bf16(0.125)
            vt = v.T
            vt = vt[64:] if h else vt[:64]
            cols, tops = [], []
            for r, n in QT:
                s = mm(k, q[r : r + n], NT) + keybias
                e = jnp.exp(s - jnp.max(s, axis=0, keepdims=True))
                inv = 1.0 / jnp.sum(e, axis=0, keepdims=True)
                low_e = e.astype(bf16)
                probs[g, h, :, pl.ds(r, n)] = low_e
                cols.append(mm(vt, low_e) * inv)
                tops.append(inv)
            outs.append(jnp.concatenate(cols, axis=1))
            scales.append(jnp.concatenate(tops, axis=1))
        invs[g] = jnp.concatenate(scales + [jnp.zeros((5, LEN), f32)], axis=0)
        att[g, :, 128:256] = jnp.concatenate(outs[:2], axis=0).T.astype(bf16)
        att[g, :, 0:128] = jnp.concatenate([jnp.zeros_like(outs[2]), outs[2]], axis=0).T.astype(bf16)
        for r in row_tiles(RT):
            rs = pl.ds(r, RT)
            acc[rs] += mm(att[g, rs], wa(g, 512, D), NT)
        at(g, [[(square, 1)], [], [(corner, 1)], [(square, 2)]])
        return carry
    lax.fori_loop(0, 4, forward, 0)

    for r in row_tiles(RL):
        rs = pl.ds(r, RL)
        m = x[rs].astype(f32) + acc[rs] + vecs[2:3]
        middle[rs] = m
        second_in[rs] = (normal_of(m)[0] * vecs[3:4] + vecs[4:5]).astype(bf16)
    transpose(left_t, second_in)
    acc[...] = jnp.zeros_like(acc)
    ready(1)

    def mlp_up(g, carry):
        for r in row_tiles(RT):
            rs = pl.ds(r, RT)
            u = mm(second_in[rs], wb(g)) + bias[1, g]
            phi = 0.5 * (1.0 + lax.erf(u * SQRT_HALF))
            hidden[g, rs] = (u * phi).astype(bf16)
            slope[g, rs] = (phi + u * jnp.exp(-0.5 * u * u) * INV_ROOT_TAU).astype(bf16)
        return carry
    lax.fori_loop(0, 4, mlp_up, 0)
    corner(2)
    ready(2)

    def mlp_down(g, carry):
        for r in row_tiles(RT):
            rs = pl.ds(r, RT)
            acc[rs] += mm(hidden[g, rs], wc(g), NT)
        return carry
    lax.fori_loop(0, 4, mlp_down, 0)
    for r in row_tiles(RL):
        rs = pl.ds(r, RL)
        mixed[rs] = ((middle[rs] + acc[rs] + vecs[5:6]) * valid(r)).astype(bf16)
    mopen()
    acc[...] = jnp.zeros_like(acc)

    def off(dst, g, slot):
        return pltpu.make_async_copy(stage.at[slot], dst.at[g, :, pl.ds(0, band)], sems.at[slot])
    def put(dst, g, slot, part):
        @pl.when(g > 0)
        def _():
            off(dst, g - 1, slot).wait()
        for c in range(0, D, 2 * band):
            stage[slot, pl.ds(c // band, 2)] = part(c).astype(bf16).reshape(2, band, D)
        off(dst, g, slot).start()
    def share_out(b, g, slot, part):
        def sending(gg):
            return [twin(b, gg, staged(slot, j), j) for j in range(4)]
        kept = part(0, 4 * band).astype(bf16)
        for j in range(4):
            parts[b][j, g, pl.ds(0, band)] = kept[j * band : (j + 1) * band]
        @pl.when(g > 0)
        def _():
            for copy in sending(g - 1):
                copy.wait_send()
        stage[pl.ds(4 * slot * band, 4 * band)] = part(4 * band, 4 * band).astype(bf16)
        for copy in sending(g):
            copy.start()
        @pl.when(g == 3)
        def _():
            for copy in sending(g):
                copy.wait_send()
    def give(b, g, slot, part):
        if linked:
            share_out(b, g, slot, part)
        else:
            put((gA, gB, gC)[b], g, slot, lambda c: part(c, 2 * band))

    def mlp_back(g, carry):
        for r in row_tiles(RT):
            rs = pl.ds(r, RT)
            gp = (mm(gout_low[rs], wc(g)) * slope[g, rs].astype(f32)).astype(bf16)
            slope[g, rs] = gp
            acc[rs] += mm(gp, wb(g), NT)
        bsum[1, g] = colsum(slope[g].astype(f32))
        give(2, g, 0, lambda c, n: mm(right_t[pl.ds(c, n)], hidden[g]))
        give(1, g, 1, lambda c, n: mm(left_t[pl.ds(c, n)], slope[g]))
        at(g, [[], [], [(mhop, 1, 0)], [(mhop, 1, 1)]])
        return carry
    for b in range(3):
        sent(b)
    lax.fori_loop(0, 4, mlp_back, 0)
    release()
    if not linked:
        off(gC, 3, 0).wait()
        off(gB, 3, 1).wait()

    sums = [jnp.zeros((1, D), f32) for _ in range(6)]
    for r in row_tiles(RL):
        rs = pl.ds(r, RL)
        n, inv = normal_of(middle[rs])
        gn = acc[rs]
        go = gout_low[rs].astype(f32)
        t = go + normal_back(gn, n, inv, vecs[3:4])
        middle[rs] = t
        gm_low[rs] = t.astype(bf16)
        sums[2] += colsum(t)
        sums[3] += colsum(gn * n)
        sums[4] += colsum(gn)
        sums[5] += colsum(go)
    merged = [(mhop, 1, 2), (acquire,), (merge, 2), (merge, 1), (mhop, 2, 0)]
    for act, *args in merged:
        act(*args)
    transpose(left_t, first_in)
    transpose(right_t, gm_low)
    acc[...] = jnp.zeros_like(acc)

    def backward(g, carry):
        ga = mm(gm_low[...], wa(g, 512, D)).astype(bf16)
        def tile(i):
            return qkv[g, :, 128 * i : 128 * i + 128]
        dq, dk, dv = [], [], []
        scale = invs[g].T
        for h in range(3):
            q, k, v = (tile(0), tile(1), tile(2)) if h < 2 else (tile(3), tile(4), tile(3))
            gt = ga[:, 128:256] if h < 2 else ga[:, 0:128]
            gt = (gt.astype(f32) * scale[:, h : h + 1]).astype(bf16)
            gmask = jnp.where(low if h == 0 else ~low, gt, 0)
            kt = k.T
            kt = kt[64:] if h == 1 else kt[:64]
            dqs, dks, dvs = [], 0.0, 0.0
            for r, n in QT:
                p = probs[g, h, :, pl.ds(r, n)]
                dp = mm(v, gmask[r : r + n], NT)
                pf = p.astype(f32)
                inner = jnp.sum(pf * dp, axis=0, keepdims=True)
                ds = (pf * (dp - inner * invs[g, h : h + 1, pl.ds(r, n)])).astype(bf16)
                dqs.append(mm(kt, ds))
                dks = dks + mm(ds, q[r : r + n])
                dvs = dvs + mm(p, gt[r : r + n])
            dq.append(jnp.concatenate(dqs, axis=1))
            dk.append(dks * 0.125)
            dv.append(dvs)
        dq01 = jnp.concatenate(dq[:2], axis=0).T * 0.125
        dq2 = jnp.concatenate([dq[2], jnp.zeros_like(dq[2])], axis=0).T * 0.125
        parts = [
            dq01,
            jnp.where(low, dk[0], dk[1]),
            jnp.where(low, dv[0], dv[1]),
            jnp.where(low, dq2, dv[2]),
            jnp.where(low, dk[2], 0.0),
        ]
        for i, part in enumerate(parts):
            part = part.astype(bf16)
            qkv[g, :, 128 * i : 128 * i + 128] = part
            bsum[0, g, :, 128 * i : 128 * i + 128] = colsum(part.astype(f32))
        qkv[g, :, 640:768] = jnp.zeros((LEN, 128), bf16)
        bsum[0, g, :, 640:768] = jnp.zeros((1, 128), f32)
        for r in row_tiles(RT):
            rs = pl.ds(r, RT)
            acc[rs] += mm(qkv[g, rs], wa(g), NT)
        at(g, BACK)
        return carry
    BACK = [
        [(third, 2), (mhop, 2, 1)],
        [(mhop, 2, 2), (third, 1)],
        [],
        [],
    ]
    lax.fori_loop(0, 4, backward, 0)

    for r in row_tiles(RL):
        rs = pl.ds(r, RL)
        n, inv = normal_of(x[rs].astype(f32))
        gn = acc[rs]
        first_in[rs] = (middle[rs] + normal_back(gn, n, inv, vecs[0:1])).astype(bf16)
        sums[0] += colsum(gn * n)
        sums[1] += colsum(gn)
    lines = sums + [bsum[i, j] for i in range(2) for j in range(4)] + [jnp.zeros((2, D), f32)]
    lines = jnp.concatenate(lines, axis=0).astype(bf16)
    fourth(2)
    if linked:
        for c in range(3):
            iopen(c)

    def attention_grads(g, carry):
        def part(c, n):
            first = mm(left_t[pl.ds(c, n)], qkv[g])
            second = mm(right_t[pl.ds(c, n)], att[g])
            return jnp.concatenate([first[:, :512], first[:, 512:] + second], axis=1)
        give(0, g, 0, part)
        at(g, [[], [], [(along, 2, 1)], []])
        return carry
    lax.fori_loop(0, 4, attention_grads, 0)
    if linked:
        vrow[0] = lines
        def vec_step(g, act):
            for j in range(4):
                act(twin_vec(g, j, vrow.at[0]))
        for g in range(4):
            vec_step(g, lambda copy: copy.start())
            for j in range(4):
                parts[0][j, g, pl.ds(band, 16)] = lines
        fourth(1)
        merge(0)
        ihop(1, 0)
        third(0)
        ihop(1, 1)
        along(1, 1)
        ihop(1, 2)
        along(2, 2)
        ihop(2, 0)
        fourth(0)
        ihop(2, 1)
        along(1, 2)
        along(0, 1)
        ihop(2, 2)
        last(2, acc, 2 * band + 16)
        along(0, 2)
        last(1, acc, band + 16)
        last(0, acc, 0)
        done = pltpu.make_async_copy(acc.at[pl.ds(0, 3 * band + 16)], total_out, sems.at[1])
        done.start()
        for c in range(3):
            ihop(3, c)
        for g in range(4):
            vec_step(g, lambda copy: copy.wait_send())
        done.wait()
        for c in range(3):
            pieces[3 + c][2]()
        for b in range(3):
            closed(b)
    else:
        for i in range(8):
            vrow[i] = lines
        copies = [pltpu.make_async_copy(ig, ig_out, sems.at[1])]
        copies += [pltpu.make_async_copy(vrow, gA.at[g, :, pl.ds(band, 16)], sems.at[2 + g]) for g in range(4)]
        for copy in copies:
            copy.start()
        for copy in copies:
            copy.wait()
        off(gA, 3, 0).wait()
    for c in range(3):
        mhop(3, c)
    mclose()


def layer(linked, tokens, cotangent, counts, weights, cid=1):
    V, S = pltpu.VMEM, pltpu.SemaphoreType.DMA
    shape = jax.ShapeDtypeStruct
    hb, vm = pl.BlockSpec(memory_space=pl.ANY), pl.BlockSpec(memory_space=V)
    band, nb = BAND, 3
    rows_of = (band + 16, band, band)
    scratch = [V((4, 8, r, D), bf16) for r in rows_of]
    scratch += [V((LEN, D), bf16)] * 4 + [V((D, LEN), bf16)] * 2
    scratch += [V((4, LEN, D), bf16), V((4, 3, LEN, LEN), bf16), V((4, LEN, 256), bf16)]
    scratch += [V((LEN, D), f32)] * 2 + [V((8, LEN, D), bf16), V((8 * band, D) if linked else (2, 8, band, D), bf16)]
    scratch += [V((2, 4, 1, D), f32), V((1 if linked else 8, 16, D), bf16), V((16, D), f32)]
    scratch += [V((2, 4, 1, D), f32), V((LEN, D), bf16), V((4, 8, LEN), f32), S((12,))]
    outs = [shape((LEN, D), bf16)] * 2 + [shape((4, 8, r, D), bf16) for r in rows_of]
    if linked:
        outs = [shape((4, LEN, D), bf16)] * 2 + [shape((sum(rows_of), D), f32)]
        scratch += [V((16, 128), f32)]
        scratch += [S((nb,)), S((nb, 2, 4)), S((nb, 4))]
        scratch += [S((nb, 2, 4))] * 2 + [S((nb, 2))] * 2 + [S((nb, 4))] * 2
        scratch += [V((4, 4, r, D), bf16) for r in rows_of] + [V((4, 4, band, D), bf16)] * 2
        scratch += [pltpu.SemaphoreType.REGULAR] + [S((nb, 4, 4))] * 2 + [S((nb, 2))] * 4
        scratch += [S((nb, 4)), S((nb, 2, 4))] + [S((4, 4))] * 2
        scratch += [S((2, 4)), S((4,)), S((1,))] * 6
    params = dict(collective_id=cid, has_side_effects=True) if linked else {}
    return pl.pallas_call(
        functools.partial(layer_kernel, linked),
        out_shape=outs,
        in_specs=[hb, hb, pl.BlockSpec(memory_space=pltpu.SMEM)] + ([vm] * 6 if linked else [hb] * 3),
        out_specs=[hb] * len(outs),
        scratch_shapes=scratch,
        compiler_params=pltpu.CompilerParams(vmem_limit_bytes=63 * 1024 * 1024, **params),
        cost_estimate=pl.CostEstimate(
            flops=57_000_000_000, bytes_accessed=32_000_000, transcendentals=6_000_000
        ),
    )(tokens, cotangent, counts, *weights)


def step_kernel(total, low, first, *refs):
    ins, outs, full, same, (held, wide, passed, got, put) = refs[:18], refs[18:42], refs[42], refs[43], refs[44:]
    entry = pltpu.make_async_copy(first, passed, got.at[4])
    leave = pltpu.make_async_copy(passed, same, put.at[4])
    fetch = [pltpu.make_async_copy(low.at[s], held.at[s], got.at[s]) for s in range(4)]
    store = [pltpu.make_async_copy(wide.at[s], full.at[s], put.at[s]) for s in range(4)]
    for copy in fetch + [entry]:
        copy.start()
    for s in range(4):
        fetch[s].wait()
        for r in row_tiles(RL):
            wide[s, pl.ds(r, RL)] = held[s, pl.ds(r, RL)].astype(f32)
        store[s].start()
    entry.wait()
    leave.start()
    z, me = lax.axis_index("tensor"), lax.axis_index("dp")
    band, thin = ins[12].shape[1], ins[15].shape[1]
    vec = total[band : band + 16]
    row = lax.broadcasted_iota(jnp.int32, (D, 128), 0)
    col = lax.broadcasted_iota(jnp.int32, (D, 128), 1)

    def pick(source):
        chosen = jnp.where(row == source, 1.0, 0.0)
        return lax.dot_general(
            vec, chosen, NN, precision=lax.Precision.HIGHEST, preferred_element_type=f32
        )

    place = me * thin + col
    shared = pick(me * band + col)[:6, :band]
    head = jnp.where(place < 128, place, place + 256)
    late = jnp.where(place < 128, place + 256, place + 320)
    spots = [head, late] + [f * (D // 4) + place for f in range(4)]
    at = lax.broadcasted_iota(jnp.int32, (16, 128), 0)
    lines = []
    for i, spot in enumerate(spots):
        mine = jnp.where(at == z + (6 if i < 2 else 10), pick(spot), 0.0)
        lines.append(jnp.sum(mine, axis=0, keepdims=True)[:, :thin])
    split = jnp.concatenate(lines, axis=0)

    def apply(kind, where, gradient):
        rates, decays = kind_rates(), (MATRIX_DECAY,) * 4 + (0.0, 0.0)
        m, f, s = (ins[3 * kind + i][where] for i in range(3))
        results = adamw(m, f, s, gradient, rates[kind], decays[kind])
        for i in range(4):
            outs[4 * kind + i][where] = results[i]

    attn = total[:band]
    def pair(a, b):
        return jnp.concatenate([attn[:, a : a + 128], attn[:, b : b + 64]], axis=1)
    apply(0, (0,), pair(0, 384))
    apply(0, (1,), pair(128, 512))
    apply(0, (2,), pair(256, 448))
    apply(1, (slice(None),), pair(640, 576).T)
    up = total[band + 16 : 2 * band + 16]
    down = total[2 * band + 16 :]
    down = down.T
    width = D // 4
    for f in range(4):
        apply(2, (slice(None), f), up[:, f * width : (f + 1) * width])
        apply(3, (f,), down[f * width : (f + 1) * width])
    apply(4, (slice(None),), shared)
    apply(5, (slice(None),), split)
    for copy in store + [leave]:
        copy.wait()


def step(total, low, first, state):
    V, S = pltpu.VMEM, pltpu.SemaphoreType.DMA
    vm, hb = pl.BlockSpec(memory_space=V), pl.BlockSpec(memory_space=pl.ANY)
    shapes = []
    for kind in range(6):
        shape = state[3 * kind].shape
        shapes += [jax.ShapeDtypeStruct(shape, t) for t in (f32, bf16, f32, f32)]
    shapes += [jax.ShapeDtypeStruct(low.shape, t) for t in (f32, bf16)]
    return pl.pallas_call(
        step_kernel,
        out_shape=shapes,
        in_specs=[vm, hb, hb] + [vm] * 18,
        out_specs=[vm] * 24 + [hb] * 2,
        scratch_shapes=[V(low.shape, bf16), V(low.shape, f32), V(low.shape, bf16), S((5,)), S((5,))],
        compiler_params=pltpu.CompilerParams(vmem_limit_bytes=56 * 1024 * 1024),
    )(total, low, first, *state)


def pack_attention(qkv, out):
    q, k, v = qkv[:, 0], qkv[:, 1], qkv[:, 2]
    return jnp.concatenate(
        [
            q[:, :128], k[:, :128], v[:, :128],
            q[:, 128:], v[:, 128:], k[:, 128:], out[:, 128:], out[:, :128],
        ],
        axis=1,
    )


def unpack_attention(block):
    pair = [block[:, 128 * i : 128 * i + 128] for i in range(6)]
    q = jnp.concatenate([pair[0], pair[3][:, :64]], axis=1)
    k = jnp.concatenate([pair[1], pair[4][:, :64]], axis=1)
    v = jnp.concatenate([pair[2], pair[3][:, 64:]], axis=1)
    o = jnp.concatenate([pair[5], pair[4][:, 64:]], axis=1)
    return jnp.stack([q, k, v], axis=1), o


def gather_plain(masters):
    qkv, out, up, down, shared, split = (t.astype(bf16) for t in masters)
    band, thin, width = shared.shape[1], split.shape[1], down.shape[1] * lax.axis_size("tensor")
    groups = lax.axis_size("tensor")
    own = jnp.stack(
        [pack_attention(qkv, out.T), up.reshape(band, -1), down.reshape(-1, band).T]
    )
    mats = lax.all_gather(own, AXES, axis=1, tiled=True).reshape(3, groups, 8, BAND, width)
    shared = lax.all_gather(shared, "dp", axis=1, tiled=True)
    split = lax.all_gather(split, AXES, axis=1, tiled=True).reshape(-1, groups, width // groups)
    bq, bv = split[0], split[1]
    zero = jnp.zeros((groups, 128), bf16)
    attn_bias = [bq[:, :128], zero, bv[:, :128], bq[:, 128:], bv[:, 128:], zero, zero]
    lines = [
        jnp.broadcast_to(shared, (groups, 6, width)),
        jnp.concatenate(attn_bias, axis=1)[:, None],
        jnp.swapaxes(split[2:], 0, 1).reshape(groups, 1, width),
    ]
    lines = jnp.pad(jnp.concatenate(lines, axis=1)[:, None], ((0, 0), (0, 7), (0, 8), (0, 0)))
    return jnp.concatenate([mats[0], lines], axis=2), mats[1], mats[2]


def step_plain(grads, mixed, grad_inputs, state):
    masters, firsts, seconds = state[0::3], state[1::3], state[2::3]
    band, thin = masters[4].shape[1], masters[5].shape[1]
    groups, copies = lax.axis_size("tensor"), lax.axis_size("dp")
    z, at = lax.axis_index("tensor"), lax.axis_index("dp")
    width = grads[0].shape[-1]
    summed = [
        lax.psum_scatter(
            g[:, :, :BAND].reshape(groups * copies, band, width), AXES, scatter_dimension=0
        ).astype(f32)
        for g in grads
    ]
    vec = lax.psum(grads[0][0, 0, BAND:].astype(f32), AXES)
    shared = lax.dynamic_slice_in_dim(vec[:6], at * band, band, 1)
    cols = lax.dynamic_slice_in_dim(vec[6:10], z, 1, 0)[0]
    ups = lax.dynamic_slice_in_dim(vec[10:14], z, 1, 0).reshape(-1, width // groups)
    split = jnp.stack(
        [
            jnp.concatenate([cols[:128], cols[384:448]]),
            jnp.concatenate([cols[256:384], cols[448:512]]),
        ]
    )
    split = lax.dynamic_slice_in_dim(jnp.concatenate([split, ups]), at * thin, thin, 1)
    sum_qkv, sum_out = unpack_attention(summed[0])
    gradients = (
        sum_qkv,
        sum_out.T,
        summed[1].reshape(masters[2].shape),
        summed[2].T.reshape(masters[3].shape),
        shared,
        split,
    )
    decays = (MATRIX_DECAY, MATRIX_DECAY, MATRIX_DECAY, MATRIX_DECAY, 0.0, 0.0)
    rates = kind_rates()
    outputs = []
    for kind in range(6):
        outputs.extend(
            adamw(masters[kind], firsts[kind], seconds[kind], gradients[kind], rates[kind], decays[kind])
        )
    mixed, grad_inputs = (lax.all_gather(t, "tensor") for t in (mixed, grad_inputs))
    return mixed, grad_inputs, outputs


def local(tokens, cotangent, counts, *state):
    masters = state[0::3]
    if (lax.axis_size("tensor"), lax.axis_size("dp")) == (4, 8):
        turned = tuple(jnp.swapaxes(t, 0, 1) for t in state[:3])
        mixed, low, total = layer(True, tokens, cotangent, counts, turned[:1] + masters[1:])
        *outputs, grad_inputs, mixed = step(total, low, mixed, turned + state[3:])
        outputs[:4] = [jnp.swapaxes(t, 0, 1) for t in outputs[:4]]
    else:
        mats = gather_plain(masters)
        mixed, grad_inputs, *grads = layer(False, tokens, cotangent, counts, mats)
        mixed, grad_inputs, outputs = step_plain(grads, mixed, grad_inputs, state)
        grad_inputs = grad_inputs.astype(f32)
    return (mixed, grad_inputs, *outputs)


def solution(mesh):
    rows = P("dp", None, None)
    state = (
        P("dp", None, "tensor"),
        P("tensor", "dp"),
        P("dp", None, "tensor"),
        P(None, "tensor", "dp"),
        P(None, "dp"),
        P(None, ("tensor", "dp")),
    )
    in_specs = (rows, rows, P("dp")) + tuple(s for s in state for _ in range(3))
    out_specs = (rows, rows) + tuple(s for s in state for _ in range(4))
    return jax.shard_map(local, mesh=mesh, in_specs=in_specs, out_specs=out_specs, check_vma=False)
```

```python
import functools

import jax
import jax.numpy as jnp
from jax import lax
from jax.experimental import pallas as pl
from jax.experimental.pallas import tpu as pltpu
from jax.sharding import PartitionSpec as P

D = 768
FF = 3072
HEAD_DIM = 64
LEN = 576
STEP = 10


LN_EPS = 1e-05
MASK_FILL = -1e30
BETA_ONE = 0.5
BETA_TWO = 0.5
ADAM_EPS = 1e-08
MATRIX_DECAY = 0.01
SQRT_HALF = 0.7071067811865476
INV_ROOT_TAU = 0.3989422804014327
AXES = ("tensor", "dp")
MESH = pl.DeviceIdType.MESH
bf16, f32 = jnp.bfloat16, jnp.float32
NN = (((1,), (0,)), ((), ()))
NT = (((1,), (1,)), ((), ()))
RT = 192
RL = 96
BAND = 96


def kind_rates():
    return (
        0.7 * D ** (-0.5),
        0.7 * (D * 16 // LEN) ** (-0.5),
        0.7 * D ** (-0.5),
        0.7 * FF ** (-0.5),
        0.6,
        0.4,
    )


def adamw(master, first, second, gradient, step_rate, decay_rate):
    first_new = BETA_ONE * first + (1.0 - BETA_ONE) * gradient
    second_new = BETA_TWO * second + (1.0 - BETA_TWO) * gradient * gradient
    first_hat = first_new / (1.0 - BETA_ONE**STEP)
    second_hat = second_new / (1.0 - BETA_TWO**STEP)
    master_new = master - step_rate * (
        first_hat / (jnp.sqrt(second_hat) + ADAM_EPS) + decay_rate * master
    )
    return (master_new, master_new.astype(jnp.bfloat16), first_new, second_new)


def flip(index, bit):
    return index + bit - 2 * bit * lax.rem(lax.div(index, bit), 2)

def send(src, dst, ssem, rsem, to):
    return pltpu.make_async_remote_copy(
        src_ref=src, dst_ref=dst, send_sem=ssem, recv_sem=rsem, device_id=to, device_id_type=MESH
    )

def arrived(dst, sem):
    pltpu.make_async_copy(dst, dst, sem).wait()

def greet(z, nz, me, others, meanwhile):
    bar = pltpu.get_barrier_semaphore()
    for d in others:
        pl.semaphore_signal(bar, inc=1, device_id=(d, z), device_id_type=MESH)
    @pl.when(z > 0)
    def _():
        pl.semaphore_signal(bar, inc=1, device_id=(me, z - 1), device_id_type=MESH)
    @pl.when(z < nz - 1)
    def _():
        pl.semaphore_signal(bar, inc=1, device_id=(me, z + 1), device_id_type=MESH)
    meanwhile()
    edges = jnp.where(z > 0, 1, 0) + jnp.where(z < nz - 1, 1, 0)
    pl.semaphore_wait(bar, len(others) + edges)


def mm(a, b, dims=NN):
    return lax.dot_general(a, b, dims, preferred_element_type=f32)

def normal_of(rows):
    mean = jnp.mean(rows, axis=-1, keepdims=True)
    centred = rows - mean
    inverse = lax.rsqrt(jnp.mean(centred * centred, axis=-1, keepdims=True) + LN_EPS)
    return centred * inverse, inverse

def normal_back(grad, normal, inverse, gain):
    scaled = grad * gain
    return inverse * (
        scaled
        - jnp.mean(scaled, axis=-1, keepdims=True)
        - normal * jnp.mean(scaled * normal, axis=-1, keepdims=True)
    )

def row_tiles(size):
    return range(0, LEN, size)

def colsum(v):
    return jnp.sum(v, axis=0, keepdims=True)

def pack(own, pad, qkv, out, shared, split):
    band, thin = shared.shape[1], split.shape[1]
    me = lax.axis_index("dp")
    low = [qkv[i].astype(bf16) for i in range(3)]
    ot = out[...].T.astype(bf16)
    pieces = [
        low[0][:, :128], low[1][:, :128], low[2][:, :128],
        jnp.concatenate([low[0][:, 128:], low[2][:, 128:]], axis=1),
        jnp.concatenate([low[1][:, 128:], ot[:, 128:]], axis=1),
        ot[:, :128],
    ]
    for i, piece in enumerate(pieces):
        own[0:band, 128 * i : 128 * i + 128] = piece
    width = D // 4
    pad[...] = jnp.zeros_like(pad)
    pad[0:6, 0:band] = shared[...]
    pad[8:14, 0:thin] = split[...]
    vals = pad[...].astype(bf16)
    src = lax.broadcasted_iota(jnp.int32, (128, D), 0)
    col = lax.broadcasted_iota(jnp.int32, (128, D), 1)

    def placed(spot):
        return mm(vals, jnp.where(col == spot, 1.0, 0.0).astype(bf16))

    at = me * thin + src
    attn = placed(jnp.where(at < 128, at, at + 256))[8:9]
    attn += placed(jnp.where(at < 128, at + 256, at + 320))[9:10]
    ups = sum(placed(f * width + at)[10 + f : 11 + f] for f in range(4))
    rows = [placed(me * band + src)[0:6], attn, ups, jnp.zeros((8, D), f32)]
    own[band : band + 16] = jnp.concatenate(rows, axis=0).astype(bf16)


def pack_rest(own, up, down):
    band = up.shape[0]
    width = D // 4
    for f in range(4):
        own[band + 16 : 2 * band + 16, f * width : (f + 1) * width] = up[:, f].astype(bf16)
        own[2 * band + 16 : 3 * band + 16, f * width : (f + 1) * width] = down[f].T.astype(bf16)


def gather_steps(own, outs, masters_rows, z, me, sems):
    rows_of = masters_rows
    nb, nz = len(rows_of), 4
    lsem, zs, zr, ps, pr, ds, dr, cs, cr = sems
    cp, xp, yp = flip(me, 1), flip(me, 2), flip(me, 4)
    dg = flip(xp, 4)
    pair = (xp, yp)
    starts = [sum(rows_of[:b]) for b in range(nb)]
    half = [[(0, 48), (48, r - 48)] for r in rows_of]

    def own_ref(b):
        return own.at[pl.ds(starts[b], rows_of[b])]
    def right(b, s, src):
        return send(src, outs[b].at[s, me], zs.at[b, 0, z - s], zr.at[b, s], (me, z + 1))
    def left(b, s, src):
        return send(src, outs[b].at[s, me], zs.at[b, 1, s - z], zr.at[b, s], (me, z - 1))
    def side(b, s, src, k):
        return send(src, outs[b].at[s, me], ps.at[b, k, s], pr.at[b, k, s], (pair[k], z))
    def spread(b, s, src):
        for k in range(2):
            side(b, s, src, k).start()
    def diag(b, k):
        lo, n = half[b][k]
        part = outs[b].at[:, pair[k], pl.ds(lo, n)]
        return send(part, part, ds.at[b, k], dr.at[b, k], (pair[1 - k], z))
    def twin(b, j):
        part = outs[b].at[:, (me, xp, yp, dg)[j]]
        return send(part, part, cs.at[b, j], cr.at[b, j], (cp, z))
    def keep(b):
        return pltpu.make_async_copy(own_ref(b), outs[b].at[z, me], lsem.at[b])

    def opens(b):
        @pl.when(z < nz - 1)
        def _():
            right(b, z, own_ref(b)).start()
        @pl.when(z > 0)
        def _():
            left(b, z, own_ref(b)).start()
        spread(b, z, own_ref(b))
        keep(b).start()
    def hop(b, t):
        @pl.when(z >= t)
        def _():
            s = z - t
            arrived(outs[b].at[s, me], zr.at[b, s])
            @pl.when(z < nz - 1)
            def _():
                right(b, s, outs[b].at[s, me]).start()
            spread(b, s, outs[b].at[s, me])
        @pl.when(z + t < nz)
        def _():
            s = z + t
            arrived(outs[b].at[s, me], zr.at[b, s])
            @pl.when(z > 0)
            def _():
                left(b, s, outs[b].at[s, me]).start()
            spread(b, s, outs[b].at[s, me])
    def lined(b):
        keep(b).wait()
        twin(b, 0).start()
    def square(b):
        for k in range(2):
            for s in range(4):
                arrived(outs[b].at[s, pair[k]], pr.at[b, k, s])
            diag(b, k).start()
            twin(b, 1 + k).start()
    def corner(b):
        for k in range(2):
            lo, n = half[b][k]
            arrived(outs[b].at[:, dg, pl.ds(lo, n)], dr.at[b, k])
        twin(b, 3).start()
    def ready(b):
        for j, d in enumerate((cp, flip(xp, 1), flip(yp, 1), flip(dg, 1))):
            arrived(outs[b].at[:, d], cr.at[b, j])
    def sent(b):
        for t in range(4):
            @pl.when((z < nz - 1) & (z >= t))
            def _():
                right(b, z - t, outs[b].at[z - t, me]).wait_send()
            @pl.when((z > 0) & (z + t < nz))
            def _():
                left(b, z + t, outs[b].at[z + t, me]).wait_send()
            for k in range(2):
                side(b, t, outs[b].at[t, me], k).wait_send()
            twin(b, t).wait_send()
        for k in range(2):
            diag(b, k).wait_send()
    return opens, hop, lined, square, corner, ready, sent


def line_steps(block, whole, z, me, sems, rows=pl.ds(0, LEN)):
    nz = 4
    ms, mr, ml = sems

    def along(s, src, way):
        return send(src, whole.at[s, rows], ms.at[(way + 1) // 2, jnp.abs(s - z)], mr.at[s], (me, z + way))
    def keep():
        return pltpu.make_async_copy(block.at[rows], whole.at[z, rows], ml.at[0])
    def opens():
        @pl.when(z < nz - 1)
        def _():
            along(z, block.at[rows], 1).start()
        @pl.when(z > 0)
        def _():
            along(z, block.at[rows], -1).start()
        keep().start()
    def hop(t):
        for way, ok in ((-1, z >= t), (1, z + t < nz)):
            @pl.when(ok)
            def _():
                s = z + way * t
                arrived(whole.at[s, rows], mr.at[s])
                @pl.when((z < nz - 1) if way < 0 else (z > 0))
                def _():
                    along(s, whole.at[s, rows], -way).start()
    def close():
        keep().wait()
        for t in range(4):
            @pl.when((z < nz - 1) & (z >= t))
            def _():
                along(z - t, whole.at[z - t, rows], 1).wait_send()
            @pl.when((z > 0) & (z + t < nz))
            def _():
                along(z + t, whole.at[z + t, rows], -1).wait_send()
    return opens, hop, close


def reduce_steps(own, got_b, landing, rows_of, z, me, sems):
    cs, cr, hs, hr, ss, sr, zs, zr, ds, dr = sems
    nz = 4
    xp, yp = flip(me, 2), flip(me, 4)
    pair = (xp, yp)
    cp = flip(me, 1)
    half = [((0, 48), (48, r - 48)) for r in rows_of]
    everything = slice(None)

    def add(dst, *srcs):
        dst[...] = sum((t[...].astype(f32) for t in srcs), dst[...].astype(f32)).astype(bf16)
    def over_z(body):
        lax.fori_loop(0, nz, lambda g, c: (body(g), c)[1], 0)
    def twin(b, g, src, j):
        return send(src, came(b, j, g), cs.at[b, j, g], cr.at[b, j, g], (cp, z))
    def came(b, j, g):
        return got_b[b - 1].at[j, g] if b else landing(0, 5 + j, g, pl.ds(0, 96))
    def twin_vec(g, j, src):
        return send(src, landing(0, 5 + j, g, pl.ds(96, 16)), ds.at[j, g], dr.at[j, g], (cp, z))
    def merge(b):
        def body(g):
            for j in (3, 1, 2, 0):
                arrived(came(b, j, g), cr.at[b, j, g])
                if b:
                    add(own[b].at[j, g], came(b, j, g))
                else:
                    arrived(landing(0, 5 + j, g, pl.ds(96, 16)), dr.at[j, g])
                    add(own[0].at[j, g], landing(0, 5 + j, g, pl.ds(0, 112)))
        over_z(body)
        for k in range(2):
            corner(b, k).start()
    def corner(b, k):
        part = pl.ds(*half[b][k])
        return send(own[b].at[3, :, part], landing(b, 0, everything, part), hs.at[b, k], hr.at[b, k], (pair[k], z))
    def square(b, k):
        return send(own[b].at[1 + k], landing(b, 1 + k), ss.at[b, k], sr.at[b, k], (pair[k], z))
    def third(b):
        for k in range(2):
            part = pl.ds(*half[b][k])
            arrived(landing(b, 0, everything, part), hr.at[b, k])
            over_z(lambda g: add(own[b].at[2 - k, g, part], landing(b, 0, g, part)))
            square(b, 1 - k).start()
    def fourth(b):
        for k in range(2):
            arrived(landing(b, 1 + k), sr.at[b, k])
        over_z(lambda g: add(own[b].at[0, g], landing(b, 1, g), landing(b, 2, g)))
        along(b, 0)
    def line(b, t, way):
        side = (1 - way) // 2
        return send(own[b].at[0, t], landing(b, 3 + side, t), zs.at[b, t], zr.at[b, side, t], (me, z + way))
    def along(b, i):
        for way, begin in ((1, i), (-1, nz - 1 - i)):
            side = (1 - way) // 2
            targets = range(nz - 1, begin, -1) if way > 0 else range(begin)
            @pl.when(z == begin)
            def _():
                for t in targets:
                    if i:
                        arrived(landing(b, 3 + side, t), zr.at[b, side, t])
                        add(own[b].at[0, t], landing(b, 3 + side, t))
                    line(b, t, way).start()
    def last(b, total, at):
        total[pl.ds(at, rows_of[b])] = own[b][0, z].astype(f32)
        for side, ok in ((0, z > 0), (1, z < nz - 1)):
            @pl.when(ok)
            def _():
                arrived(landing(b, 3 + side, z), zr.at[b, side, z])
                total[pl.ds(at, rows_of[b])] += landing(b, 3 + side, z)[...].astype(f32)
    def closed(b):
        for k in range(2):
            corner(b, k).wait_send()
            square(b, k).wait_send()
        for t in range(nz):
            @pl.when(z < t)
            def _():
                line(b, t, 1).wait_send()
            @pl.when(z > t)
            def _():
                line(b, t, -1).wait_send()
    return twin, twin_vec, merge, third, fourth, along, last, closed


QT = ((0, 256), (256, 256), (512, 64))


def layer_kernel(linked, *refs):
    tokens, cotangent, counts = refs[:3]
    weights_in = refs[3 : 9 if linked else 6]
    refs = refs[9 if linked else 6 :]
    n_out = 3 if linked else 5
    outs, refs = refs[:n_out], refs[n_out:]
    (WA, WB, WC, x, gout_low, first_in, second_in, left_t, right_t, qkv, probs, att,
     middle, acc, hs, stage, bsum, vrow, vecs, bias, mixed, invs, sems) = refs[:23]
    refs = refs[23:]
    gm_low, ig = second_in, first_in
    hidden, slope = hs.at[pl.ds(0, 4)], hs.at[pl.ds(4, 4)]
    z, me = lax.axis_index("tensor"), lax.axis_index("dp")
    band = BAND
    if linked:
        mixed_all, ig_all, total_out = outs
        own, pad = stage, refs[0]
        rows_of = (band + 16, band, band)
        opens, hop, lined, square, corner, ready, sent = gather_steps(
            own, (WA, WB, WC), rows_of, z, me, refs[1:10]
        )
        tail_sems = refs[len(refs) - 18 :]
        pieces = [
            line_steps(block, whole, z, me, tail_sems[3 * (3 * i + c) : 3 * (3 * i + c) + 3], pl.ds(192 * c, 192))
            for i, (block, whole) in enumerate(((mixed, mixed_all), (ig, ig_all)))
            for c in range(3)
        ]
        def mopen():
            for c in range(3):
                pieces[c][0]()
        def mhop(t, c):
            pieces[c][1](t)
        def mclose():
            for c in range(3):
                pieces[c][2]()
        def iopen(c):
            pieces[3 + c][0]()
        def ihop(t, c):
            pieces[3 + c][1](t)
        parts, got_b, freed = refs[10:13], refs[13:15], refs[15]
        def landing(b, i, g=slice(None), part=None):
            if b:
                part = pl.ds(0, band) if part is None else part
                return (WB, WC)[b - 1].at[g, i, part]
            base, spot = (0, 4) if i == 0 else (4, i - 1) if i < 5 else (0, i - 5)
            lo, n = (0, band + 16) if part is None else (part.start, part.size)
            g = pl.ds(base, 4) if isinstance(g, slice) else base + g
            return hs.at[g, pl.ds((band + 16) * spot + lo, n)]
        twin, twin_vec, merge, third, fourth, along, last, closed = reduce_steps(
            parts, got_b, landing, rows_of, z, me, refs[16:26]
        )
        def staged(slot, j):
            return stage.at[pl.ds((4 * slot + j) * band, band)]
        def release():
            for d in (flip(me, 1), flip(me, 2), flip(me, 4)):
                pl.semaphore_signal(freed, inc=1, device_id=(d, z), device_id_type=MESH)
            @pl.when(z > 0)
            def _():
                pl.semaphore_signal(freed, inc=1, device_id=(me, z - 1), device_id_type=MESH)
            @pl.when(z < 3)
            def _():
                pl.semaphore_signal(freed, inc=1, device_id=(me, z + 1), device_id_type=MESH)
        def acquire():
            pl.semaphore_wait(freed, 3 + jnp.where(z > 0, 1, 0) + jnp.where(z < 3, 1, 0))
    else:
        def nothing(*args):
            return None
        opens = hop = lined = square = corner = sent = mhop = nothing
        release = acquire = merge = third = fourth = along = nothing
        mixed_all, ig_out, gA, gB, gC = outs
        def ready(b):
            pltpu.make_async_copy(weights_in[b], (WA, WB, WC)[b], sems.at[8 + b]).wait()
        def mopen():
            pltpu.make_async_copy(mixed, mixed_all, sems.at[11]).start()
        def mclose():
            pltpu.make_async_copy(mixed, mixed_all, sems.at[11]).wait()

    loads = [
        pltpu.make_async_copy(tokens.at[z], x, sems.at[6]),
        pltpu.make_async_copy(cotangent.at[z], gout_low, sems.at[7]),
    ]
    for load in loads:
        load.start()
    if linked:
        greet(z, 4, me, (flip(me, 1), flip(me, 2), flip(me, 4)), lambda: pack(own, pad, *weights_in[:2], *weights_in[4:]))
    else:
        for b in range(3):
            pltpu.make_async_copy(weights_in[b], (WA, WB, WC)[b], sems.at[8 + b]).start()
    count = counts[z]
    column = lax.broadcasted_iota(jnp.int32, (LEN, 1), 0)
    keybias = jnp.where(column < count, 0.0, MASK_FILL)
    def valid(r):
        return jnp.where(lax.broadcasted_iota(jnp.int32, (RL, 1), 0) + r < count, 1.0, 0.0)

    def transpose(dst, src):
        turned = src[...].T
        for d in range(8):
            spot = d
            if linked:
                apart = [lax.rem(lax.div(me, 1 << i) + (d >> i), 2) for i in range(3)]
                spot = 4 * apart[0] + apart[1] + 2 * apart[2]
            dst[pl.ds(pl.multiple_of(spot * band, 32), band)] = turned[d * band : (d + 1) * band]

    opens(0)
    if linked:
        pack_rest(own, *weights_in[2:4])
    for load in loads:
        load.wait()
    for r in row_tiles(RL):
        rs = pl.ds(r, RL)
        gout_low[rs] = (gout_low[rs].astype(f32) * valid(r)).astype(bf16)
        middle[rs] = normal_of(x[rs].astype(f32))[0]
    hop(0, 1)
    hop(0, 2)
    opens(1)
    transpose(right_t, gout_low)
    hop(0, 3)
    lined(0)
    hop(1, 1)
    opens(2)
    square(0)
    hop(1, 2)
    hop(2, 1)
    hop(1, 3)
    lined(1)
    hop(2, 2)
    corner(0)
    hop(2, 3)
    lined(2)
    ready(0)
    lines = [sum(WA[g, i, band : band + 16].astype(f32) for i in range(8)) for g in range(4)]
    vecs[...] = lines[0]
    for g in range(4):
        bias[0, g] = lines[g][6:7]
        bias[1, g] = lines[g][7:8]
    for r in row_tiles(RL):
        rs = pl.ds(r, RL)
        first_in[rs] = (middle[rs] * vecs[0:1] + vecs[1:2]).astype(bf16)
    lane = lax.broadcasted_iota(jnp.int32, (1, 128), 1)
    low = lane < 64
    acc[...] = jnp.zeros_like(acc)

    def at(g, table):
        for i, steps in enumerate(table):
            if steps:
                @pl.when(g == i)
                def _():
                    for step, *args in steps:
                        step(*args)
    def wa(g, lo=0, hi=D):
        return WA[g, :, 0:band, lo:hi].reshape(D, hi - lo)
    def wb(g):
        return WB[g].reshape(D, D)
    def wc(g):
        return WC[g].reshape(D, D)

    def forward(g, carry):
        for r in row_tiles(RT):
            rs = pl.ds(r, RT)
            qkv[g, rs] = (mm(first_in[rs], wa(g)) + bias[0, g]).astype(bf16)
        def tile(i):
            return qkv[g, :, 128 * i : 128 * i + 128]
        outs, scales = [], []
        for h in range(3):
            q, k, v = (tile(0), tile(1), tile(2)) if h < 2 else (tile(3), tile(4), tile(3))
            q = jnp.where(low if h != 1 else ~low, q, 0) * bf16(0.125)
            vt = v.T
            vt = vt[64:] if h else vt[:64]
            cols, tops = [], []
            for r, n in QT:
                s = mm(k, q[r : r + n], NT) + keybias
                e = jnp.exp(s - jnp.max(s, axis=0, keepdims=True))
                inv = 1.0 / jnp.sum(e, axis=0, keepdims=True)
                low_e = e.astype(bf16)
                probs[g, h, :, pl.ds(r, n)] = low_e
                cols.append(mm(vt, low_e) * inv)
                tops.append(inv)
            outs.append(jnp.concatenate(cols, axis=1))
            scales.append(jnp.concatenate(tops, axis=1))
        invs[g] = jnp.concatenate(scales + [jnp.zeros((5, LEN), f32)], axis=0)
        att[g, :, 128:256] = jnp.concatenate(outs[:2], axis=0).T.astype(bf16)
        att[g, :, 0:128] = jnp.concatenate([jnp.zeros_like(outs[2]), outs[2]], axis=0).T.astype(bf16)
        for r in row_tiles(RT):
            rs = pl.ds(r, RT)
            acc[rs] += mm(att[g, rs], wa(g, 512, D), NT)
        at(g, [[(square, 1)], [], [(corner, 1)], [(square, 2)]])
        return carry
    lax.fori_loop(0, 4, forward, 0)

    for r in row_tiles(RL):
        rs = pl.ds(r, RL)
        m = x[rs].astype(f32) + acc[rs] + vecs[2:3]
        middle[rs] = m
        second_in[rs] = (normal_of(m)[0] * vecs[3:4] + vecs[4:5]).astype(bf16)
    transpose(left_t, second_in)
    acc[...] = jnp.zeros_like(acc)
    ready(1)

    def mlp_up(g, carry):
        for r in row_tiles(RT):
            rs = pl.ds(r, RT)
            u = mm(second_in[rs], wb(g)) + bias[1, g]
            phi = 0.5 * (1.0 + lax.erf(u * SQRT_HALF))
            hidden[g, rs] = (u * phi).astype(bf16)
            slope[g, rs] = (phi + u * jnp.exp(-0.5 * u * u) * INV_ROOT_TAU).astype(bf16)
        return carry
    lax.fori_loop(0, 4, mlp_up, 0)
    corner(2)
    ready(2)

    def mlp_down(g, carry):
        for r in row_tiles(RT):
            rs = pl.ds(r, RT)
            acc[rs] += mm(hidden[g, rs], wc(g), NT)
        return carry
    lax.fori_loop(0, 4, mlp_down, 0)
    for r in row_tiles(RL):
        rs = pl.ds(r, RL)
        mixed[rs] = ((middle[rs] + acc[rs] + vecs[5:6]) * valid(r)).astype(bf16)
    mopen()
    acc[...] = jnp.zeros_like(acc)

    def off(dst, g, slot):
        return pltpu.make_async_copy(stage.at[slot], dst.at[g, :, pl.ds(0, band)], sems.at[slot])
    def put(dst, g, slot, part):
        @pl.when(g > 0)
        def _():
            off(dst, g - 1, slot).wait()
        for c in range(0, D, 2 * band):
            stage[slot, pl.ds(c // band, 2)] = part(c).astype(bf16).reshape(2, band, D)
        off(dst, g, slot).start()
    def share_out(b, g, slot, part):
        def sending(gg):
            return [twin(b, gg, staged(slot, j), j) for j in range(4)]
        kept = part(0, 4 * band).astype(bf16)
        for j in range(4):
            parts[b][j, g, pl.ds(0, band)] = kept[j * band : (j + 1) * band]
        @pl.when(g > 0)
        def _():
            for copy in sending(g - 1):
                copy.wait_send()
        stage[pl.ds(4 * slot * band, 4 * band)] = part(4 * band, 4 * band).astype(bf16)
        for copy in sending(g):
            copy.start()
        @pl.when(g == 3)
        def _():
            for copy in sending(g):
                copy.wait_send()
    def give(b, g, slot, part):
        if linked:
            share_out(b, g, slot, part)
        else:
            put((gA, gB, gC)[b], g, slot, lambda c: part(c, 2 * band))

    def mlp_back(g, carry):
        for r in row_tiles(RT):
            rs = pl.ds(r, RT)
            gp = (mm(gout_low[rs], wc(g)) * slope[g, rs].astype(f32)).astype(bf16)
            slope[g, rs] = gp
            acc[rs] += mm(gp, wb(g), NT)
        bsum[1, g] = colsum(slope[g].astype(f32))
        give(2, g, 0, lambda c, n: mm(right_t[pl.ds(c, n)], hidden[g]))
        give(1, g, 1, lambda c, n: mm(left_t[pl.ds(c, n)], slope[g]))
        at(g, [[], [], [(mhop, 1, 0)], [(mhop, 1, 1)]])
        return carry
    for b in range(3):
        sent(b)
    lax.fori_loop(0, 4, mlp_back, 0)
    release()
    if not linked:
        off(gC, 3, 0).wait()
        off(gB, 3, 1).wait()

    sums = [jnp.zeros((1, D), f32) for _ in range(6)]
    for r in row_tiles(RL):
        rs = pl.ds(r, RL)
        n, inv = normal_of(middle[rs])
        gn = acc[rs]
        go = gout_low[rs].astype(f32)
        t = go + normal_back(gn, n, inv, vecs[3:4])
        middle[rs] = t
        gm_low[rs] = t.astype(bf16)
        sums[2] += colsum(t)
        sums[3] += colsum(gn * n)
        sums[4] += colsum(gn)
        sums[5] += colsum(go)
    merged = [(mhop, 1, 2), (acquire,), (merge, 2), (merge, 1), (mhop, 2, 0)]
    for act, *args in merged:
        act(*args)
    transpose(left_t, first_in)
    transpose(right_t, gm_low)
    acc[...] = jnp.zeros_like(acc)

    def backward(g, carry):
        ga = mm(gm_low[...], wa(g, 512, D)).astype(bf16)
        def tile(i):
            return qkv[g, :, 128 * i : 128 * i + 128]
        dq, dk, dv = [], [], []
        scale = invs[g].T
        for h in range(3):
            q, k, v = (tile(0), tile(1), tile(2)) if h < 2 else (tile(3), tile(4), tile(3))
            gt = ga[:, 128:256] if h < 2 else ga[:, 0:128]
            gt = (gt.astype(f32) * scale[:, h : h + 1]).astype(bf16)
            gmask = jnp.where(low if h == 0 else ~low, gt, 0)
            kt = k.T
            kt = kt[64:] if h == 1 else kt[:64]
            dqs, dks, dvs = [], 0.0, 0.0
            for r, n in QT:
                p = probs[g, h, :, pl.ds(r, n)]
                dp = mm(v, gmask[r : r + n], NT)
                pf = p.astype(f32)
                inner = jnp.sum(pf * dp, axis=0, keepdims=True)
                ds = (pf * (dp - inner * invs[g, h : h + 1, pl.ds(r, n)])).astype(bf16)
                dqs.append(mm(kt, ds))
                dks = dks + mm(ds, q[r : r + n])
                dvs = dvs + mm(p, gt[r : r + n])
            dq.append(jnp.concatenate(dqs, axis=1))
            dk.append(dks * 0.125)
            dv.append(dvs)
        dq01 = jnp.concatenate(dq[:2], axis=0).T * 0.125
        dq2 = jnp.concatenate([dq[2], jnp.zeros_like(dq[2])], axis=0).T * 0.125
        parts = [
            dq01,
            jnp.where(low, dk[0], dk[1]),
            jnp.where(low, dv[0], dv[1]),
            jnp.where(low, dq2, dv[2]),
            jnp.where(low, dk[2], 0.0),
        ]
        for i, part in enumerate(parts):
            part = part.astype(bf16)
            qkv[g, :, 128 * i : 128 * i + 128] = part
            bsum[0, g, :, 128 * i : 128 * i + 128] = colsum(part.astype(f32))
        qkv[g, :, 640:768] = jnp.zeros((LEN, 128), bf16)
        bsum[0, g, :, 640:768] = jnp.zeros((1, 128), f32)
        for r in row_tiles(RT):
            rs = pl.ds(r, RT)
            acc[rs] += mm(qkv[g, rs], wa(g), NT)
        at(g, BACK)
        return carry
    BACK = [
        [(third, 2), (mhop, 2, 1)],
        [(mhop, 2, 2), (third, 1)],
        [],
        [],
    ]
    lax.fori_loop(0, 4, backward, 0)

    for r in row_tiles(RL):
        rs = pl.ds(r, RL)
        n, inv = normal_of(x[rs].astype(f32))
        gn = acc[rs]
        first_in[rs] = (middle[rs] + normal_back(gn, n, inv, vecs[0:1])).astype(bf16)
        sums[0] += colsum(gn * n)
        sums[1] += colsum(gn)
    lines = sums + [bsum[i, j] for i in range(2) for j in range(4)] + [jnp.zeros((2, D), f32)]
    lines = jnp.concatenate(lines, axis=0).astype(bf16)
    fourth(2)
    if linked:
        for c in range(3):
            iopen(c)

    def attention_grads(g, carry):
        def part(c, n):
            first = mm(left_t[pl.ds(c, n)], qkv[g])
            second = mm(right_t[pl.ds(c, n)], att[g])
            return jnp.concatenate([first[:, :512], first[:, 512:] + second], axis=1)
        give(0, g, 0, part)
        at(g, [[], [], [(along, 2, 1)], []])
        return carry
    lax.fori_loop(0, 4, attention_grads, 0)
    if linked:
        vrow[0] = lines
        def vec_step(g, act):
            for j in range(4):
                act(twin_vec(g, j, vrow.at[0]))
        for g in range(4):
            vec_step(g, lambda copy: copy.start())
            for j in range(4):
                parts[0][j, g, pl.ds(band, 16)] = lines
        merge(0)
        fourth(1)
        ihop(1,0)
        third(0)
        ihop(1,1)
        along(1,1)
        ihop(1,2)
        along(2,2)
        ihop(2,0)
        fourth(0)
        along(0,1)
        ihop(2,1)
        along(1,2)
        along(0,2)
        ihop(2,2)
        last(2, acc, 2 * band + 16)
        last(1, acc, band + 16)
        last(0, acc, 0)
        done = pltpu.make_async_copy(acc.at[pl.ds(0, 3 * band + 16)], total_out, sems.at[1])
        done.start()
        for c in range(3):
            ihop(3, c)
        for g in range(4):
            vec_step(g, lambda copy: copy.wait_send())
        done.wait()
        for c in range(3):
            pieces[3 + c][2]()
        for b in range(3):
            closed(b)
    else:
        for i in range(8):
            vrow[i] = lines
        copies = [pltpu.make_async_copy(ig, ig_out, sems.at[1])]
        copies += [pltpu.make_async_copy(vrow, gA.at[g, :, pl.ds(band, 16)], sems.at[2 + g]) for g in range(4)]
        for copy in copies:
            copy.start()
        for copy in copies:
            copy.wait()
        off(gA, 3, 0).wait()
    for c in range(3):
        mhop(3, c)
    mclose()


def layer(linked, tokens, cotangent, counts, weights, cid=1):
    V, S = pltpu.VMEM, pltpu.SemaphoreType.DMA
    shape = jax.ShapeDtypeStruct
    hb, vm = pl.BlockSpec(memory_space=pl.ANY), pl.BlockSpec(memory_space=V)
    band, nb = BAND, 3
    rows_of = (band + 16, band, band)
    scratch = [V((4, 8, r, D), bf16) for r in rows_of]
    scratch += [V((LEN, D), bf16)] * 4 + [V((D, LEN), bf16)] * 2
    scratch += [V((4, LEN, D), bf16), V((4, 3, LEN, LEN), bf16), V((4, LEN, 256), bf16)]
    scratch += [V((LEN, D), f32)] * 2 + [V((8, LEN, D), bf16), V((8 * band, D) if linked else (2, 8, band, D), bf16)]
    scratch += [V((2, 4, 1, D), f32), V((1 if linked else 8, 16, D), bf16), V((16, D), f32)]
    scratch += [V((2, 4, 1, D), f32), V((LEN, D), bf16), V((4, 8, LEN), f32), S((12,))]
    outs = [shape((LEN, D), bf16)] * 2 + [shape((4, 8, r, D), bf16) for r in rows_of]
    if linked:
        outs = [shape((4, LEN, D), bf16)] * 2 + [shape((sum(rows_of), D), f32)]
        scratch += [V((16, 128), f32)]
        scratch += [S((nb,)), S((nb, 2, 4)), S((nb, 4))]
        scratch += [S((nb, 2, 4))] * 2 + [S((nb, 2))] * 2 + [S((nb, 4))] * 2
        scratch += [V((4, 4, r, D), bf16) for r in rows_of] + [V((4, 4, band, D), bf16)] * 2
        scratch += [pltpu.SemaphoreType.REGULAR] + [S((nb, 4, 4))] * 2 + [S((nb, 2))] * 4
        scratch += [S((nb, 4)), S((nb, 2, 4))] + [S((4, 4))] * 2
        scratch += [S((2, 4)), S((4,)), S((1,))] * 6
    params = dict(collective_id=cid, has_side_effects=True) if linked else {}
    return pl.pallas_call(
        functools.partial(layer_kernel, linked),
        out_shape=outs,
        in_specs=[hb, hb, pl.BlockSpec(memory_space=pltpu.SMEM)] + ([vm] * 6 if linked else [hb] * 3),
        out_specs=[hb] * len(outs),
        scratch_shapes=scratch,
        compiler_params=pltpu.CompilerParams(vmem_limit_bytes=63 * 1024 * 1024, **params),
        cost_estimate=pl.CostEstimate(
            flops=57_000_000_000, bytes_accessed=32_000_000, transcendentals=6_000_000
        ),
    )(tokens, cotangent, counts, *weights)


def step_kernel(total, low, first, *refs):
    ins, outs, full, same, (held, wide, passed, got, put) = refs[:18], refs[18:42], refs[42], refs[43], refs[44:]
    entry = pltpu.make_async_copy(first, passed, got.at[4])
    leave = pltpu.make_async_copy(passed, same, put.at[4])
    fetch = [pltpu.make_async_copy(low.at[s], held.at[s], got.at[s]) for s in range(4)]
    store = [pltpu.make_async_copy(wide.at[s], full.at[s], put.at[s]) for s in range(4)]
    for copy in fetch + [entry]:
        copy.start()
    for s in range(4):
        fetch[s].wait()
        for r in row_tiles(RL):
            wide[s, pl.ds(r, RL)] = held[s, pl.ds(r, RL)].astype(f32)
        store[s].start()
    entry.wait()
    leave.start()
    z, me = lax.axis_index("tensor"), lax.axis_index("dp")
    band, thin = ins[12].shape[1], ins[15].shape[1]
    vec = total[band : band + 16]
    high = vec.astype(bf16)
    rest = vec - high.astype(f32)
    mid = rest.astype(bf16)
    parts = jnp.concatenate([high, mid, (rest - mid.astype(f32)).astype(bf16)], axis=0)
    row = lax.broadcasted_iota(jnp.int32, (D, 256), 0)
    col = lax.broadcasted_iota(jnp.int32, (D, 256), 1)
    kind = lax.div(col - band, thin)
    place = me * thin + lax.rem(col - band, thin)
    head = jnp.where(place < 128, place, place + 256)
    late = jnp.where(place < 128, place + 256, place + 320)
    spot = jnp.where(kind == 0, head, jnp.where(kind == 1, late, (kind - 2) * (D // 4) + place))
    spot = jnp.where(col < band, me * band + col, spot)
    found = mm(parts, jnp.where(row == spot, 1.0, 0.0).astype(bf16))
    found = found[0:16] + found[16:32] + found[32:48]
    shared = found[:6, :band]
    at = lax.broadcasted_iota(jnp.int32, (16, 256), 0)
    lines = []
    for i in range(6):
        mine = jnp.where(at == z + (6 if i < 2 else 10), found, 0.0)
        mine = jnp.sum(mine, axis=0, keepdims=True)
        lines.append(mine[:, band + i * thin : band + (i + 1) * thin])
    split = jnp.concatenate(lines, axis=0)

    def apply(kind, where, gradient):
        rates, decays = kind_rates(), (MATRIX_DECAY,) * 4 + (0.0, 0.0)
        m, f, s = (ins[3 * kind + i][where] for i in range(3))
        results = adamw(m, f, s, gradient, rates[kind], decays[kind])
        for i in range(4):
            outs[4 * kind + i][where] = results[i]

    attn = total[:band]
    def pair(a, b):
        return jnp.concatenate([attn[:, a : a + 128], attn[:, b : b + 64]], axis=1)
    apply(0, (0,), pair(0, 384))
    apply(0, (1,), pair(128, 512))
    apply(0, (2,), pair(256, 448))
    apply(1, (slice(None),), pair(640, 576).T)
    up = total[band + 16 : 2 * band + 16]
    down = total[2 * band + 16 :]
    down = down.T
    width = D // 4
    for f in range(4):
        apply(2, (slice(None), f), up[:, f * width : (f + 1) * width])
        apply(3, (f,), down[f * width : (f + 1) * width])
    apply(4, (slice(None),), shared)
    apply(5, (slice(None),), split)
    for copy in store + [leave]:
        copy.wait()


def step(total, low, first, state):
    V, S = pltpu.VMEM, pltpu.SemaphoreType.DMA
    vm, hb = pl.BlockSpec(memory_space=V), pl.BlockSpec(memory_space=pl.ANY)
    shapes = []
    for kind in range(6):
        shape = state[3 * kind].shape
        shapes += [jax.ShapeDtypeStruct(shape, t) for t in (f32, bf16, f32, f32)]
    shapes += [jax.ShapeDtypeStruct(low.shape, t) for t in (f32, bf16)]
    return pl.pallas_call(
        step_kernel,
        out_shape=shapes,
        in_specs=[vm, hb, hb] + [vm] * 18,
        out_specs=[vm] * 24 + [hb] * 2,
        scratch_shapes=[V(low.shape, bf16), V(low.shape, f32), V(low.shape, bf16), S((5,)), S((5,))],
        compiler_params=pltpu.CompilerParams(vmem_limit_bytes=56 * 1024 * 1024),
    )(total, low, first, *state)


def pack_attention(qkv, out):
    q, k, v = qkv[:, 0], qkv[:, 1], qkv[:, 2]
    return jnp.concatenate(
        [
            q[:, :128], k[:, :128], v[:, :128],
            q[:, 128:], v[:, 128:], k[:, 128:], out[:, 128:], out[:, :128],
        ],
        axis=1,
    )


def unpack_attention(block):
    pair = [block[:, 128 * i : 128 * i + 128] for i in range(6)]
    q = jnp.concatenate([pair[0], pair[3][:, :64]], axis=1)
    k = jnp.concatenate([pair[1], pair[4][:, :64]], axis=1)
    v = jnp.concatenate([pair[2], pair[3][:, 64:]], axis=1)
    o = jnp.concatenate([pair[5], pair[4][:, 64:]], axis=1)
    return jnp.stack([q, k, v], axis=1), o


def gather_plain(masters):
    qkv, out, up, down, shared, split = (t.astype(bf16) for t in masters)
    band, thin, width = shared.shape[1], split.shape[1], down.shape[1] * lax.axis_size("tensor")
    groups = lax.axis_size("tensor")
    own = jnp.stack(
        [pack_attention(qkv, out.T), up.reshape(band, -1), down.reshape(-1, band).T]
    )
    mats = lax.all_gather(own, AXES, axis=1, tiled=True).reshape(3, groups, 8, BAND, width)
    shared = lax.all_gather(shared, "dp", axis=1, tiled=True)
    split = lax.all_gather(split, AXES, axis=1, tiled=True).reshape(-1, groups, width // groups)
    bq, bv = split[0], split[1]
    zero = jnp.zeros((groups, 128), bf16)
    attn_bias = [bq[:, :128], zero, bv[:, :128], bq[:, 128:], bv[:, 128:], zero, zero]
    lines = [
        jnp.broadcast_to(shared, (groups, 6, width)),
        jnp.concatenate(attn_bias, axis=1)[:, None],
        jnp.swapaxes(split[2:], 0, 1).reshape(groups, 1, width),
    ]
    lines = jnp.pad(jnp.concatenate(lines, axis=1)[:, None], ((0, 0), (0, 7), (0, 8), (0, 0)))
    return jnp.concatenate([mats[0], lines], axis=2), mats[1], mats[2]


def step_plain(grads, mixed, grad_inputs, state):
    masters, firsts, seconds = state[0::3], state[1::3], state[2::3]
    band, thin = masters[4].shape[1], masters[5].shape[1]
    groups, copies = lax.axis_size("tensor"), lax.axis_size("dp")
    z, at = lax.axis_index("tensor"), lax.axis_index("dp")
    width = grads[0].shape[-1]
    summed = [
        lax.psum_scatter(
            g[:, :, :BAND].reshape(groups * copies, band, width), AXES, scatter_dimension=0
        ).astype(f32)
        for g in grads
    ]
    vec = lax.psum(grads[0][0, 0, BAND:].astype(f32), AXES)
    shared = lax.dynamic_slice_in_dim(vec[:6], at * band, band, 1)
    cols = lax.dynamic_slice_in_dim(vec[6:10], z, 1, 0)[0]
    ups = lax.dynamic_slice_in_dim(vec[10:14], z, 1, 0).reshape(-1, width // groups)
    split = jnp.stack(
        [
            jnp.concatenate([cols[:128], cols[384:448]]),
            jnp.concatenate([cols[256:384], cols[448:512]]),
        ]
    )
    split = lax.dynamic_slice_in_dim(jnp.concatenate([split, ups]), at * thin, thin, 1)
    sum_qkv, sum_out = unpack_attention(summed[0])
    gradients = (
        sum_qkv,
        sum_out.T,
        summed[1].reshape(masters[2].shape),
        summed[2].T.reshape(masters[3].shape),
        shared,
        split,
    )
    decays = (MATRIX_DECAY, MATRIX_DECAY, MATRIX_DECAY, MATRIX_DECAY, 0.0, 0.0)
    rates = kind_rates()
    outputs = []
    for kind in range(6):
        outputs.extend(
            adamw(masters[kind], firsts[kind], seconds[kind], gradients[kind], rates[kind], decays[kind])
        )
    mixed, grad_inputs = (lax.all_gather(t, "tensor") for t in (mixed, grad_inputs))
    return mixed, grad_inputs, outputs


def local(tokens, cotangent, counts, *state):
    masters = state[0::3]
    if (lax.axis_size("tensor"), lax.axis_size("dp")) == (4, 8):
        turned = tuple(jnp.swapaxes(t, 0, 1) for t in state[:3])
        mixed, low, total = layer(True, tokens, cotangent, counts, turned[:1] + masters[1:])
        *outputs, grad_inputs, mixed = step(total, low, mixed, turned + state[3:])
        outputs[:4] = [jnp.swapaxes(t, 0, 1) for t in outputs[:4]]
    else:
        mats = gather_plain(masters)
        mixed, grad_inputs, *grads = layer(False, tokens, cotangent, counts, mats)
        mixed, grad_inputs, outputs = step_plain(grads, mixed, grad_inputs, state)
        grad_inputs = grad_inputs.astype(f32)
    return (mixed, grad_inputs, *outputs)


def solution(mesh):
    rows = P("dp", None, None)
    state = (
        P("dp", None, "tensor"),
        P("tensor", "dp"),
        P("dp", None, "tensor"),
        P(None, "tensor", "dp"),
        P(None, "dp"),
        P(None, ("tensor", "dp")),
    )
    in_specs = (rows, rows, P("dp")) + tuple(s for s in state for _ in range(3))
    out_specs = (rows, rows) + tuple(s for s in state for _ in range(4))
    return jax.shard_map(local, mesh=mesh, in_specs=in_specs, out_specs=out_specs, check_vma=False)
```
